32 devices in a mesh: groups: 2 (over y), tm: 4 (over z), space: 2 (over x), clip: 2 (over core).
Axes of the slice: x: 2, y: 2, z: 4, core: 2. Of those that a mesh axis runs over, the one named last changes fastest.
Arguments:
- latents: bfloat16 [4, 16, 8, 6144], P(('groups', 'clip'), 'tm', 'space'), parts along dimension 0, may hold values from -6 to 6
- frame_counts: int32 [4], P(('groups', 'clip')), parts along dimension 0, may hold values from 2 to 16, as said below
- gain_first: float32 [192], replicated, may hold values from 0.5 to 1.5
- bias_first: float32 [192], replicated, may hold values from -3 to 3
- weight_first: bfloat16 [3, 3, 3, 192, 192], replicated, may hold values from -0.078125 to 0.078125
- gain_second: float32 [192], replicated, may hold values from 0.5 to 1.5
- bias_second: float32 [192], replicated, may hold values from -3 to 3
- weight_second: bfloat16 [3, 3, 3, 192, 192], replicated, may hold values from -0.078125 to 0.078125
Outputs:
- encoded: bfloat16 [4, 16, 8, 6144], P(('groups', 'clip'), 'tm', 'space'), parts along dimension 0
The draws below stay inside these ranges and needn't reach their ends.
There are 2 independent parts, one for each index of `groups`. The reference program is written for one: setup_inputs(seed, part) draws one part's arguments, and reference() takes and returns one part's arrays. A program takes and returns all parts, laid end to end along the dimension named above; an argument that names none is the same for every part. Nothing has to cross between parts.
Inputs may be any that keep to these rules, and one draw needn't show every extreme that they name: `frame_counts`: in every part exactly one clip has all 16 frames valid; every other clip has fewer.
All inputs are finite; a program needn't handle non-finite values.
Results may differ from the reference program's by a relative error of at most 0.007.
Values may be sent and summed in bfloat16 or wider, within the bound.
No kernel may reach another device: no remote copies, remote signals or barrier semaphores. Data moves between devices by JAX's collectives and lax.ppermute only.
A program may use at most 64 MiB of HBM per device.

```python
import jax
import jax.numpy as jnp
from jax import lax

C = 192
COLS = 32
CLIPS = 2
FRAMES = 16
ROWS = 8


def draw_frame_counts(key, part):
    count_key = jax.random.fold_in(key, 11)
    pick_key = jax.random.fold_in(key, 23)
    drawn = jax.random.randint(count_key, (CLIPS,), 2, FRAMES)
    full_clip = jax.random.randint(pick_key, (), 0, CLIPS)
    return jnp.where(jnp.arange(CLIPS, dtype=jnp.int32) == full_clip, FRAMES, drawn).astype(jnp.int32)


def level_of(key, dims, shards, smallest, largest):
    level = 1.0
    for axis_at, blocks in shards:
        draws = jax.random.uniform(jax.random.fold_in(jax.random.fold_in(key, 6), axis_at), (blocks,), jnp.float32, smallest / len(shards), largest / len(shards))
        level = level * jnp.repeat(jnp.exp(draws), dims[axis_at] // blocks).reshape((-1,) + (1,) * (len(dims) - 1 - axis_at))
    return level


def noise(own_key, extent, deviation, most, pieces=(), kind=jnp.bfloat16):
    values = deviation * jax.random.normal(own_key, extent, jnp.float32)
    if pieces:
        values = values * level_of(own_key, extent, pieces, -0.22, 0.18)
    return jnp.clip(values, -most, most).astype(kind)


def setup_inputs(seed: int = 0, part: int = 0) -> dict:
    splits = jax.random.split(jax.random.key(seed), 9)
    part_splits = jax.random.split(jax.random.fold_in(splits[8], part), 9)
    latents = noise(part_splits[0], (CLIPS, FRAMES, ROWS, COLS * C), 1.0, 6.0, ((0, 2), (1, 4), (2, 2)))
    frame_counts = draw_frame_counts(jax.random.fold_in(jax.random.fold_in(splits[8], part), 71), part)
    gain_first = jnp.clip(jax.random.uniform(splits[2], (C,), jnp.float32, 0.5, 1.5), 0.5, 1.5)
    bias_first = noise(splits[3], (C,), 0.5, 3.0, (), jnp.float32)
    weight_first = noise(splits[4], (3, 3, 3, C, C), (27 * C) ** -0.5, 0.078125)
    gain_second = jnp.clip(jax.random.uniform(splits[5], (C,), jnp.float32, 0.5, 1.5), 0.5, 1.5)
    bias_second = noise(splits[6], (C,), 0.5, 3.0, (), jnp.float32)
    weight_second = noise(splits[7], (3, 3, 3, C, C), (27 * C) ** -0.5, 0.078125)
    return dict(latents=latents, frame_counts=frame_counts, gain_first=gain_first, bias_first=bias_first, weight_first=weight_first, gain_second=gain_second, bias_second=bias_second, weight_second=weight_second)


def norm_silu(values, gain):
    values = values.astype(jnp.float32)
    mean_square = lax.optimization_barrier(jnp.mean(values * values, axis=-1, keepdims=True))
    scaled = values * lax.rsqrt(mean_square + 1e-06) * gain
    return jax.nn.silu(scaled).astype(jnp.bfloat16)

def causal_conv(inputs, kernel):
    return lax.conv_general_dilated(inputs.astype(jnp.float32), kernel.astype(jnp.float32), (1, 1, 1), ((2, 0), (1, 1), (1, 1)), dimension_numbers=('NDHWC', 'DHWIO', 'NDHWC'), precision=lax.Precision.HIGHEST)

def reference(latents, frame_counts, gain_first, bias_first, weight_first, gain_second, bias_second, weight_second):
    channels = gain_first.shape[0]
    clips, frames, rows, flat_width = latents.shape
    shaped = latents.reshape(clips, frames, rows, flat_width // channels, channels)
    frame_index = jnp.arange(frames, dtype=jnp.int32)
    valid = frame_index[None, :] < frame_counts[:, None]
    frame_mask = valid[:, :, None, None, None]
    masked_input = jnp.where(frame_mask, shaped, jnp.zeros_like(shaped))
    normed_first = norm_silu(masked_input, gain_first)
    hidden_first = jnp.where(frame_mask, causal_conv(normed_first, weight_first) + bias_first, 0.0).astype(jnp.bfloat16)
    normed_second = norm_silu(hidden_first, gain_second)
    summed = masked_input.astype(jnp.float32) + causal_conv(normed_second, weight_second) + bias_second
    encoded = jnp.where(frame_mask, summed, 0.0).astype(jnp.bfloat16)
    return encoded.reshape(clips, frames, rows, flat_width)
```

```python
import functools

import jax
import jax.numpy as jnp
from jax import lax
from jax.experimental import pallas as pl
from jax.experimental.pallas import tpu as pltpu
from jax.sharding import PartitionSpec as P

F32 = jnp.float32
BF16 = jnp.bfloat16
LANES = 128
PAD = 8


def norm_silu_pair(t, gain, channels):
    square = t * t
    first = lax.broadcasted_iota(jnp.int32, t.shape, 1) < channels
    left = jnp.sum(jnp.where(first, square, 0.0), axis=1, keepdims=True)
    right = jnp.sum(jnp.where(first, 0.0, square), axis=1, keepdims=True)
    left = lax.rsqrt(left * (1.0 / channels) + 1e-06)
    right = lax.rsqrt(right * (1.0 / channels) + 1e-06)
    y = t * jnp.where(first, left, right) * gain
    return y * (0.5 + 0.5 * jnp.tanh(0.5 * y))


def clear_pads(stage, steps, pairs):
    stride = pairs + PAD
    zeros = jnp.zeros((PAD, LANES), F32)
    for f in range(stage.shape[0]):
        for k in range(3):
            for r in range(steps + 1):
                stage[f, k, pl.ds(r * stride, PAD), :] = zeros


def widen(dst, at, stage, f, r, pairs):
    base = r * (pairs + PAD) + PAD
    pieces = ((1, -1), (2, -1), (0, 0), (1, 0), (2, 0), (0, 1), (1, 1))
    for n, (k, shift) in enumerate(pieces):
        part = stage[f, k, pl.ds(base + shift, pairs), :]
        dst[at[0], at[1], :, n * LANES : (n + 1) * LANES] = part.astype(BF16)


def fill_window(window, stage, own, before, after, gain, keep_frame, keep_row, pairs, channels):
    frames, rows = own.shape[0], own.shape[1]
    halo = before.shape[1]
    tall = rows + 2 * halo
    wide = 2 * channels
    stride = pairs + PAD
    for f in range(frames):
        keep = keep_row & keep_frame(f)
        for p in range(pairs):
            lanes = pl.ds(p * wide, wide)
            t = jnp.concatenate(
                [ref[f, :, lanes].astype(F32) for ref in (before, own, after)], axis=0
            )
            y = norm_silu_pair(jnp.where(keep, t, 0.0), gain, channels)
            for k in range(3):
                stage[f, k, pl.ds(PAD + p, tall, stride=stride), :] = y[
                    :, k * LANES : (k + 1) * LANES
                ]
        for r in range(tall):
            widen(window, (f, r), stage, f, r, pairs)


def taps(window, weight, parity, source, frames, start, rows, a, channels):
    pairs = window.shape[2]
    low = 2 * LANES * parity
    span = 5 * LANES
    lead = span - 3 * channels
    zeros = jnp.zeros((lead, channels), BF16)
    left, right = [], []
    for b in range(3):
        part = window[source : source + frames, pl.ds(start + b, rows), :, low : low + span]
        left.append(part.reshape(frames * rows * pairs, span))
        right += [zeros, weight[a, b]] if parity == 0 else [weight[a, b], zeros]
    return jnp.dot(
        jnp.concatenate(left, axis=1), jnp.concatenate(right, axis=0), preferred_element_type=F32
    )


def place():
    return lax.axis_index("tm"), lax.axis_index("space")


def twice(ref):
    return jnp.concatenate([ref[...], ref[...]], axis=1)


def row_mask(halo, rows, total_rows):
    row = lax.axis_index("space") * rows - halo
    row = row + lax.broadcasted_iota(jnp.int32, (rows + 2 * halo, 1), 0)
    return (row >= 0) & (row < total_rows)


def first_kernel(dims, count, own, before, after, gain, weight, partial, window, stage):
    frames, rows, pairs, channels, total_rows, deep = dims
    tm, space = place()
    start = (1 - space) if deep == rows + 1 else 0
    clear_pads(stage, rows + 4, pairs)
    fill_window(
        window, stage, own, before, after, twice(gain),
        lambda f: tm * frames + f < count[0], row_mask(2, rows, total_rows), pairs, channels,
    )
    for parity in range(2):
        for a in (2, 1, 0):
            skip = 2 - a
            part = taps(window, weight, parity, 0, frames - skip, start, deep, a, channels)
            if skip == 0:
                partial[parity] = part
            else:
                at = pl.ds(skip * deep * pairs, (frames - skip) * deep * pairs)
                partial[parity, at, :] += part


def second_kernel(
    dims, count, own, earlier, before, after, partial, gain, bias, weight, gain_two, bias_two,
    weight_two, out, window, stage, total, hidden, hidden_stage, final,
):
    frames, rows, pairs, channels, total_rows, deep = dims
    tm, space = place()
    first_frame = tm * frames
    start = (1 - space) if deep == rows + 1 else 0
    fill = deep * pairs
    clear_pads(stage, rows + 4, pairs)
    clear_pads(hidden_stage, deep, pairs)
    fill_window(
        window, stage, earlier, before, after, twice(gain),
        lambda f: (tm > 0) & (first_frame - frames + f < count[0]),
        row_mask(2, rows, total_rows), pairs, channels,
    )
    late = (frames - 2) * fill
    for parity in range(2):
        total[parity, 0 : 2 * fill] = jnp.zeros((2 * fill, channels), F32)
        total[parity, 2 * fill :] = partial[parity]
        for a in (0, 1, 2):
            part = taps(window, weight, parity, a, frames - a, start, deep, a, channels)
            total[parity, 0 : (frames - a) * fill] += part

    bias_wide, gain_wide = twice(bias), twice(gain_two)
    row = lax.broadcasted_iota(jnp.int32, (fill, 1), 0) // pairs + (space * rows - 1 + start)
    row_ok = (row >= 0) & (row < total_rows)
    for h in range(frames + 2):
        at = first_frame + h - 2
        keep = row_ok & (at >= 0) & (at < count[0])
        t = jnp.concatenate([total[q, h * fill : (h + 1) * fill, :] for q in range(2)], axis=1)
        t = jnp.where(keep, t + bias_wide, 0.0).astype(BF16).astype(F32)
        y = norm_silu_pair(t, gain_wide, channels)
        hidden[h, 0] = jnp.zeros(hidden.shape[2:], BF16)
        hidden[h, rows + 1] = jnp.zeros(hidden.shape[2:], BF16)
        for r in range(deep):
            for k in range(3):
                hidden_stage[h, k, pl.ds(r * (pairs + PAD) + PAD, pairs), :] = y[
                    r * pairs : (r + 1) * pairs, k * LANES : (k + 1) * LANES
                ]
            widen(hidden, (h, start + r), hidden_stage, h, r, pairs)

    sums = []
    for parity in range(2):
        acc = taps(hidden, weight_two, parity, 0, frames, 0, rows, 0, channels)
        acc = acc + taps(hidden, weight_two, parity, 1, frames, 0, rows, 1, channels)
        sums.append(acc + taps(hidden, weight_two, parity, 2, frames, 0, rows, 2, channels))
    both = jnp.concatenate(sums, axis=1) + twice(bias_two)
    for k in range(3):
        final[k] = both[:, k * LANES : (k + 1) * LANES]
    for f in range(0, frames, 2):
        for p in range(pairs):
            for k in range(3):
                block = final[k, pl.ds(f * rows * pairs + p, 2 * rows, stride=pairs), :]
                lanes = pl.ds(p * 2 * channels + k * LANES, LANES)
                for n in range(2):
                    value = own[f + n, :, lanes].astype(F32) + block[n * rows : (n + 1) * rows]
                    keep = first_frame + f + n < count[0]
                    out[f + n, :, lanes] = jnp.where(keep, value, 0.0).astype(BF16)


def shards(latents, counts, gain_first, bias_first, weight_first, gain_second, bias_second, weight_second):
    channels = gain_first.shape[0]
    frames, rows, flat = latents.shape[1:]
    pairs = flat // (2 * channels)
    blocks, bands = lax.axis_size("tm"), lax.axis_size("space")
    total_rows = bands * rows
    own = latents.reshape(frames, rows, flat)
    space = lax.axis_index("space")
    axes = ("tm", "space")

    def halo(sent, step, along):
        pairs_of = [
            (t * bands + s, (t + along) * bands + s + step)
            for t in range(blocks - along)
            for s in range(bands)
            if 0 <= s + step < bands
        ]
        return lax.ppermute(sent, axes, pairs_of)

    earlier = halo(own, 0, 1)
    if bands == 2:
        sent = lax.dynamic_slice_in_dim(own, (rows - 2) * (1 - space), 2, axis=1)
        swaps = [(t * 2 + s, t * 2 + 1 - s) for t in range(blocks) for s in range(2)]
        near = (lax.ppermute(sent, axes, swaps),) * 2
        swaps = [(t * 2 + s, t * 2 + 3 - s) for t in range(blocks - 1) for s in range(2)]
        far = (lax.ppermute(sent, axes, swaps),) * 2
        deep = rows + 1
    else:
        low, high = own[:, rows - 2 :], own[:, :2]
        near = (halo(low, 1, 0), halo(high, -1, 0))
        far = (halo(low, 1, 1), halo(high, -1, 1))
        deep = rows + 2

    dims = (frames, rows, pairs, channels, total_rows, deep)
    fill = deep * pairs
    tall = rows + 4
    stride = pairs + PAD
    vmem = pl.BlockSpec(memory_space=pltpu.VMEM)
    smem = pl.BlockSpec(memory_space=pltpu.SMEM)
    window = pltpu.VMEM((frames, tall, pairs, 7 * LANES), BF16)
    stage = pltpu.VMEM((frames, 3, (tall + 1) * stride, LANES), F32)
    first_weight = weight_first.reshape(3, 3, 3 * channels, channels)
    second_weight = weight_second.reshape(3, 3, 3 * channels, channels)
    flops = 2 * 9 * fill * 9 * channels * channels * 3
    params = pltpu.CompilerParams(vmem_limit_bytes=24 << 20)
    partial = pl.pallas_call(
        functools.partial(first_kernel, dims),
        out_shape=jax.ShapeDtypeStruct((2, frames * fill, channels), F32),
        in_specs=[smem] + [vmem] * 5,
        out_specs=vmem,
        scratch_shapes=[window, stage],
        compiler_params=params,
        cost_estimate=pl.CostEstimate(flops=flops, bytes_accessed=4 << 20, transcendentals=0),
        name="first_half",
    )(counts, own, *near, gain_first.reshape(1, channels), first_weight)
    out = pl.pallas_call(
        functools.partial(second_kernel, dims),
        out_shape=jax.ShapeDtypeStruct((frames, rows, flat), BF16),
        in_specs=[smem] + [vmem] * 11,
        out_specs=vmem,
        scratch_shapes=[
            window,
            stage,
            pltpu.VMEM((2, (frames + 2) * fill, channels), F32),
            pltpu.VMEM((frames + 2, rows + 2, pairs, 7 * LANES), BF16),
            pltpu.VMEM((frames + 2, 3, (deep + 1) * stride, LANES), F32),
            pltpu.VMEM((3, frames * rows * pairs, LANES), F32),
        ],
        compiler_params=params,
        cost_estimate=pl.CostEstimate(flops=2 * flops, bytes_accessed=6 << 20, transcendentals=0),
        name="second_half",
    )(
        counts, own, earlier, *far, partial,
        gain_first.reshape(1, channels), bias_first.reshape(1, channels), first_weight,
        gain_second.reshape(1, channels), bias_second.reshape(1, channels), second_weight,
    )
    return out.reshape(1, frames, rows, flat)


def solution(mesh):
    spread = P(("groups", "clip"), "tm", "space", None)
    return jax.shard_map(
        shards,
        mesh=mesh,
        in_specs=(spread, P(("groups", "clip")), P(), P(), P(), P(), P(), P()),
        out_specs=spread,
        check_vma=False,
    )
```

```python
import functools

import jax
import jax.numpy as jnp
from jax import lax
from jax.experimental import pallas as pl
from jax.experimental.pallas import tpu as pltpu
from jax.sharding import PartitionSpec as P

F32 = jnp.float32
BF16 = jnp.bfloat16
LANES = 128
PAD = 8


def norm_silu_pair(t, gain, channels):
    square = t * t
    first = lax.broadcasted_iota(jnp.int32, t.shape, 1) < channels
    left = jnp.sum(jnp.where(first, square, 0.0), axis=1, keepdims=True)
    right = jnp.sum(jnp.where(first, 0.0, square), axis=1, keepdims=True)
    left = lax.rsqrt(left * (1.0 / channels) + 1e-06)
    right = lax.rsqrt(right * (1.0 / channels) + 1e-06)
    y = t * jnp.where(first, left, right) * gain
    return y * (0.5 + 0.5 * jnp.tanh(0.5 * y))


def clear_pads(stage, steps, pairs):
    stride = pairs + PAD
    zeros = jnp.zeros((PAD, LANES), F32)
    for f in range(stage.shape[0]):
        for k in range(3):
            for r in range(steps + 1):
                stage[f, k, pl.ds(r * stride, PAD), :] = zeros


def widen(dst, at, stage, f, r, pairs):
    base = r * (pairs + PAD) + PAD
    pieces = ((1, -1), (2, -1), (0, 0), (1, 0), (2, 0), (0, 1), (1, 1))
    for n, (k, shift) in enumerate(pieces):
        part = stage[f, k, pl.ds(base + shift, pairs), :]
        dst[at[0], at[1], :, n * LANES : (n + 1) * LANES] = part.astype(BF16)


def fill_window(window, stage, own, before, after, gain, keep_frame, keep_row, pairs, channels):
    frames, rows = own.shape[0], own.shape[1]
    halo = before.shape[1]
    tall = rows + 2 * halo
    wide = 2 * channels
    stride = pairs + PAD
    for f in range(frames):
        keep = keep_row & keep_frame(f)
        for p in range(pairs):
            lanes = pl.ds(p * wide, wide)
            t = jnp.concatenate(
                [ref[f, :, lanes].astype(F32) for ref in (before, own, after)], axis=0
            )
            y = norm_silu_pair(jnp.where(keep, t, 0.0), gain, channels)
            for k in range(3):
                stage[f, k, pl.ds(PAD + p, tall, stride=stride), :] = y[
                    :, k * LANES : (k + 1) * LANES
                ]
        for r in range(tall):
            widen(window, (f, r), stage, f, r, pairs)


def taps(window, weight, parity, source, frames, start, rows, a, channels):
    pairs = window.shape[2]
    low = 2 * LANES * parity
    span = 5 * LANES
    lead = span - 3 * channels
    zeros = jnp.zeros((lead, channels), BF16)
    left, right = [], []
    for b in range(3):
        part = window[source : source + frames, pl.ds(start + b, rows), :, low : low + span]
        left.append(part.reshape(frames * rows * pairs, span))
        right += [zeros, weight[a, b]] if parity == 0 else [weight[a, b], zeros]
    return jnp.dot(
        jnp.concatenate(left, axis=1), jnp.concatenate(right, axis=0), preferred_element_type=F32
    )


def place():
    return lax.axis_index("tm"), lax.axis_index("space")


def twice(ref):
    return jnp.concatenate([ref[...], ref[...]], axis=1)


def row_mask(halo, rows, total_rows):
    row = lax.axis_index("space") * rows - halo
    row = row + lax.broadcasted_iota(jnp.int32, (rows + 2 * halo, 1), 0)
    return (row >= 0) & (row < total_rows)


def cut_kernel(swap, own, *sent):
    frames, rows = own.shape[0], own.shape[1]
    for f in range(frames):
        if swap:
            below = lax.axis_index("space") == 0
            sent[0][f] = jnp.where(below, own[f, rows - 2 :, :], own[f, :2, :])
        else:
            sent[0][f] = own[f, rows - 2 :, :]
            sent[1][f] = own[f, :2, :]


def first_kernel(dims, count, own, before, after, gain, weight, partial, window, stage):
    frames, rows, pairs, channels, total_rows, deep = dims
    tm, space = place()
    start = (1 - space) if deep == rows + 1 else 0
    clear_pads(stage, rows + 4, pairs)
    fill_window(
        window, stage, own, before, after, twice(gain), lambda f: tm * frames + f < count[...],
        row_mask(2, rows, total_rows), pairs, channels,
    )
    for parity in range(2):
        for a in (2, 1, 0):
            skip = 2 - a
            part = taps(window, weight, parity, 0, frames - skip, start, deep, a, channels)
            if skip == 0:
                partial[parity] = part
            else:
                at = pl.ds(skip * deep * pairs, (frames - skip) * deep * pairs)
                partial[parity, at, :] += part


def second_kernel(
    dims, count, own, earlier, before, after, partial, gain, bias, weight, gain_two, bias_two,
    weight_two, out, window, stage, total, hidden, hidden_stage, final,
):
    frames, rows, pairs, channels, total_rows, deep = dims
    tm, space = place()
    start = (1 - space) if deep == rows + 1 else 0
    fill = deep * pairs

    def valid(f):
        at = (tm - 1) * frames + f
        return (at >= 0) & (at < count[...])

    clear_pads(stage, rows + 4, pairs)
    clear_pads(hidden_stage, deep, pairs)
    fill_window(
        window, stage, earlier, before, after, twice(gain), valid,
        row_mask(2, rows, total_rows), pairs, channels,
    )
    for parity in range(2):
        total[parity, 0 : 2 * fill] = jnp.zeros((2 * fill, channels), F32)
        total[parity, 2 * fill :] = partial[parity]
        for a in (0, 1, 2):
            part = taps(window, weight, parity, a, frames - a, start, deep, a, channels)
            total[parity, 0 : (frames - a) * fill] += part

    row = lax.broadcasted_iota(jnp.int32, (fill, 1), 0) // pairs + (space * rows - 1 + start)
    row_ok = (row >= 0) & (row < total_rows)
    bias_wide, gain_wide = twice(bias), twice(gain_two)
    for h in range(frames + 2):
        good = row_ok & valid(frames + h - 2)
        t = jnp.concatenate([total[q, h * fill : (h + 1) * fill, :] for q in range(2)], axis=1)
        t = jnp.where(good, t + bias_wide, 0.0).astype(BF16).astype(F32)
        y = norm_silu_pair(t, gain_wide, channels)
        hidden[h, 0] = jnp.zeros(hidden.shape[2:], BF16)
        hidden[h, rows + 1] = jnp.zeros(hidden.shape[2:], BF16)
        for r in range(deep):
            for k in range(3):
                hidden_stage[h, k, pl.ds(r * (pairs + PAD) + PAD, pairs), :] = y[
                    r * pairs : (r + 1) * pairs, k * LANES : (k + 1) * LANES
                ]
            widen(hidden, (h, start + r), hidden_stage, h, r, pairs)

    sums = []
    for parity in range(2):
        acc = taps(hidden, weight_two, parity, 0, frames, 0, rows, 0, channels)
        acc = acc + taps(hidden, weight_two, parity, 1, frames, 0, rows, 1, channels)
        sums.append(acc + taps(hidden, weight_two, parity, 2, frames, 0, rows, 2, channels))
    both = jnp.concatenate(sums, axis=1) + twice(bias_two)
    for k in range(3):
        final[k] = both[:, k * LANES : (k + 1) * LANES]
    for f in range(0, frames, 2):
        good = [valid(frames + f + n) for n in range(2)]
        for p in range(pairs):
            for k in range(3):
                block = final[k, pl.ds(f * rows * pairs + p, 2 * rows, stride=pairs), :]
                lanes = pl.ds(p * 2 * channels + k * LANES, LANES)
                for n in range(2):
                    value = own[f + n, :, lanes].astype(F32) + block[n * rows : (n + 1) * rows]
                    out[f + n, :, lanes] = jnp.where(good[n], value, 0.0).astype(BF16)


def shards(latents, counts, gain_first, bias_first, weight_first, gain_second, bias_second, weight_second):
    channels = gain_first.shape[0]
    frames, rows, flat = latents.shape[1:]
    pairs = flat // (2 * channels)
    blocks, bands = lax.axis_size("tm"), lax.axis_size("space")
    total_rows = bands * rows
    block = latents.reshape(frames, rows, flat)
    count = counts.reshape(1, 1)

    def shift(sent, step, along):
        pairs_of = [
            (t * bands + s, (t + along) % blocks * bands + (s + step) % bands)
            for t in range(blocks)
            for s in range(bands)
        ]
        return lax.ppermute(sent, ("tm", "space"), pairs_of)

    earlier = shift(block, 0, 1)
    vmem = pl.BlockSpec(memory_space=pltpu.VMEM)
    swap = bands == 2
    rim = jax.ShapeDtypeStruct((frames, 2, flat), BF16)
    sent = pl.pallas_call(
        functools.partial(cut_kernel, swap),
        out_shape=[rim] * (1 if swap else 2),
        in_specs=[vmem],
        out_specs=[vmem] * (1 if swap else 2),
        cost_estimate=pl.CostEstimate(flops=4 << 30, bytes_accessed=1 << 20, transcendentals=0),
        name="cut_rows",
    )(block)
    if swap:
        near = (shift(sent[0], 1, 0),) * 2
        far = (shift(sent[0], 1, 1),) * 2
        deep = rows + 1
    else:
        near = (shift(sent[0], 1, 0), shift(sent[1], -1, 0))
        far = (shift(sent[0], 1, 1), shift(sent[1], -1, 1))
        deep = rows + 2

    dims = (frames, rows, pairs, channels, total_rows, deep)
    fill = deep * pairs
    tall = rows + 4
    stride = pairs + PAD
    window = pltpu.VMEM((frames, tall, pairs, 7 * LANES), BF16)
    stage = pltpu.VMEM((frames, 3, (tall + 1) * stride, LANES), F32)
    first_weight = weight_first.reshape(3, 3, 3 * channels, channels)
    second_weight = weight_second.reshape(3, 3, 3 * channels, channels)
    flops = 2 * 9 * fill * 9 * channels * channels * 3
    params = pltpu.CompilerParams(vmem_limit_bytes=24 << 20)
    partial = pl.pallas_call(
        functools.partial(first_kernel, dims),
        out_shape=jax.ShapeDtypeStruct((2, frames * fill, channels), F32),
        in_specs=[vmem] * 6,
        out_specs=vmem,
        scratch_shapes=[window, stage],
        compiler_params=params,
        cost_estimate=pl.CostEstimate(flops=flops, bytes_accessed=4 << 20, transcendentals=0),
        name="first_half",
    )(count, block, *near, gain_first.reshape(1, channels), first_weight)
    out = pl.pallas_call(
        functools.partial(second_kernel, dims),
        out_shape=jax.ShapeDtypeStruct((frames, rows, flat), BF16),
        in_specs=[vmem] * 12,
        out_specs=vmem,
        scratch_shapes=[
            window,
            stage,
            pltpu.VMEM((2, (frames + 2) * fill, channels), F32),
            pltpu.VMEM((frames + 2, rows + 2, pairs, 7 * LANES), BF16),
            pltpu.VMEM((frames + 2, 3, (deep + 1) * stride, LANES), F32),
            pltpu.VMEM((3, frames * rows * pairs, LANES), F32),
        ],
        compiler_params=params,
        cost_estimate=pl.CostEstimate(flops=2 * flops, bytes_accessed=6 << 20, transcendentals=0),
        name="second_half",
    )(
        count, block, earlier, *far, partial,
        gain_first.reshape(1, channels), bias_first.reshape(1, channels), first_weight,
        gain_second.reshape(1, channels), bias_second.reshape(1, channels), second_weight,
    )
    return out.reshape(1, frames, rows, flat)


def solution(mesh):
    spread = P(("groups", "clip"), "tm", "space", None)
    return jax.shard_map(
        shards,
        mesh=mesh,
        in_specs=(spread, P(("groups", "clip")), P(), P(), P(), P(), P(), P()),
        out_specs=spread,
        check_vma=False,
    )
```

```python
import functools

import jax
import jax.numpy as jnp
from jax import lax
from jax.experimental import pallas as pl
from jax.experimental.pallas import tpu as pltpu
from jax.sharding import PartitionSpec as P

F32 = jnp.float32
BF16 = jnp.bfloat16
LANES = 128
PAD = 8


def norm_silu_pair(t, gain, channels):
    square = t * t
    first = lax.broadcasted_iota(jnp.int32, t.shape, 1) < channels
    left = jnp.sum(jnp.where(first, square, 0.0), axis=1, keepdims=True)
    right = jnp.sum(jnp.where(first, 0.0, square), axis=1, keepdims=True)
    left = lax.rsqrt(left * (1.0 / channels) + 1e-06)
    right = lax.rsqrt(right * (1.0 / channels) + 1e-06)
    y = t * jnp.where(first, left, right) * gain
    return y * (0.5 + 0.5 * jnp.tanh(0.5 * y))


def clear_pads(stage, steps, pairs):
    stride = pairs + PAD
    zeros = jnp.zeros((PAD, LANES), F32)
    for f in range(stage.shape[0]):
        for k in range(3):
            for r in range(steps + 1):
                stage[f, k, pl.ds(r * stride, PAD), :] = zeros


def widen(dst, at, stage, f, r, pairs):
    base = r * (pairs + PAD) + PAD
    pieces = ((1, -1), (2, -1), (0, 0), (1, 0), (2, 0), (0, 1), (1, 1))
    for n, (k, shift) in enumerate(pieces):
        part = stage[f, k, pl.ds(base + shift, pairs), :]
        dst[at[0], at[1], :, n * LANES : (n + 1) * LANES] = part.astype(BF16)


def fill_window(window, stage, own, before, after, gain, keep_frame, keep_row, pairs, channels):
    frames, rows = own.shape[0], own.shape[1]
    halo = before.shape[1]
    tall = rows + 2 * halo
    wide = 2 * channels
    stride = pairs + PAD
    for f in range(frames):
        keep = keep_row & keep_frame(f)
        for p in range(pairs):
            lanes = pl.ds(p * wide, wide)
            t = jnp.concatenate(
                [ref[f, :, lanes].astype(F32) for ref in (before, own, after)], axis=0
            )
            y = norm_silu_pair(jnp.where(keep, t, 0.0), gain, channels)
            for k in range(3):
                stage[f, k, pl.ds(PAD + p, tall, stride=stride), :] = y[
                    :, k * LANES : (k + 1) * LANES
                ]
        for r in range(tall):
            widen(window, (f, r), stage, f, r, pairs)


def taps(window, weight, parity, source, frames, start, rows, a, channels):
    pairs = window.shape[2]
    low = 2 * LANES * parity
    span = 5 * LANES
    lead = span - 3 * channels
    zeros = jnp.zeros((lead, channels), BF16)
    left, right = [], []
    for b in range(3):
        part = window[source : source + frames, pl.ds(start + b, rows), :, low : low + span]
        left.append(part.reshape(frames * rows * pairs, span))
        right += [zeros, weight[a, b]] if parity == 0 else [weight[a, b], zeros]
    return jnp.dot(
        jnp.concatenate(left, axis=1), jnp.concatenate(right, axis=0), preferred_element_type=F32
    )


def place():
    return lax.axis_index("tm"), lax.axis_index("space")


def twice(ref):
    return jnp.concatenate([ref[...], ref[...]], axis=1)


def row_mask(halo, rows, total_rows):
    row = lax.axis_index("space") * rows - halo
    row = row + lax.broadcasted_iota(jnp.int32, (rows + 2 * halo, 1), 0)
    return (row >= 0) & (row < total_rows)


def cut_kernel(swap, own, *sent):
    frames, rows = own.shape[0], own.shape[1]
    for f in range(frames):
        if swap:
            below = lax.axis_index("space") == 0
            sent[0][f] = jnp.where(below, own[f, rows - 2 :, :], own[f, :2, :])
        else:
            sent[0][f] = own[f, rows - 2 :, :]
            sent[1][f] = own[f, :2, :]


def first_kernel(dims, count, own, before, after, gain, weight, partial, window, stage):
    frames, rows, pairs, channels, total_rows, deep = dims
    tm, space = place()
    start = (1 - space) if deep == rows + 1 else 0
    clear_pads(stage, rows + 4, pairs)
    fill_window(
        window, stage, own, before, after, twice(gain), lambda f: tm * frames + f < count[0],
        row_mask(2, rows, total_rows), pairs, channels,
    )
    for parity in range(2):
        for a in (2, 1, 0):
            skip = 2 - a
            part = taps(window, weight, parity, 0, frames - skip, start, deep, a, channels)
            if skip == 0:
                partial[parity] = part
            else:
                at = pl.ds(skip * deep * pairs, (frames - skip) * deep * pairs)
                partial[parity, at, :] += part


def second_kernel(
    dims, count, own, earlier, before, after, partial, gain, bias, weight, gain_two, bias_two,
    weight_two, out, window, stage, total, hidden, hidden_stage, final,
):
    frames, rows, pairs, channels, total_rows, deep = dims
    tm, space = place()
    start = (1 - space) if deep == rows + 1 else 0
    fill = deep * pairs

    def valid(f):
        at = (tm - 1) * frames + f
        return (at >= 0) & (at < count[0])

    clear_pads(stage, rows + 4, pairs)
    clear_pads(hidden_stage, deep, pairs)
    fill_window(
        window, stage, earlier, before, after, twice(gain), valid,
        row_mask(2, rows, total_rows), pairs, channels,
    )
    for parity in range(2):
        total[parity, 0 : 2 * fill] = jnp.zeros((2 * fill, channels), F32)
        total[parity, 2 * fill :] = partial[parity]
        for a in (0, 1, 2):
            part = taps(window, weight, parity, a, frames - a, start, deep, a, channels)
            total[parity, 0 : (frames - a) * fill] += part

    row = lax.broadcasted_iota(jnp.int32, (fill, 1), 0) // pairs + (space * rows - 1 + start)
    row_ok = (row >= 0) & (row < total_rows)
    bias_wide, gain_wide = twice(bias), twice(gain_two)
    for h in range(frames + 2):
        good = row_ok & valid(frames + h - 2)
        t = jnp.concatenate([total[q, h * fill : (h + 1) * fill, :] for q in range(2)], axis=1)
        t = jnp.where(good, t + bias_wide, 0.0).astype(BF16).astype(F32)
        y = norm_silu_pair(t, gain_wide, channels)
        hidden[h, 0] = jnp.zeros(hidden.shape[2:], BF16)
        hidden[h, rows + 1] = jnp.zeros(hidden.shape[2:], BF16)
        for r in range(deep):
            for k in range(3):
                hidden_stage[h, k, pl.ds(r * (pairs + PAD) + PAD, pairs), :] = y[
                    r * pairs : (r + 1) * pairs, k * LANES : (k + 1) * LANES
                ]
            widen(hidden, (h, start + r), hidden_stage, h, r, pairs)

    sums = []
    for parity in range(2):
        acc = taps(hidden, weight_two, parity, 0, frames, 0, rows, 0, channels)
        acc = acc + taps(hidden, weight_two, parity, 1, frames, 0, rows, 1, channels)
        sums.append(acc + taps(hidden, weight_two, parity, 2, frames, 0, rows, 2, channels))
    both = jnp.concatenate(sums, axis=1) + twice(bias_two)
    for k in range(3):
        final[k] = both[:, k * LANES : (k + 1) * LANES]
    for f in range(0, frames, 2):
        good = [valid(frames + f + n) for n in range(2)]
        for p in range(pairs):
            for k in range(3):
                block = final[k, pl.ds(f * rows * pairs + p, 2 * rows, stride=pairs), :]
                lanes = pl.ds(p * 2 * channels + k * LANES, LANES)
                for n in range(2):
                    value = own[f + n, :, lanes].astype(F32) + block[n * rows : (n + 1) * rows]
                    out[f + n, :, lanes] = jnp.where(good[n], value, 0.0).astype(BF16)


def shards(latents, counts, gain_first, bias_first, weight_first, gain_second, bias_second, weight_second):
    channels = gain_first.shape[0]
    frames, rows, flat = latents.shape[1:]
    pairs = flat // (2 * channels)
    blocks, bands = lax.axis_size("tm"), lax.axis_size("space")
    total_rows = bands * rows
    block = latents.reshape(frames, rows, flat)

    def shift(sent, step, along):
        pairs_of = [
            (t * bands + s, (t + along) % blocks * bands + (s + step) % bands)
            for t in range(blocks)
            for s in range(bands)
        ]
        return lax.ppermute(sent, ("tm", "space"), pairs_of)

    earlier = shift(block, 0, 1)
    vmem = pl.BlockSpec(memory_space=pltpu.VMEM)
    smem = pl.BlockSpec(memory_space=pltpu.SMEM)
    swap = bands == 2
    rim = jax.ShapeDtypeStruct((frames, 2, flat), BF16)
    sent = pl.pallas_call(
        functools.partial(cut_kernel, swap),
        out_shape=[rim] * (1 if swap else 2),
        in_specs=[vmem],
        out_specs=[vmem] * (1 if swap else 2),
        cost_estimate=pl.CostEstimate(flops=4 << 30, bytes_accessed=1 << 20, transcendentals=0),
        name="cut_rows",
    )(block)
    if swap:
        near = (shift(sent[0], 1, 0),) * 2
        far = (shift(sent[0], 1, 1),) * 2
        deep = rows + 1
    else:
        near = (shift(sent[0], 1, 0), shift(sent[1], -1, 0))
        far = (shift(sent[0], 1, 1), shift(sent[1], -1, 1))
        deep = rows + 2

    dims = (frames, rows, pairs, channels, total_rows, deep)
    fill = deep * pairs
    tall = rows + 4
    stride = pairs + PAD
    window = pltpu.VMEM((frames, tall, pairs, 7 * LANES), BF16)
    stage = pltpu.VMEM((frames, 3, (tall + 1) * stride, LANES), F32)
    first_weight = weight_first.reshape(3, 3, 3 * channels, channels)
    second_weight = weight_second.reshape(3, 3, 3 * channels, channels)
    flops = 2 * 9 * fill * 9 * channels * channels * 3
    params = pltpu.CompilerParams(vmem_limit_bytes=24 << 20)
    partial = pl.pallas_call(
        functools.partial(first_kernel, dims),
        out_shape=jax.ShapeDtypeStruct((2, frames * fill, channels), F32),
        in_specs=[smem] + [vmem] * 5,
        out_specs=vmem,
        scratch_shapes=[window, stage],
        compiler_params=params,
        cost_estimate=pl.CostEstimate(flops=1 << 20, bytes_accessed=1 << 16, transcendentals=0),
        name="first_half",
    )(counts, block, *near, gain_first.reshape(1, channels), first_weight)
    out = pl.pallas_call(
        functools.partial(second_kernel, dims),
        out_shape=jax.ShapeDtypeStruct((frames, rows, flat), BF16),
        in_specs=[smem] + [vmem] * 11,
        out_specs=vmem,
        scratch_shapes=[
            window,
            stage,
            pltpu.VMEM((2, (frames + 2) * fill, channels), F32),
            pltpu.VMEM((frames + 2, rows + 2, pairs, 7 * LANES), BF16),
            pltpu.VMEM((frames + 2, 3, (deep + 1) * stride, LANES), F32),
            pltpu.VMEM((3, frames * rows * pairs, LANES), F32),
        ],
        compiler_params=params,
        cost_estimate=pl.CostEstimate(flops=2 * flops, bytes_accessed=6 << 20, transcendentals=0),
        name="second_half",
    )(
        counts, block, earlier, *far, partial,
        gain_first.reshape(1, channels), bias_first.reshape(1, channels), first_weight,
        gain_second.reshape(1, channels), bias_second.reshape(1, channels), second_weight,
    )
    return out.reshape(1, frames, rows, flat)


def solution(mesh):
    spread = P(("groups", "clip"), "tm", "space", None)
    return jax.shard_map(
        shards,
        mesh=mesh,
        in_specs=(spread, P(("groups", "clip")), P(), P(), P(), P(), P(), P()),
        out_specs=spread,
        check_vma=False,
    )
```

```python
import functools

import jax
import jax.numpy as jnp
from jax import lax
from jax.experimental import pallas as pl
from jax.experimental.pallas import tpu as pltpu
from jax.sharding import PartitionSpec as P

F32 = jnp.float32
BF16 = jnp.bfloat16
LANES = 128


def mask_kernel(channels, mask):
    lane = lax.broadcasted_iota(jnp.int32, mask.shape, 1)
    mask[...] = jnp.where(lane < channels, 1.0, 0.0)


def norm_silu_pair(t, gain, first, channels):
    square = t * t
    left = jnp.sum(jnp.where(first, square, 0.0), axis=1, keepdims=True)
    right = jnp.sum(jnp.where(first, 0.0, square), axis=1, keepdims=True)
    left = lax.rsqrt(left * (1.0 / channels) + 1e-06)
    right = lax.rsqrt(right * (1.0 / channels) + 1e-06)
    y = t * jnp.where(first, left, right) * gain
    return y * (0.5 + 0.5 * jnp.tanh(0.5 * y))


def twice(ref):
    return jnp.concatenate([ref[...], ref[...]], axis=1)


def norm_kernel(swap, mask, own, gain, normed, *rest):
    sent, stage = rest[:-1], rest[-1]
    frames, rows, pairs, wide = normed.shape
    gain_wide = twice(gain)
    first = mask[...] > 0.5
    for f in range(0, frames, 2):
        for p in range(pairs):
            lanes = pl.ds(p * wide, wide)
            t = jnp.concatenate([own[f + n, :, lanes].astype(F32) for n in range(2)], axis=0)
            y = norm_silu_pair(t, gain_wide, first, wide // 2)
            for k in range(3):
                at = pl.ds(f * rows * pairs + p, 2 * rows, stride=pairs)
                stage[k, at, :] = y[:, k * LANES : (k + 1) * LANES]
        for n in range(2):
            for r in range(rows):
                for k in range(3):
                    part = stage[k, pl.ds(((f + n) * rows + r) * pairs, pairs), :]
                    normed[f + n, r, :, k * LANES : (k + 1) * LANES] = part.astype(BF16)
    if swap:
        first = (rows - 2) * (1 - lax.axis_index("space"))
        sent[0][...] = normed[:, pl.ds(first, 2)]
    else:
        sent[0][...] = normed[:, rows - 2 :]
        sent[1][...] = normed[:, :2]


def gather_rows(window, own, before, after, keep, bands):
    frames, rows, pairs, wide = own.shape
    space = lax.axis_index("space")
    nothing = jnp.zeros((pairs, wide), BF16)
    for f in range(frames):
        good = keep(f)
        if bands == 2:
            window[f, (rows + 2) * space] = nothing
            for r in range(2):
                window[f, (rows + 1) * (1 - space) + r] = jnp.where(good, before[f, r], nothing)
            for r in range(rows):
                window[f, 1 + space + r] = jnp.where(good, own[f, r], nothing)
        else:
            for r in range(2):
                window[f, r] = jnp.where(good & (space > 0), before[f, r], nothing)
                window[f, rows + 2 + r] = jnp.where(good & (space < bands - 1), after[f, r], nothing)
            for r in range(rows):
                window[f, 2 + r] = jnp.where(good, own[f, r], nothing)


def taps(window, weight, source, frames, rows, a, channels):
    pairs, wide = window.shape[2], window.shape[3]
    lead = jnp.zeros((2 * LANES - channels, channels), BF16)
    parts = [
        window[source : source + frames, b : b + rows].reshape(frames * rows * pairs, wide)
        for b in range(3)
    ]
    rims = [weight[a, b] for b in range(3)]
    whole = jnp.concatenate(parts, axis=1)
    high = jnp.concatenate([x[:, LANES:] for x in parts], axis=1)
    low = jnp.concatenate([x[:, : 2 * LANES] for x in parts], axis=1)

    def product(left, right):
        return jnp.dot(left, jnp.concatenate(right, axis=0), preferred_element_type=F32)

    mine = (
        product(whole, [w[channels:] for w in rims]),
        product(whole, [w[: 2 * channels] for w in rims]),
    )
    moved = (
        product(high, [x for w in rims for x in (lead, w[:channels])]),
        product(low, [x for w in rims for x in (w[2 * channels :], lead)]),
    )
    return mine, moved


def add_moved(mine, moved, pairs):
    place = lax.broadcasted_iota(jnp.int32, mine[0].shape, 0) % pairs
    count = mine[0].shape[0]
    left = jnp.where(place == 0, 0.0, pltpu.roll(moved[0], 1, 0))
    right = jnp.where(place == pairs - 1, 0.0, pltpu.roll(moved[1], count - 1, 0))
    return mine[0] + left, mine[1] + right


def first_kernel(bands, deep, count, own, before, after, weight, partial, window, moved):
    frames, rows, pairs, wide = own.shape
    channels = wide // 2
    tm = lax.axis_index("tm")
    gather_rows(window, own, before, after, lambda f: tm * frames + f < count[0], bands)
    fill = deep * pairs
    for a in (2, 1, 0):
        skip = 2 - a
        new = taps(window, weight, 0, frames - skip, deep, a, channels)
        at = pl.ds(skip * fill, (frames - skip) * fill)
        for q in range(2):
            if skip == 0:
                partial[q] = new[0][q]
                moved[q] = new[1][q]
            else:
                partial[q, at, :] += new[0][q]
                moved[q, at, :] += new[1][q]
    both = add_moved([partial[q] for q in range(2)], [moved[q] for q in range(2)], pairs)
    for q in range(2):
        partial[q] = both[q]


def second_kernel(
    bands, deep, count, own, earlier, before, after, partial, bias, weight, gain_two, bias_two,
    weight_two, out, window, total, moved, hidden, final,
):
    frames, rows, pairs, wide = earlier.shape
    channels = wide // 2
    tm, space = lax.axis_index("tm"), lax.axis_index("space")
    first_frame = tm * frames
    fill = deep * pairs

    def valid(f):
        at = first_frame - frames + f
        return (at >= 0) & (at < count[0])

    gather_rows(window, earlier, before, after, valid, bands)
    for a in (0, 1, 2):
        new = taps(window, weight, a, frames - a, deep, a, channels)
        size = (frames - a) * fill
        for q in range(2):
            if a == 0:
                total[q, 0:size] = new[0][q]
                moved[q] = new[1][q]
            else:
                total[q, 0:size] += new[0][q]
                moved[q, 0:size] += new[1][q]
    both = add_moved(
        [total[q, 0 : frames * fill] for q in range(2)], [moved[q] for q in range(2)], pairs
    )
    for q in range(2):
        total[q, 0 : 2 * fill] = both[q][: 2 * fill]
        total[q, 2 * fill : 4 * fill] = both[q][2 * fill :] + partial[q, 0 : 2 * fill]
        total[q, 4 * fill :] = partial[q, 2 * fill :]

    start = (1 - space) if bands == 2 else 0
    row = lax.broadcasted_iota(jnp.int32, (fill, 1), 0) // pairs + (space * rows - 1 + start)
    row_ok = (row >= 0) & (row < bands * rows)
    bias_wide, gain_wide = twice(bias), twice(gain_two)
    first_lanes = lax.broadcasted_iota(jnp.int32, (fill, wide), 1) < channels
    for h in range(frames + 2):
        good = row_ok & valid(frames + h - 2)
        t = jnp.concatenate([total[q, h * fill : (h + 1) * fill, :] for q in range(2)], axis=1)
        t = jnp.where(good, t + bias_wide, 0.0).astype(BF16).astype(F32)
        y = norm_silu_pair(t, gain_wide, first_lanes, channels).astype(BF16)
        hidden[h, 0] = jnp.zeros((pairs, wide), BF16)
        hidden[h, rows + 1] = jnp.zeros((pairs, wide), BF16)
        for r in range(deep):
            hidden[h, start + r] = y[r * pairs : (r + 1) * pairs]

    mine, shifted = taps(hidden, weight_two, 0, frames, rows, 0, channels)
    for a in (1, 2):
        new = taps(hidden, weight_two, a, frames, rows, a, channels)
        mine = [mine[q] + new[0][q] for q in range(2)]
        shifted = [shifted[q] + new[1][q] for q in range(2)]
    both = jnp.concatenate(add_moved(mine, shifted, pairs), axis=1) + twice(bias_two)
    for k in range(3):
        final[k] = both[:, k * LANES : (k + 1) * LANES]
    for f in range(0, frames, 2):
        good = [valid(frames + f + n) for n in range(2)]
        for p in range(pairs):
            for k in range(3):
                block = final[k, pl.ds(f * rows * pairs + p, 2 * rows, stride=pairs), :]
                lanes = pl.ds(p * wide + k * LANES, LANES)
                for n in range(2):
                    value = own[f + n, :, lanes].astype(F32) + block[n * rows : (n + 1) * rows]
                    out[f + n, :, lanes] = jnp.where(good[n], value, 0.0).astype(BF16)


def shards(latents, counts, gain_first, bias_first, weight_first, gain_second, bias_second, weight_second):
    channels = gain_first.shape[0]
    frames, rows, flat = latents.shape[1:]
    wide = 2 * channels
    pairs = flat // wide
    blocks, bands = lax.axis_size("tm"), lax.axis_size("space")
    block = latents.reshape(frames, rows, flat)

    def shift(sent, step, along):
        pairs_of = [
            (t * bands + s, (t + along) % blocks * bands + (s + step) % bands)
            for t in range(blocks)
            for s in range(bands)
        ]
        return lax.ppermute(sent, ("tm", "space"), pairs_of)

    vmem = pl.BlockSpec(memory_space=pltpu.VMEM)
    smem = pl.BlockSpec(memory_space=pltpu.SMEM)
    swap = bands == 2
    rims = 1 if swap else 2
    rim = jax.ShapeDtypeStruct((frames, 2, pairs, wide), BF16)
    mask = pl.pallas_call(
        functools.partial(mask_kernel, channels),
        out_shape=jax.ShapeDtypeStruct((2 * rows, wide), F32),
        out_specs=vmem,
        cost_estimate=pl.CostEstimate(flops=4 << 30, bytes_accessed=1 << 16, transcendentals=0),
        name="lane_mask",
    )()
    normed, *sent = pl.pallas_call(
        functools.partial(norm_kernel, swap),
        out_shape=[jax.ShapeDtypeStruct((frames, rows, pairs, wide), BF16)] + [rim] * rims,
        in_specs=[vmem] * 3,
        out_specs=[vmem] * (1 + rims),
        scratch_shapes=[pltpu.VMEM((3, frames * rows * pairs, LANES), F32)],
        cost_estimate=pl.CostEstimate(flops=4 << 30, bytes_accessed=1 << 20, transcendentals=0),
        name="norm_and_cut",
    )(mask, block, gain_first.reshape(1, channels))
    earlier = shift(normed, 0, 1)
    if swap:
        near = (shift(sent[0], 1, 0),) * 2
        far = (shift(sent[0], 1, 1),) * 2
        deep = rows + 1
    else:
        near = (shift(sent[0], 1, 0), shift(sent[1], -1, 0))
        far = (shift(sent[0], 1, 1), shift(sent[1], -1, 1))
        deep = rows + 2

    fill = deep * pairs
    window = pltpu.VMEM((frames, deep + 2, pairs, wide), BF16)
    moved = pltpu.VMEM((2, frames * fill, channels), F32)
    first_weight = weight_first.reshape(3, 3, 3 * channels, channels)
    second_weight = weight_second.reshape(3, 3, 3 * channels, channels)
    params = pltpu.CompilerParams(vmem_limit_bytes=24 << 20)
    partial = pl.pallas_call(
        functools.partial(first_kernel, bands, deep),
        out_shape=jax.ShapeDtypeStruct((2, frames * fill, channels), F32),
        in_specs=[smem] + [vmem] * 4,
        out_specs=vmem,
        scratch_shapes=[window, moved],
        compiler_params=params,
        cost_estimate=pl.CostEstimate(flops=1 << 20, bytes_accessed=1 << 16, transcendentals=0),
        name="first_half",
    )(counts, normed, *near, first_weight)
    out = pl.pallas_call(
        functools.partial(second_kernel, bands, deep),
        out_shape=jax.ShapeDtypeStruct((frames, rows, flat), BF16),
        in_specs=[smem] + [vmem] * 10,
        out_specs=vmem,
        scratch_shapes=[
            window,
            pltpu.VMEM((2, (frames + 2) * fill, channels), F32),
            moved,
            pltpu.VMEM((frames + 2, rows + 2, pairs, wide), BF16),
            pltpu.VMEM((3, frames * rows * pairs, LANES), F32),
        ],
        compiler_params=params,
        cost_estimate=pl.CostEstimate(flops=4 << 30, bytes_accessed=6 << 20, transcendentals=0),
        name="second_half",
    )(
        counts, block, earlier, *far, partial,
        bias_first.reshape(1, channels), first_weight,
        gain_second.reshape(1, channels), bias_second.reshape(1, channels), second_weight,
    )
    return out.reshape(1, frames, rows, flat)


def solution(mesh):
    spread = P(("groups", "clip"), "tm", "space", None)
    return jax.shard_map(
        shards,
        mesh=mesh,
        in_specs=(spread, P(("groups", "clip")), P(), P(), P(), P(), P(), P()),
        out_specs=spread,
        check_vma=False,
    )
```

```python
import functools

import jax
import jax.numpy as jnp
from jax import lax
from jax.experimental import pallas as pl
from jax.experimental.pallas import tpu as pltpu
from jax.sharding import PartitionSpec as P

F32 = jnp.float32
BF16 = jnp.bfloat16
LANES = 128


def mask_kernel(channels, mask):
    lane = lax.broadcasted_iota(jnp.int32, mask.shape, 1)
    mask[...] = jnp.where(lane < channels, 1.0, 0.0)


def norm_silu_pair(t, gain, first, channels):
    square = t * t
    left = jnp.sum(jnp.where(first, square, 0.0), axis=1, keepdims=True)
    right = jnp.sum(jnp.where(first, 0.0, square), axis=1, keepdims=True)
    left = lax.rsqrt(left * (1.0 / channels) + 1e-06)
    right = lax.rsqrt(right * (1.0 / channels) + 1e-06)
    y = t * jnp.where(first, left, right) * gain
    return y * (0.5 + 0.5 * jnp.tanh(0.5 * y))


def twice(ref):
    return jnp.concatenate([ref[...], ref[...]], axis=1)


def norm_kernel(swap, mask, own, gain, normed, *rest):
    sent, stage = rest[:-1], rest[-1]
    frames, rows, pairs, wide = normed.shape
    gain_wide = twice(gain)
    first = mask[...] > 0.5
    for f in range(0, frames, 2):
        for p in range(pairs):
            lanes = pl.ds(p * wide, wide)
            t = jnp.concatenate([own[f + n, :, lanes].astype(F32) for n in range(2)], axis=0)
            y = norm_silu_pair(t, gain_wide, first, wide // 2)
            for k in range(3):
                at = pl.ds(f * rows * pairs + p, 2 * rows, stride=pairs)
                stage[k, at, :] = y[:, k * LANES : (k + 1) * LANES]
        for n in range(2):
            for r in range(rows):
                for k in range(3):
                    part = stage[k, pl.ds(((f + n) * rows + r) * pairs, pairs), :]
                    normed[f + n, r, :, k * LANES : (k + 1) * LANES] = part.astype(BF16)
    if swap:
        first = (rows - 2) * (1 - lax.axis_index("space"))
        sent[0][...] = normed[:, pl.ds(first, 2)]
    else:
        sent[0][...] = normed[:, rows - 2 :]
        sent[1][...] = normed[:, :2]


def gather_rows(window, own, before, after, keep, bands):
    frames, rows, pairs, wide = own.shape
    space = lax.axis_index("space")
    nothing = jnp.zeros((pairs, wide), BF16)
    for f in range(frames):
        good = keep(f)
        if bands == 2:
            window[f, (rows + 2) * space] = nothing
            for r in range(2):
                window[f, (rows + 1) * (1 - space) + r] = jnp.where(good, before[f, r], nothing)
            for r in range(rows):
                window[f, 1 + space + r] = jnp.where(good, own[f, r], nothing)
        else:
            for r in range(2):
                window[f, r] = jnp.where(good & (space > 0), before[f, r], nothing)
                window[f, rows + 2 + r] = jnp.where(good & (space < bands - 1), after[f, r], nothing)
            for r in range(rows):
                window[f, 2 + r] = jnp.where(good, own[f, r], nothing)


def taps(window, weight, source, frames, rows, a, channels):
    pairs, wide = window.shape[2], window.shape[3]
    lead = jnp.zeros((2 * LANES - channels, channels), BF16)
    parts = [
        window[source : source + frames, b : b + rows].reshape(frames * rows * pairs, wide)
        for b in range(3)
    ]
    rims = [weight[a, b] for b in range(3)]
    whole = jnp.concatenate(parts, axis=1)
    high = jnp.concatenate([x[:, LANES:] for x in parts], axis=1)
    low = jnp.concatenate([x[:, : 2 * LANES] for x in parts], axis=1)

    def product(left, right):
        return jnp.dot(left, jnp.concatenate(right, axis=0), preferred_element_type=F32)

    mine = (
        product(whole, [w[channels:] for w in rims]),
        product(whole, [w[: 2 * channels] for w in rims]),
    )
    moved = (
        product(high, [x for w in rims for x in (lead, w[:channels])]),
        product(low, [x for w in rims for x in (w[2 * channels :], lead)]),
    )
    return mine, moved


def add_moved(mine, moved, pairs):
    place = lax.broadcasted_iota(jnp.int32, mine[0].shape, 0) % pairs
    count = mine[0].shape[0]
    left = jnp.where(place == 0, 0.0, pltpu.roll(moved[0], 1, 0))
    right = jnp.where(place == pairs - 1, 0.0, pltpu.roll(moved[1], count - 1, 0))
    return mine[0] + left, mine[1] + right


def first_kernel(bands, deep, count, own, before, after, weight, partial, window, moved):
    frames, rows, pairs, wide = own.shape
    channels = wide // 2
    tm = lax.axis_index("tm")
    gather_rows(window, own, before, after, lambda f: tm * frames + f < count[0], bands)
    fill = deep * pairs
    for a in (2, 1, 0):
        skip = 2 - a
        new = taps(window, weight, 0, frames - skip, deep, a, channels)
        at = pl.ds(skip * fill, (frames - skip) * fill)
        for q in range(2):
            if skip == 0:
                partial[q] = new[0][q]
                moved[q] = new[1][q]
            else:
                partial[q, at, :] += new[0][q]
                moved[q, at, :] += new[1][q]
    both = add_moved([partial[q] for q in range(2)], [moved[q] for q in range(2)], pairs)
    for q in range(2):
        partial[q] = both[q]


def second_kernel(
    bands, deep, count, own, earlier, before, after, partial, bias, weight, gain_two, bias_two,
    weight_two, out, window, total, moved, hidden, final,
):
    frames, rows, pairs, wide = earlier.shape
    channels = wide // 2
    tm, space = lax.axis_index("tm"), lax.axis_index("space")
    first_frame = tm * frames
    fill = deep * pairs

    def valid(f):
        at = first_frame - frames + f
        return (at >= 0) & (at < count[0])

    gather_rows(window, earlier, before, after, valid, bands)
    for a in (0, 1, 2):
        new = taps(window, weight, a, frames - a, deep, a, channels)
        size = (frames - a) * fill
        for q in range(2):
            if a == 0:
                total[q, 0:size] = new[0][q]
                moved[q] = new[1][q]
            else:
                total[q, 0:size] += new[0][q]
                moved[q, 0:size] += new[1][q]
    both = add_moved(
        [total[q, 0 : frames * fill] for q in range(2)], [moved[q] for q in range(2)], pairs
    )
    for q in range(2):
        total[q, 0 : 2 * fill] = both[q][: 2 * fill]
        total[q, 2 * fill : 4 * fill] = both[q][2 * fill :] + partial[q, 0 : 2 * fill]
        total[q, 4 * fill :] = partial[q, 2 * fill :]

    start = (1 - space) if bands == 2 else 0
    row = lax.broadcasted_iota(jnp.int32, (fill, 1), 0) // pairs + (space * rows - 1 + start)
    row_ok = (row >= 0) & (row < bands * rows)
    bias_wide, gain_wide = twice(bias), twice(gain_two)
    first_lanes = lax.broadcasted_iota(jnp.int32, (fill, wide), 1) < channels
    for h in range(frames + 2):
        good = row_ok & valid(frames + h - 2)
        t = jnp.concatenate([total[q, h * fill : (h + 1) * fill, :] for q in range(2)], axis=1)
        t = jnp.where(good, t + bias_wide, 0.0).astype(BF16).astype(F32)
        y = norm_silu_pair(t, gain_wide, first_lanes, channels).astype(BF16)
        hidden[h, 0] = jnp.zeros((pairs, wide), BF16)
        hidden[h, rows + 1] = jnp.zeros((pairs, wide), BF16)
        for r in range(deep):
            hidden[h, start + r] = y[r * pairs : (r + 1) * pairs]

    mine, shifted = taps(hidden, weight_two, 0, frames, rows, 0, channels)
    for a in (1, 2):
        new = taps(hidden, weight_two, a, frames, rows, a, channels)
        mine = [mine[q] + new[0][q] for q in range(2)]
        shifted = [shifted[q] + new[1][q] for q in range(2)]
    both = jnp.concatenate(add_moved(mine, shifted, pairs), axis=1) + twice(bias_two)
    for k in range(3):
        final[k] = both[:, k * LANES : (k + 1) * LANES]
    for f in range(0, frames, 2):
        good = [valid(frames + f + n) for n in range(2)]
        for p in range(pairs):
            for k in range(3):
                block = final[k, pl.ds(f * rows * pairs + p, 2 * rows, stride=pairs), :]
                lanes = pl.ds(p * wide + k * LANES, LANES)
                for n in range(2):
                    value = own[f + n, :, lanes].astype(F32) + block[n * rows : (n + 1) * rows]
                    out[f + n, :, lanes] = jnp.where(good[n], value, 0.0).astype(BF16)


def shards(latents, counts, gain_first, bias_first, weight_first, gain_second, bias_second, weight_second):
    channels = gain_first.shape[0]
    frames, rows, flat = latents.shape[1:]
    wide = 2 * channels
    pairs = flat // wide
    blocks, bands = lax.axis_size("tm"), lax.axis_size("space")
    block = latents.reshape(frames, rows, flat)

    def shift(sent, step, along):
        pairs_of = [
            (t * bands + s, (t + along) % blocks * bands + (s + step) % bands)
            for t in range(blocks)
            for s in range(bands)
        ]
        return lax.ppermute(sent, ("tm", "space"), pairs_of)

    vmem = pl.BlockSpec(memory_space=pltpu.VMEM)
    smem = pl.BlockSpec(memory_space=pltpu.SMEM)
    params = pltpu.CompilerParams(vmem_limit_bytes=24 << 20)
    swap = bands == 2
    rims = 1 if swap else 2
    rim = jax.ShapeDtypeStruct((frames, 2, pairs, wide), BF16)
    mask = pl.pallas_call(
        functools.partial(mask_kernel, channels),
        out_shape=jax.ShapeDtypeStruct((2 * rows, wide), F32),
        out_specs=vmem,
        compiler_params=params,
        cost_estimate=pl.CostEstimate(flops=4 << 30, bytes_accessed=1 << 16, transcendentals=0),
        name="lane_mask",
    )()
    normed, *sent = pl.pallas_call(
        functools.partial(norm_kernel, swap),
        out_shape=[jax.ShapeDtypeStruct((frames, rows, pairs, wide), BF16)] + [rim] * rims,
        in_specs=[vmem] * 3,
        out_specs=[vmem] * (1 + rims),
        scratch_shapes=[pltpu.VMEM((3, frames * rows * pairs, LANES), F32)],
        compiler_params=params,
        cost_estimate=pl.CostEstimate(flops=4 << 30, bytes_accessed=1 << 20, transcendentals=0),
        name="norm_and_cut",
    )(mask, block, gain_first.reshape(1, channels))
    earlier = shift(normed, 0, 1)
    if swap:
        near = (shift(sent[0], 1, 0),) * 2
        far = (shift(sent[0], 1, 1),) * 2
        deep = rows + 1
    else:
        near = (shift(sent[0], 1, 0), shift(sent[1], -1, 0))
        far = (shift(sent[0], 1, 1), shift(sent[1], -1, 1))
        deep = rows + 2

    fill = deep * pairs
    window = pltpu.VMEM((frames, deep + 2, pairs, wide), BF16)
    moved = pltpu.VMEM((2, frames * fill, channels), F32)
    first_weight = weight_first.reshape(3, 3, 3 * channels, channels)
    second_weight = weight_second.reshape(3, 3, 3 * channels, channels)
    partial = pl.pallas_call(
        functools.partial(first_kernel, bands, deep),
        out_shape=jax.ShapeDtypeStruct((2, frames * fill, channels), F32),
        in_specs=[smem] + [vmem] * 4,
        out_specs=vmem,
        scratch_shapes=[window, moved],
        compiler_params=params,
        cost_estimate=pl.CostEstimate(flops=1 << 20, bytes_accessed=1 << 16, transcendentals=0),
        name="first_half",
    )(counts, normed, *near, first_weight)
    out = pl.pallas_call(
        functools.partial(second_kernel, bands, deep),
        out_shape=jax.ShapeDtypeStruct((frames, rows, flat), BF16),
        in_specs=[smem] + [vmem] * 10,
        out_specs=vmem,
        scratch_shapes=[
            window,
            pltpu.VMEM((2, (frames + 2) * fill, channels), F32),
            moved,
            pltpu.VMEM((frames + 2, rows + 2, pairs, wide), BF16),
            pltpu.VMEM((3, frames * rows * pairs, LANES), F32),
        ],
        compiler_params=params,
        cost_estimate=pl.CostEstimate(flops=4 << 30, bytes_accessed=6 << 20, transcendentals=0),
        name="second_half",
    )(
        counts, block, earlier, *far, partial,
        bias_first.reshape(1, channels), first_weight,
        gain_second.reshape(1, channels), bias_second.reshape(1, channels), second_weight,
    )
    return out.reshape(1, frames, rows, flat)


def solution(mesh):
    spread = P(("groups", "clip"), "tm", "space", None)
    return jax.shard_map(
        shards,
        mesh=mesh,
        in_specs=(spread, P(("groups", "clip")), P(), P(), P(), P(), P(), P()),
        out_specs=spread,
        check_vma=False,
    )
```

```python
import functools

import jax
import jax.numpy as jnp
from jax import lax
from jax.experimental import pallas as pl
from jax.experimental.pallas import tpu as pltpu
from jax.sharding import PartitionSpec as P

F32 = jnp.float32
BF16 = jnp.bfloat16
LANES = 128


def mask_kernel(channels, mask):
    lane = lax.broadcasted_iota(jnp.int32, mask.shape, 1)
    mask[...] = jnp.where(lane < channels, 1.0, 0.0)


def norm_silu_pair(t, gain, first, channels):
    square = t * t
    left = jnp.sum(jnp.where(first, square, 0.0), axis=1, keepdims=True)
    right = jnp.sum(jnp.where(first, 0.0, square), axis=1, keepdims=True)
    left = lax.rsqrt(left * (1.0 / channels) + 1e-06)
    right = lax.rsqrt(right * (1.0 / channels) + 1e-06)
    y = t * jnp.where(first, left, right) * gain
    return y * (0.5 + 0.5 * jnp.tanh(0.5 * y))


def twice(ref):
    return jnp.concatenate([ref[...], ref[...]], axis=1)


def norm_block(block, gain_wide, first, stage, store, pairs):
    frames, rows = block.shape[0], block.shape[1]
    wide = gain_wide.shape[1]
    for f in range(0, frames, 2):
        for p in range(pairs):
            lanes = pl.ds(p * wide, wide)
            t = jnp.concatenate([block[f + n, :, lanes].astype(F32) for n in range(2)], axis=0)
            y = norm_silu_pair(t, gain_wide, first, wide // 2)
            for k in range(3):
                at = pl.ds(f * rows * pairs + p, 2 * rows, stride=pairs)
                stage[k, at, :] = y[:, k * LANES : (k + 1) * LANES]
        for n in range(2):
            for r in range(rows):
                at = pl.ds(((f + n) * rows + r) * pairs, pairs)
                store(f + n, r, [stage[k, at, :].astype(BF16) for k in range(3)])


def norm_kernel(swap, mask, block, gain, normed, *rest):
    sent, stage = rest[:-1], rest[-1]
    rows, pairs = normed.shape[1], normed.shape[2]

    def store(f, r, parts):
        for k in range(3):
            normed[f, r, :, k * LANES : (k + 1) * LANES] = parts[k]

    norm_block(block, twice(gain), mask[...] > 0.5, stage, store, pairs)
    if swap:
        first = (rows - 2) * (1 - lax.axis_index("space"))
        sent[0][...] = normed[:, pl.ds(first, 2)]
    else:
        sent[0][...] = normed[:, rows - 2 :]
        sent[1][...] = normed[:, :2]


def dot(left, right):
    return jnp.dot(
        jnp.concatenate(left, axis=1), jnp.concatenate(right, axis=0), preferred_element_type=F32
    )


def products(parts, rims, channels):
    lead = jnp.zeros((2 * LANES - channels, channels), BF16)
    mine = (
        dot(parts, [w[channels:] for w in rims]),
        dot(parts, [w[: 2 * channels] for w in rims]),
    )
    high = [x[:, LANES:] for x in parts]
    low = [x[:, : 2 * LANES] for x in parts]
    moved = (
        dot(high, [x for w in rims for x in (lead, w[:channels])]),
        dot(low, [x for w in rims for x in (w[2 * channels :], lead)]),
    )
    return mine, moved


def conv(window, weight, frames, rows, channels):
    pairs, wide = window.shape[2], window.shape[3]
    taps = [(a, b) for a in range(3) for b in range(3)]
    parts = [
        window[a : a + frames, b : b + rows].reshape(frames * rows * pairs, wide) for a, b in taps
    ]
    return add_moved(*products(parts, [weight[a, b] for a, b in taps], channels), pairs)


def add_moved(mine, moved, pairs):
    place = lax.broadcasted_iota(jnp.int32, mine[0].shape, 0) % pairs
    count = mine[0].shape[0]
    left = jnp.where(place == 0, 0.0, pltpu.roll(moved[0], 1, 0))
    right = jnp.where(place == pairs - 1, 0.0, pltpu.roll(moved[1], count - 1, 0))
    return mine[0] + left, mine[1] + right


def first_kernel(
    bands, deep, count, mask, normed, earlier, before, after, gain, weight, total, window, stage
):
    frames, rows, pairs, wide = normed.shape
    tm, space = lax.axis_index("tm"), lax.axis_index("space")
    nothing = jnp.zeros((pairs, wide), BF16)
    top = 1 + space if bands == 2 else 2

    def valid(f):
        at = (tm - 1) * frames + f
        return (at >= 0) & (at < count[0])

    def store(f, r, parts):
        good = valid(f)
        for k in range(3):
            part = jnp.where(good, parts[k], jnp.zeros_like(parts[k]))
            window[f, top + r, :, k * LANES : (k + 1) * LANES] = part

    for f in range(2 * frames):
        good = valid(f)
        near = f >= frames
        if bands == 2:
            window[f, (rows + 2) * space] = nothing
            for r in range(2):
                rim = jnp.where(good, before[f - frames, r], nothing) if near else nothing
                window[f, (rows + 1) * (1 - space) + r] = rim
        else:
            for r in range(2):
                above = jnp.where(good & (space > 0), before[f - frames, r], nothing) if near else nothing
                below = (
                    jnp.where(good & (space < bands - 1), after[f - frames, r], nothing)
                    if near else nothing
                )
                window[f, r] = above
                window[f, rows + 2 + r] = below
        if near:
            for r in range(rows):
                window[f, top + r] = jnp.where(good, normed[f - frames, r], nothing)
    norm_block(earlier, twice(gain), mask[...] > 0.5, stage, store, pairs)
    both = conv(window, weight, frames + 2, deep, wide // 2)
    for q in range(2):
        total[q] = both[q].reshape(total.shape[1:])


def add_corner(total, corner, weight, side, keep, channels):
    frames, pairs, wide = corner.shape[0], corner.shape[2], corner.shape[3]
    deep = total.shape[2]
    low = (deep - 2) * side
    halo = (deep - 1) * side
    nothing = jnp.zeros((pairs, wide), BF16)
    rows = [
        [jnp.where(keep(f), corner[f, r], nothing) if f < frames else nothing for r in range(2)]
        for f in range(frames + 2)
    ]
    inner = [
        jnp.where(keep(f), corner[f, 1 - side], nothing) if f < frames else nothing
        for f in range(frames + 2)
    ]
    parts = [
        jnp.concatenate([x for f in range(frames) for x in rows[f + a]], axis=0) for a in range(3)
    ]
    added = add_moved(*products(parts, [weight[a, 2 * side] for a in range(3)], channels), pairs)
    for q in range(2):
        total[q, 0:frames, pl.ds(low, 2)] += added[q].reshape(frames, 2, pairs, channels)
    parts = [jnp.concatenate([inner[f + a] for f in range(frames)], axis=0) for a in range(3)]
    added = add_moved(*products(parts, [weight[a, 1] for a in range(3)], channels), pairs)
    for q in range(2):
        total[q, 0:frames, halo] += added[q].reshape(frames, pairs, channels)


def second_kernel(
    bands, deep, count, own, before, after, first_total, bias, weight, gain_two, bias_two,
    weight_two, out, total, hidden, final,
):
    frames, rows, pairs, wide = before.shape[0], own.shape[1], before.shape[2], before.shape[3]
    channels = wide // 2
    tm, space = lax.axis_index("tm"), lax.axis_index("space")
    fill = deep * pairs

    def valid(f):
        at = (tm - 1) * frames + f
        return (at >= 0) & (at < count[0])

    total[...] = first_total[...]
    if bands == 2:
        add_corner(total, before, weight, 1 - space, valid, channels)
    else:
        add_corner(total, before, weight, 0, lambda f: valid(f) & (space > 0), channels)
        add_corner(total, after, weight, 1, lambda f: valid(f) & (space < bands - 1), channels)

    start = (1 - space) if bands == 2 else 0
    row = lax.broadcasted_iota(jnp.int32, (fill, 1), 0) // pairs + (space * rows - 1 + start)
    row_ok = (row >= 0) & (row < bands * rows)
    bias_wide, gain_wide = twice(bias), twice(gain_two)
    first_lanes = lax.broadcasted_iota(jnp.int32, (fill, wide), 1) < channels
    for h in range(frames + 2):
        good = row_ok & valid(frames + h - 2)
        t = jnp.concatenate([total[q, h].reshape(fill, channels) for q in range(2)], axis=1)
        t = jnp.where(good, t + bias_wide, 0.0).astype(BF16).astype(F32)
        y = norm_silu_pair(t, gain_wide, first_lanes, channels).astype(BF16)
        hidden[h, 0] = jnp.zeros((pairs, wide), BF16)
        hidden[h, rows + 1] = jnp.zeros((pairs, wide), BF16)
        for r in range(deep):
            hidden[h, start + r] = y[r * pairs : (r + 1) * pairs]

    both = jnp.concatenate(conv(hidden, weight_two, frames, rows, channels), axis=1)
    both = both + twice(bias_two)
    for k in range(3):
        final[k] = both[:, k * LANES : (k + 1) * LANES]
    for f in range(0, frames, 2):
        good = [valid(frames + f + n) for n in range(2)]
        for p in range(pairs):
            for k in range(3):
                block = final[k, pl.ds(f * rows * pairs + p, 2 * rows, stride=pairs), :]
                lanes = pl.ds(p * wide + k * LANES, LANES)
                for n in range(2):
                    value = own[f + n, :, lanes].astype(F32) + block[n * rows : (n + 1) * rows]
                    out[f + n, :, lanes] = jnp.where(good[n], value, 0.0).astype(BF16)


def shards(latents, counts, gain_first, bias_first, weight_first, gain_second, bias_second, weight_second):
    channels = gain_first.shape[0]
    frames, rows, flat = latents.shape[1:]
    wide = 2 * channels
    pairs = flat // wide
    blocks, bands = lax.axis_size("tm"), lax.axis_size("space")
    block = latents.reshape(frames, rows, flat)

    def shift(sent, step, along):
        pairs_of = [
            (t * bands + s, (t + along) % blocks * bands + (s + step) % bands)
            for t in range(blocks)
            for s in range(bands)
        ]
        return lax.ppermute(sent, ("tm", "space"), pairs_of)

    vmem = pl.BlockSpec(memory_space=pltpu.VMEM)
    smem = pl.BlockSpec(memory_space=pltpu.SMEM)
    params = pltpu.CompilerParams(vmem_limit_bytes=24 << 20)
    swap = bands == 2
    rims = 1 if swap else 2
    rim = jax.ShapeDtypeStruct((frames, 2, pairs, wide), BF16)
    mask = pl.pallas_call(
        functools.partial(mask_kernel, channels),
        out_shape=jax.ShapeDtypeStruct((2 * rows, wide), F32),
        out_specs=vmem,
        compiler_params=params,
        cost_estimate=pl.CostEstimate(flops=4 << 30, bytes_accessed=1 << 16, transcendentals=0),
        name="lane_mask",
    )()
    normed, *sent = pl.pallas_call(
        functools.partial(norm_kernel, swap),
        out_shape=[jax.ShapeDtypeStruct((frames, rows, pairs, wide), BF16)] + [rim] * rims,
        in_specs=[vmem] * 3,
        out_specs=[vmem] * (1 + rims),
        scratch_shapes=[pltpu.VMEM((3, frames * rows * pairs, LANES), F32)],
        compiler_params=params,
        cost_estimate=pl.CostEstimate(flops=4 << 30, bytes_accessed=1 << 20, transcendentals=0),
        name="norm_and_cut",
    )(mask, block, gain_first.reshape(1, channels))
    earlier = shift(block, 0, 1)
    if swap:
        near = (shift(sent[0], 1, 0),) * 2
        far = (shift(sent[0], 1, 1),) * 2
        deep = rows + 1
    else:
        near = (shift(sent[0], 1, 0), shift(sent[1], -1, 0))
        far = (shift(sent[0], 1, 1), shift(sent[1], -1, 1))
        deep = rows + 2

    first_weight = weight_first.reshape(3, 3, 3 * channels, channels)
    second_weight = weight_second.reshape(3, 3, 3 * channels, channels)
    total = (2, frames + 2, deep, pairs, channels)
    first_total = pl.pallas_call(
        functools.partial(first_kernel, bands, deep),
        out_shape=jax.ShapeDtypeStruct(total, F32),
        in_specs=[smem] + [vmem] * 7,
        out_specs=vmem,
        scratch_shapes=[
            pltpu.VMEM((2 * frames, deep + 2, pairs, wide), BF16),
            pltpu.VMEM((3, frames * rows * pairs, LANES), F32),
        ],
        compiler_params=params,
        cost_estimate=pl.CostEstimate(flops=1 << 20, bytes_accessed=1 << 16, transcendentals=0),
        name="first_conv",
    )(counts, mask, normed, earlier, *near, gain_first.reshape(1, channels), first_weight)
    out = pl.pallas_call(
        functools.partial(second_kernel, bands, deep),
        out_shape=jax.ShapeDtypeStruct((frames, rows, flat), BF16),
        in_specs=[smem] + [vmem] * 9,
        out_specs=vmem,
        scratch_shapes=[
            pltpu.VMEM(total, F32),
            pltpu.VMEM((frames + 2, rows + 2, pairs, wide), BF16),
            pltpu.VMEM((3, frames * rows * pairs, LANES), F32),
        ],
        compiler_params=params,
        cost_estimate=pl.CostEstimate(flops=4 << 30, bytes_accessed=6 << 20, transcendentals=0),
        name="second_conv",
    )(
        counts, block, *far, first_total,
        bias_first.reshape(1, channels), first_weight,
        gain_second.reshape(1, channels), bias_second.reshape(1, channels), second_weight,
    )
    return out.reshape(1, frames, rows, flat)


def solution(mesh):
    spread = P(("groups", "clip"), "tm", "space", None)
    return jax.shard_map(
        shards,
        mesh=mesh,
        in_specs=(spread, P(("groups", "clip")), P(), P(), P(), P(), P(), P()),
        out_specs=spread,
        check_vma=False,
    )
```

```python
import functools

import jax
import jax.numpy as jnp
from jax import lax
from jax.experimental import pallas as pl
from jax.experimental.pallas import tpu as pltpu
from jax.sharding import PartitionSpec as P

F32 = jnp.float32
BF16 = jnp.bfloat16
LANES = 128


def mask_kernel(channels, mask):
    lane = lax.broadcasted_iota(jnp.int32, mask.shape, 1)
    mask[...] = jnp.where(lane < channels, 1.0, 0.0)


def norm_silu_pair(t, gain, first, channels):
    square = t * t
    left = jnp.sum(jnp.where(first, square, 0.0), axis=1, keepdims=True)
    right = jnp.sum(jnp.where(first, 0.0, square), axis=1, keepdims=True)
    left = lax.rsqrt(left * (1.0 / channels) + 1e-06)
    right = lax.rsqrt(right * (1.0 / channels) + 1e-06)
    y = t * jnp.where(first, left, right) * gain
    return y * (0.5 + 0.5 * jnp.tanh(0.5 * y))


def twice(ref):
    return jnp.concatenate([ref[...], ref[...]], axis=1)


def norm_block(block, gain_wide, first, stage, store, pairs):
    frames, rows = block.shape[0], block.shape[1]
    wide = gain_wide.shape[1]
    for f in range(0, frames, 2):
        for p in range(pairs):
            lanes = pl.ds(p * wide, wide)
            t = jnp.concatenate([block[f + n, :, lanes].astype(F32) for n in range(2)], axis=0)
            y = norm_silu_pair(t, gain_wide, first, wide // 2)
            for k in range(3):
                at = pl.ds(f * rows * pairs + p, 2 * rows, stride=pairs)
                stage[k, at, :] = y[:, k * LANES : (k + 1) * LANES]
        for n in range(2):
            for r in range(rows):
                at = pl.ds(((f + n) * rows + r) * pairs, pairs)
                store(f + n, r, [stage[k, at, :].astype(BF16) for k in range(3)])


def norm_kernel(swap, mask, block, gain, normed, *rest):
    sent, stage = rest[:-1], rest[-1]
    rows, pairs = normed.shape[1], normed.shape[2]

    def store(f, r, parts):
        for k in range(3):
            normed[f, r, :, k * LANES : (k + 1) * LANES] = parts[k]

    norm_block(block, twice(gain), mask[...] > 0.5, stage, store, pairs)
    if swap:
        first = (rows - 2) * (1 - lax.axis_index("space"))
        sent[0][...] = normed[:, pl.ds(first, 2)]
    else:
        sent[0][...] = normed[:, rows - 2 :]
        sent[1][...] = normed[:, :2]


def dot(left, right):
    return jnp.dot(
        jnp.concatenate(left, axis=1), jnp.concatenate(right, axis=0), preferred_element_type=F32
    )


def products(parts, rims, channels):
    lead = jnp.zeros((2 * LANES - channels, channels), BF16)
    mine = (
        dot(parts, [w[channels:] for w in rims]),
        dot(parts, [w[: 2 * channels] for w in rims]),
    )
    high = [x[:, LANES:] for x in parts]
    low = [x[:, : 2 * LANES] for x in parts]
    moved = (
        dot(high, [x for w in rims for x in (lead, w[:channels])]),
        dot(low, [x for w in rims for x in (w[2 * channels :], lead)]),
    )
    return mine, moved


def conv(window, weight, source, frames, rows, times, channels):
    pairs, wide = window.shape[2], window.shape[3]
    taps = [(a, b) for a in times for b in range(3)]
    parts = [
        window[
            source + a - times[0] : source + a - times[0] + frames, b : b + rows
        ].reshape(frames * rows * pairs, wide)
        for a, b in taps
    ]
    return add_moved(*products(parts, [weight[a, b] for a, b in taps], channels), pairs)


def add_moved(mine, moved, pairs):
    place = lax.broadcasted_iota(jnp.int32, mine[0].shape, 0) % pairs
    count = mine[0].shape[0]
    left = jnp.where(place == 0, 0.0, pltpu.roll(moved[0], 1, 0))
    right = jnp.where(place == pairs - 1, 0.0, pltpu.roll(moved[1], count - 1, 0))
    return mine[0] + left, mine[1] + right


def own_kernel(bands, deep, count, normed, before, after, weight, total, window):
    frames, rows, pairs, wide = normed.shape
    tm, space = lax.axis_index("tm"), lax.axis_index("space")
    nothing = jnp.zeros((pairs, wide), BF16)
    top = 1 + space if bands == 2 else 2
    window[0] = jnp.zeros(window.shape[1:], BF16)
    for f in range(frames):
        good = tm * frames + f < count[0]
        if bands == 2:
            window[f + 1, (rows + 2) * space] = nothing
        for r in range(2):
            if bands == 2:
                at = (rows + 1) * (1 - space) + r
                window[f + 1, at] = jnp.where(good, before[f, r], nothing)
            else:
                window[f + 1, r] = jnp.where(good & (space > 0), before[f, r], nothing)
                below = jnp.where(good & (space < bands - 1), after[f, r], nothing)
                window[f + 1, rows + 2 + r] = below
        for r in range(rows):
            window[f + 1, top + r] = jnp.where(good, normed[f, r], nothing)
    late = conv(window, weight, 1, frames - 2, deep, (0, 1, 2), wide // 2)
    soon = conv(window, weight, 0, 2, deep, (1, 2), wide // 2)
    for q in range(2):
        total[q, 0:2] = soon[q].reshape(2, *total.shape[2:])
        total[q, 2:] = late[q].reshape(frames - 2, *total.shape[2:])


def earlier_kernel(bands, deep, count, mask, earlier, gain, weight, total, window, stage):
    frames, rows = earlier.shape[0], earlier.shape[1]
    pairs, wide = window.shape[2], window.shape[3]
    tm, space = lax.axis_index("tm"), lax.axis_index("space")
    top = 1 + space if bands == 2 else 2

    def store(f, r, parts):
        good = (tm - 1) * frames + f < count[0]
        for k in range(3):
            part = jnp.where(good, parts[k], jnp.zeros_like(parts[k]))
            window[f, top + r, :, k * LANES : (k + 1) * LANES] = part

    @pl.when(tm > 0)
    def _():
        nothing = jnp.zeros((pairs, wide), BF16)
        window[frames] = jnp.zeros(window.shape[1:], BF16)
        for f in range(frames):
            if bands == 2:
                window[f, (rows + 2) * space] = nothing
            for r in range(2):
                window[f, ((rows + 1) * (1 - space) if bands == 2 else 0) + r] = nothing
                if bands != 2:
                    window[f, rows + 2 + r] = nothing
        norm_block(earlier, twice(gain), mask[...] > 0.5, stage, store, pairs)
        soon = conv(window, weight, 0, frames - 2, deep, (0, 1, 2), wide // 2)
        late = conv(window, weight, frames - 2, 2, deep, (0, 1), wide // 2)
        for q in range(2):
            total[q, 0 : frames - 2] = soon[q].reshape(frames - 2, *total.shape[2:])
            total[q, frames - 2 :] = late[q].reshape(2, *total.shape[2:])


def add_corner(total, corner, weight, side, keep, channels):
    frames, pairs, wide = corner.shape[0], corner.shape[2], corner.shape[3]
    deep = total.shape[2]
    low = (deep - 2) * side
    halo = (deep - 1) * side
    nothing = jnp.zeros((pairs, wide), BF16)
    rows = [
        [jnp.where(keep(f), corner[f, r], nothing) if f < frames else nothing for r in range(2)]
        for f in range(frames + 2)
    ]
    inner = [
        jnp.where(keep(f), corner[f, 1 - side], nothing) if f < frames else nothing
        for f in range(frames + 2)
    ]
    parts = [
        jnp.concatenate([x for f in range(frames) for x in rows[f + a]], axis=0) for a in range(3)
    ]
    added = add_moved(*products(parts, [weight[a, 2 * side] for a in range(3)], channels), pairs)
    for q in range(2):
        total[q, 0:frames, pl.ds(low, 2)] += added[q].reshape(frames, 2, pairs, channels)
    parts = [jnp.concatenate([inner[f + a] for f in range(frames)], axis=0) for a in range(3)]
    added = add_moved(*products(parts, [weight[a, 1] for a in range(3)], channels), pairs)
    for q in range(2):
        total[q, 0:frames, halo] += added[q].reshape(frames, pairs, channels)


def second_kernel(
    bands, deep, count, own, before, after, from_own, from_earlier, bias, weight, gain_two,
    bias_two, weight_two, out, total, hidden, final,
):
    frames, rows, pairs, wide = before.shape[0], own.shape[1], before.shape[2], before.shape[3]
    channels = wide // 2
    tm, space = lax.axis_index("tm"), lax.axis_index("space")
    fill = deep * pairs

    def valid(f):
        at = (tm - 1) * frames + f
        return (at >= 0) & (at < count[0])

    total[:, frames:] = from_own[:, frames - 2 :]

    @pl.when(tm == 0)
    def _():
        total[:, 2:frames] = from_own[:, : frames - 2]

    @pl.when(tm > 0)
    def _():
        total[:, :2] = from_earlier[:, :2]
        total[:, 2:frames] = from_own[:, : frames - 2] + from_earlier[:, 2:]
        if bands == 2:
            add_corner(total, before, weight, 1 - space, valid, channels)
        else:
            add_corner(total, before, weight, 0, lambda f: valid(f) & (space > 0), channels)
            add_corner(total, after, weight, 1, lambda f: valid(f) & (space < bands - 1), channels)

    start = (1 - space) if bands == 2 else 0
    row = lax.broadcasted_iota(jnp.int32, (fill, 1), 0) // pairs + (space * rows - 1 + start)
    row_ok = (row >= 0) & (row < bands * rows)
    bias_wide, gain_wide = twice(bias), twice(gain_two)
    first_lanes = lax.broadcasted_iota(jnp.int32, (fill, wide), 1) < channels

    def norm_hidden(h):
        good = row_ok & valid(frames + h - 2)
        t = jnp.concatenate([total[q, h].reshape(fill, channels) for q in range(2)], axis=1)
        t = jnp.where(good, t + bias_wide, 0.0).astype(BF16).astype(F32)
        y = norm_silu_pair(t, gain_wide, first_lanes, channels).astype(BF16)
        hidden[h, 0] = jnp.zeros((pairs, wide), BF16)
        hidden[h, rows + 1] = jnp.zeros((pairs, wide), BF16)
        for r in range(deep):
            hidden[h, start + r] = y[r * pairs : (r + 1) * pairs]

    @pl.when(tm == 0)
    def _():
        hidden[0:2] = jnp.zeros((2, *hidden.shape[1:]), BF16)

    @pl.when(tm > 0)
    def _():
        for h in range(2):
            norm_hidden(h)

    for h in range(2, frames + 2):
        norm_hidden(h)

    both = jnp.concatenate(conv(hidden, weight_two, 0, frames, rows, (0, 1, 2), channels), axis=1)
    both = both + twice(bias_two)
    for k in range(3):
        final[k] = both[:, k * LANES : (k + 1) * LANES]
    for f in range(0, frames, 2):
        good = [valid(frames + f + n) for n in range(2)]
        for p in range(pairs):
            for k in range(3):
                block = final[k, pl.ds(f * rows * pairs + p, 2 * rows, stride=pairs), :]
                lanes = pl.ds(p * wide + k * LANES, LANES)
                for n in range(2):
                    value = own[f + n, :, lanes].astype(F32) + block[n * rows : (n + 1) * rows]
                    out[f + n, :, lanes] = jnp.where(good[n], value, 0.0).astype(BF16)


def shards(latents, counts, gain_first, bias_first, weight_first, gain_second, bias_second, weight_second):
    channels = gain_first.shape[0]
    frames, rows, flat = latents.shape[1:]
    wide = 2 * channels
    pairs = flat // wide
    blocks, bands = lax.axis_size("tm"), lax.axis_size("space")
    block = latents.reshape(frames, rows, flat)

    def shift(sent, step, along):
        pairs_of = [
            (t * bands + s, (t + along) % blocks * bands + (s + step) % bands)
            for t in range(blocks)
            for s in range(bands)
        ]
        return lax.ppermute(sent, ("tm", "space"), pairs_of)

    vmem = pl.BlockSpec(memory_space=pltpu.VMEM)
    smem = pl.BlockSpec(memory_space=pltpu.SMEM)
    params = pltpu.CompilerParams(vmem_limit_bytes=24 << 20)
    swap = bands == 2
    rims = 1 if swap else 2
    rim = jax.ShapeDtypeStruct((frames, 2, pairs, wide), BF16)
    mask = pl.pallas_call(
        functools.partial(mask_kernel, channels),
        out_shape=jax.ShapeDtypeStruct((2 * rows, wide), F32),
        out_specs=vmem,
        compiler_params=params,
        cost_estimate=pl.CostEstimate(flops=4 << 30, bytes_accessed=1 << 16, transcendentals=0),
        name="lane_mask",
    )()
    normed, *sent = pl.pallas_call(
        functools.partial(norm_kernel, swap),
        out_shape=[jax.ShapeDtypeStruct((frames, rows, pairs, wide), BF16)] + [rim] * rims,
        in_specs=[vmem] * 3,
        out_specs=[vmem] * (1 + rims),
        scratch_shapes=[pltpu.VMEM((3, frames * rows * pairs, LANES), F32)],
        compiler_params=params,
        cost_estimate=pl.CostEstimate(flops=4 << 30, bytes_accessed=1 << 20, transcendentals=0),
        name="norm_and_cut",
    )(mask, block, gain_first.reshape(1, channels))
    earlier = shift(block, 0, 1)
    if swap:
        near = (shift(sent[0], 1, 0),) * 2
        far = (shift(sent[0], 1, 1),) * 2
        deep = rows + 1
    else:
        near = (shift(sent[0], 1, 0), shift(sent[1], -1, 0))
        far = (shift(sent[0], 1, 1), shift(sent[1], -1, 1))
        deep = rows + 2

    first_weight = weight_first.reshape(3, 3, 3 * channels, channels)
    second_weight = weight_second.reshape(3, 3, 3 * channels, channels)
    share = (2, frames, deep, pairs, channels)
    window = pltpu.VMEM((frames + 1, deep + 2, pairs, wide), BF16)
    stage = pltpu.VMEM((3, frames * rows * pairs, LANES), F32)
    cost = pl.CostEstimate(flops=1 << 20, bytes_accessed=1 << 16, transcendentals=0)
    from_own = pl.pallas_call(
        functools.partial(own_kernel, bands, deep),
        out_shape=jax.ShapeDtypeStruct(share, F32),
        in_specs=[smem] + [vmem] * 4,
        out_specs=vmem,
        scratch_shapes=[window],
        compiler_params=params,
        cost_estimate=cost,
        name="conv_one_own",
    )(counts, normed, *near, first_weight)
    from_earlier = pl.pallas_call(
        functools.partial(earlier_kernel, bands, deep),
        out_shape=jax.ShapeDtypeStruct(share, F32),
        in_specs=[smem] + [vmem] * 4,
        out_specs=vmem,
        scratch_shapes=[window, stage],
        compiler_params=params,
        cost_estimate=cost,
        name="conv_one_earlier",
    )(counts, mask, earlier, gain_first.reshape(1, channels), first_weight)
    out = pl.pallas_call(
        functools.partial(second_kernel, bands, deep),
        out_shape=jax.ShapeDtypeStruct((frames, rows, flat), BF16),
        in_specs=[smem] + [vmem] * 10,
        out_specs=vmem,
        scratch_shapes=[
            pltpu.VMEM((2, frames + 2, deep, pairs, channels), F32),
            pltpu.VMEM((frames + 2, rows + 2, pairs, wide), BF16),
            stage,
        ],
        compiler_params=params,
        cost_estimate=pl.CostEstimate(flops=4 << 30, bytes_accessed=6 << 20, transcendentals=0),
        name="corner_and_conv_two",
    )(
        counts, block, *far, from_own, from_earlier,
        bias_first.reshape(1, channels), first_weight,
        gain_second.reshape(1, channels), bias_second.reshape(1, channels), second_weight,
    )
    return out.reshape(1, frames, rows, flat)


def solution(mesh):
    spread = P(("groups", "clip"), "tm", "space", None)
    return jax.shard_map(
        shards,
        mesh=mesh,
        in_specs=(spread, P(("groups", "clip")), P(), P(), P(), P(), P(), P()),
        out_specs=spread,
        check_vma=False,
    )
```

```python
import functools

import jax
import jax.numpy as jnp
from jax import lax
from jax.experimental import pallas as pl
from jax.experimental.pallas import tpu as pltpu
from jax.sharding import PartitionSpec as P

F32 = jnp.float32
BF16 = jnp.bfloat16
LANES = 128


def mask_kernel(channels, mask):
    lane = lax.broadcasted_iota(jnp.int32, mask.shape, 1)
    mask[...] = jnp.where(lane < channels, 1.0, 0.0)


def norm_silu_pair(t, gain, first, channels):
    square = t * t
    left = jnp.sum(jnp.where(first, square, 0.0), axis=1, keepdims=True)
    right = jnp.sum(jnp.where(first, 0.0, square), axis=1, keepdims=True)
    left = lax.rsqrt(left * (1.0 / channels) + 1e-06)
    right = lax.rsqrt(right * (1.0 / channels) + 1e-06)
    y = t * jnp.where(first, left, right) * gain
    return y * (0.5 + 0.5 * jnp.tanh(0.5 * y))


def twice(ref):
    return jnp.concatenate([ref[...], ref[...]], axis=1)


def norm_block(block, gain_wide, first, stage, store, pairs):
    frames, rows = block.shape[0], block.shape[1]
    wide = gain_wide.shape[1]
    for f in range(0, frames, 2):
        for p in range(pairs):
            lanes = pl.ds(p * wide, wide)
            t = jnp.concatenate([block[f + n, :, lanes].astype(F32) for n in range(2)], axis=0)
            y = norm_silu_pair(t, gain_wide, first, wide // 2)
            for k in range(3):
                at = pl.ds(f * rows * pairs + p, 2 * rows, stride=pairs)
                stage[k, at, :] = y[:, k * LANES : (k + 1) * LANES]
        for n in range(2):
            for r in range(rows):
                at = pl.ds(((f + n) * rows + r) * pairs, pairs)
                store(f + n, r, [stage[k, at, :].astype(BF16) for k in range(3)])


def norm_kernel(swap, mask, block, gain, normed, *rest):
    sent, stage = rest[:-1], rest[-1]
    rows, pairs = normed.shape[1], normed.shape[2]

    def store(f, r, parts):
        for k in range(3):
            normed[f, r, :, k * LANES : (k + 1) * LANES] = parts[k]

    norm_block(block, twice(gain), mask[...] > 0.5, stage, store, pairs)
    if swap:
        first = (rows - 2) * (1 - lax.axis_index("space"))
        sent[0][...] = normed[:, pl.ds(first, 2)]
    else:
        sent[0][...] = normed[:, rows - 2 :]
        sent[1][...] = normed[:, :2]


def dot(left, right):
    return jnp.dot(
        jnp.concatenate(left, axis=1), jnp.concatenate(right, axis=0), preferred_element_type=F32
    )


def products(parts, rims, channels):
    lead = jnp.zeros((2 * LANES - channels, channels), BF16)
    mine = (
        dot(parts, [w[channels:] for w in rims]),
        dot(parts, [w[: 2 * channels] for w in rims]),
    )
    high = [x[:, LANES:] for x in parts]
    low = [x[:, : 2 * LANES] for x in parts]
    moved = (
        dot(high, [x for w in rims for x in (lead, w[:channels])]),
        dot(low, [x for w in rims for x in (w[2 * channels :], lead)]),
    )
    return mine, moved


def conv(window, weight, source, frames, rows, times, channels):
    pairs, wide = window.shape[2], window.shape[3]
    taps = [(a, b) for a in times for b in range(3)]
    parts = [
        window[
            source + a - times[0] : source + a - times[0] + frames, b : b + rows
        ].reshape(frames * rows * pairs, wide)
        for a, b in taps
    ]
    return add_moved(*products(parts, [weight[a, b] for a, b in taps], channels), pairs)


def add_moved(mine, moved, pairs):
    place = lax.broadcasted_iota(jnp.int32, mine[0].shape, 0) % pairs
    count = mine[0].shape[0]
    left = jnp.where(place == 0, 0.0, pltpu.roll(moved[0], 1, 0))
    right = jnp.where(place == pairs - 1, 0.0, pltpu.roll(moved[1], count - 1, 0))
    return mine[0] + left, mine[1] + right


def own_kernel(bands, deep, count, normed, weight, total, window):
    frames, rows, pairs, wide = normed.shape
    tm, space = lax.axis_index("tm"), lax.axis_index("space")
    nothing = jnp.zeros((pairs, wide), BF16)
    top = clear_rims(window, bands, space, rows, range(1, frames + 1))
    window[0] = jnp.zeros(window.shape[1:], BF16)
    for f in range(frames):
        good = tm * frames + f < count[0]
        for r in range(rows):
            window[f + 1, top + r] = jnp.where(good, normed[f, r], nothing)
    late = conv(window, weight, 1, frames - 2, deep, (0, 1, 2), wide // 2)
    soon = conv(window, weight, 0, 2, deep, (1, 2), wide // 2)
    for q in range(2):
        total[q, 0:2] = soon[q].reshape(2, *total.shape[2:])
        total[q, 2:] = late[q].reshape(frames - 2, *total.shape[2:])


def clear_rims(window, bands, space, rows, at):
    nothing = jnp.zeros(window.shape[2:], BF16)
    for f in at:
        if bands == 2:
            window[f, (rows + 2) * space] = nothing
            for r in range(2):
                window[f, (rows + 1) * (1 - space) + r] = nothing
        else:
            for r in range(2):
                window[f, r] = nothing
                window[f, rows + 2 + r] = nothing
    return 1 + space if bands == 2 else 2


def earlier_kernel(
    bands, deep, count, mask, earlier, gain, weight, after, total, window, stage
):
    frames, rows = earlier.shape[0], earlier.shape[1]
    pairs, wide = window.shape[2], window.shape[3]
    tm, space = lax.axis_index("tm"), lax.axis_index("space")

    @pl.when(tm > 0)
    def _():
        top = clear_rims(window, bands, space, rows, range(frames))
        window[frames] = jnp.zeros(window.shape[1:], BF16)

        def store(f, r, parts):
            good = (tm - 1) * frames + f < count[0]
            for k in range(3):
                part = jnp.where(good, parts[k], jnp.zeros_like(parts[k]))
                window[f, top + r, :, k * LANES : (k + 1) * LANES] = part

        norm_block(earlier, twice(gain), mask[...] > 0.5, stage, store, pairs)
        soon = conv(window, weight, 0, frames - 2, deep, (0, 1, 2), wide // 2)
        late = conv(window, weight, frames - 2, 2, deep, (0, 1), wide // 2)
        for q in range(2):
            total[q, 0 : frames - 2] = soon[q].reshape(frames - 2, *total.shape[2:])
            total[q, frames - 2 :] = late[q].reshape(2, *total.shape[2:])


def add_rims(total, near, far, weight, side, keep, channels):
    frames, pairs, wide = near.shape[0], near.shape[2], near.shape[3]
    deep = total.shape[2]
    low = (deep - 2) * side
    halo = (deep - 1) * side
    nothing = jnp.zeros((pairs, wide), BF16)

    def row(f, r):
        ref, at = (far, f) if f < frames else (near, f - frames)
        return jnp.where(keep(f), ref[at, r], nothing)

    rows = [[row(f, r) for r in range(2)] for f in range(2 * frames)]
    inner = [row(f, 1 - side) for f in range(2 * frames)]
    span = frames + 2
    parts = [
        jnp.concatenate([x for f in range(span) for x in rows[f + a]], axis=0) for a in range(3)
    ]
    added = add_moved(*products(parts, [weight[a, 2 * side] for a in range(3)], channels), pairs)
    for q in range(2):
        total[q, :, pl.ds(low, 2)] += added[q].reshape(span, 2, pairs, channels)
    parts = [jnp.concatenate([inner[f + a] for f in range(span)], axis=0) for a in range(3)]
    added = add_moved(*products(parts, [weight[a, 1] for a in range(3)], channels), pairs)
    for q in range(2):
        total[q, :, halo] += added[q].reshape(span, pairs, channels)


def finish(bands, count, own, near, far, bias, weight, gain_two, bias_two, weight_two, out, total, hidden, final):
    frames, rows, pairs, wide = near[0].shape[0], own.shape[1], near[0].shape[2], near[0].shape[3]
    channels = wide // 2
    deep = total.shape[2]
    tm, space = lax.axis_index("tm"), lax.axis_index("space")
    fill = deep * pairs

    def valid(f):
        at = (tm - 1) * frames + f
        return (at >= 0) & (at < count[0])

    if bands == 2:
        add_rims(total, near[0], far[0], weight, 1 - space, valid, channels)
    else:
        above = lambda f: valid(f) & (space > 0)
        below = lambda f: valid(f) & (space < bands - 1)
        add_rims(total, near[0], far[0], weight, 0, above, channels)
        add_rims(total, near[1], far[1], weight, 1, below, channels)

    start = (1 - space) if bands == 2 else 0
    row = lax.broadcasted_iota(jnp.int32, (fill, 1), 0) // pairs + (space * rows - 1 + start)
    row_ok = (row >= 0) & (row < bands * rows)
    bias_wide, gain_wide = twice(bias), twice(gain_two)
    first_lanes = lax.broadcasted_iota(jnp.int32, (fill, wide), 1) < channels
    for h in range(frames + 2):
        good = row_ok & valid(frames + h - 2)
        t = jnp.concatenate([total[q, h].reshape(fill, channels) for q in range(2)], axis=1)
        t = jnp.where(good, t + bias_wide, 0.0).astype(BF16).astype(F32)
        y = norm_silu_pair(t, gain_wide, first_lanes, channels).astype(BF16)
        hidden[h, 0] = jnp.zeros((pairs, wide), BF16)
        hidden[h, rows + 1] = jnp.zeros((pairs, wide), BF16)
        for r in range(deep):
            hidden[h, start + r] = y[r * pairs : (r + 1) * pairs]

    both = jnp.concatenate(conv(hidden, weight_two, 0, frames, rows, (0, 1, 2), channels), axis=1)
    both = both + twice(bias_two)
    for k in range(3):
        final[k] = both[:, k * LANES : (k + 1) * LANES]
    for f in range(0, frames, 2):
        good = [valid(frames + f + n) for n in range(2)]
        for p in range(pairs):
            for k in range(3):
                block = final[k, pl.ds(f * rows * pairs + p, 2 * rows, stride=pairs), :]
                lanes = pl.ds(p * wide + k * LANES, LANES)
                for n in range(2):
                    value = own[f + n, :, lanes].astype(F32) + block[n * rows : (n + 1) * rows]
                    out[f + n, :, lanes] = jnp.where(good[n], value, 0.0).astype(BF16)


def first_block_kernel(
    bands, count, own, above, below, from_own, bias, weight, gain_two, bias_two, weight_two,
    out, total, hidden, final,
):
    frames = own.shape[0]

    @pl.when(lax.axis_index("tm") == 0)
    def _():
        total[:, :2] = jnp.zeros((2, 2, *total.shape[2:]), F32)
        total[:, 2:] = from_own[...]
        near = (above, below)
        finish(
            bands, count, own, near, near, bias, weight, gain_two, bias_two, weight_two,
            out, total, hidden, final,
        )


def last_kernel(
    bands, count, own, above, below, far_above, far_below, from_own, from_earlier, first_out, bias,
    weight, gain_two, bias_two, weight_two, out, total, hidden, final,
):
    frames = own.shape[0]
    tm = lax.axis_index("tm")

    @pl.when(tm == 0)
    def _():
        out[...] = first_out[...]

    @pl.when(tm > 0)
    def _():
        total[:, :2] = from_earlier[:, :2]
        total[:, 2:frames] = from_own[:, : frames - 2] + from_earlier[:, 2:]
        total[:, frames:] = from_own[:, frames - 2 :]
        finish(
            bands, count, own, (above, below), (far_above, far_below), bias, weight, gain_two,
            bias_two, weight_two, out, total, hidden, final,
        )


def shards(latents, counts, gain_first, bias_first, weight_first, gain_second, bias_second, weight_second):
    channels = gain_first.shape[0]
    frames, rows, flat = latents.shape[1:]
    wide = 2 * channels
    pairs = flat // wide
    blocks, bands = lax.axis_size("tm"), lax.axis_size("space")
    block = latents.reshape(frames, rows, flat)

    def shift(sent, step, along):
        pairs_of = [
            (t * bands + s, (t + along) % blocks * bands + (s + step) % bands)
            for t in range(blocks)
            for s in range(bands)
        ]
        return lax.ppermute(sent, ("tm", "space"), pairs_of)

    vmem = pl.BlockSpec(memory_space=pltpu.VMEM)
    smem = pl.BlockSpec(memory_space=pltpu.SMEM)
    params = pltpu.CompilerParams(vmem_limit_bytes=24 << 20)
    swap = bands == 2
    rims = 1 if swap else 2
    rim = jax.ShapeDtypeStruct((frames, 2, pairs, wide), BF16)
    mask = pl.pallas_call(
        functools.partial(mask_kernel, channels),
        out_shape=jax.ShapeDtypeStruct((2 * rows, wide), F32),
        out_specs=vmem,
        compiler_params=params,
        cost_estimate=pl.CostEstimate(flops=4 << 30, bytes_accessed=1 << 16, transcendentals=0),
        name="lane_mask",
    )()
    normed, *sent = pl.pallas_call(
        functools.partial(norm_kernel, swap),
        out_shape=[jax.ShapeDtypeStruct((frames, rows, pairs, wide), BF16)] + [rim] * rims,
        in_specs=[vmem] * 3,
        out_specs=[vmem] * (1 + rims),
        scratch_shapes=[pltpu.VMEM((3, frames * rows * pairs, LANES), F32)],
        compiler_params=params,
        cost_estimate=pl.CostEstimate(flops=4 << 30, bytes_accessed=1 << 20, transcendentals=0),
        name="norm_and_cut",
    )(mask, block, gain_first.reshape(1, channels))
    earlier = shift(block, 0, 1)
    if swap:
        near = (shift(sent[0], 1, 0),) * 2
        far = (shift(sent[0], 1, 1),) * 2
        deep = rows + 1
    else:
        near = (shift(sent[0], 1, 0), shift(sent[1], -1, 0))
        far = (shift(sent[0], 1, 1), shift(sent[1], -1, 1))
        deep = rows + 2

    first_weight = weight_first.reshape(3, 3, 3 * channels, channels)
    second_weight = weight_second.reshape(3, 3, 3 * channels, channels)
    share = (2, frames, deep, pairs, channels)
    window = pltpu.VMEM((frames + 1, deep + 2, pairs, wide), BF16)
    stage = pltpu.VMEM((3, frames * rows * pairs, LANES), F32)
    cost = pl.CostEstimate(flops=1 << 20, bytes_accessed=1 << 16, transcendentals=0)
    from_own = pl.pallas_call(
        functools.partial(own_kernel, bands, deep),
        out_shape=jax.ShapeDtypeStruct(share, F32),
        in_specs=[smem] + [vmem] * 2,
        out_specs=vmem,
        scratch_shapes=[window],
        compiler_params=params,
        cost_estimate=cost,
        name="conv_one_own",
    )(counts, normed, first_weight)
    constants = (
        bias_first.reshape(1, channels), first_weight,
        gain_second.reshape(1, channels), bias_second.reshape(1, channels), second_weight,
    )
    result = jax.ShapeDtypeStruct((frames, rows, flat), BF16)
    scratch = [
        pltpu.VMEM((2, frames + 2, deep, pairs, channels), F32),
        pltpu.VMEM((frames + 2, rows + 2, pairs, wide), BF16),
        stage,
    ]
    first_out = pl.pallas_call(
        functools.partial(first_block_kernel, bands),
        out_shape=result,
        in_specs=[smem] + [vmem] * 9,
        out_specs=vmem,
        scratch_shapes=scratch,
        compiler_params=params,
        cost_estimate=cost,
        name="first_block",
    )(counts, block, *near, from_own, *constants)
    from_earlier = pl.pallas_call(
        functools.partial(earlier_kernel, bands, deep),
        out_shape=jax.ShapeDtypeStruct(share, F32),
        in_specs=[smem] + [vmem] * 5,
        out_specs=vmem,
        scratch_shapes=[window, stage],
        compiler_params=params,
        cost_estimate=cost,
        name="conv_one_earlier",
    )(counts, mask, earlier, gain_first.reshape(1, channels), first_weight, first_out)
    out = pl.pallas_call(
        functools.partial(last_kernel, bands),
        out_shape=result,
        in_specs=[smem] + [vmem] * 13,
        out_specs=vmem,
        scratch_shapes=scratch,
        compiler_params=params,
        cost_estimate=pl.CostEstimate(flops=4 << 30, bytes_accessed=6 << 20, transcendentals=0),
        name="last",
    )(counts, block, *near, *far, from_own, from_earlier, first_out, *constants)
    return out.reshape(1, frames, rows, flat)


def solution(mesh):
    spread = P(("groups", "clip"), "tm", "space", None)
    return jax.shard_map(
        shards,
        mesh=mesh,
        in_specs=(spread, P(("groups", "clip")), P(), P(), P(), P(), P(), P()),
        out_specs=spread,
        check_vma=False,
    )
```

```python
import functools

import jax
import jax.numpy as jnp
from jax import lax
from jax.experimental import pallas as pl
from jax.experimental.pallas import tpu as pltpu
from jax.sharding import PartitionSpec as P

F32 = jnp.float32
BF16 = jnp.bfloat16
LANES = 128


def mask_kernel(channels, mask):
    lane = lax.broadcasted_iota(jnp.int32, mask.shape, 1)
    mask[...] = jnp.where(lane < channels, 1.0, 0.0)


def norm_silu_pair(t, gain, first, channels):
    square = t * t
    left = jnp.sum(jnp.where(first, square, 0.0), axis=1, keepdims=True)
    right = jnp.sum(jnp.where(first, 0.0, square), axis=1, keepdims=True)
    left = lax.rsqrt(left * (1.0 / channels) + 1e-06)
    right = lax.rsqrt(right * (1.0 / channels) + 1e-06)
    y = t * jnp.where(first, left, right) * gain
    return y * (0.5 + 0.5 * jnp.tanh(0.5 * y))


def twice(ref):
    return jnp.concatenate([ref[...], ref[...]], axis=1)


def norm_block(block, gain_wide, first, stage, store, pairs):
    frames, rows = block.shape[0], block.shape[1]
    wide = gain_wide.shape[1]
    for f in range(0, frames, 2):
        for p in range(pairs):
            lanes = pl.ds(p * wide, wide)
            t = jnp.concatenate([block[f + n, :, lanes].astype(F32) for n in range(2)], axis=0)
            y = norm_silu_pair(t, gain_wide, first, wide // 2)
            for k in range(3):
                at = pl.ds(f * rows * pairs + p, 2 * rows, stride=pairs)
                stage[k, at, :] = y[:, k * LANES : (k + 1) * LANES]
        for n in range(2):
            for r in range(rows):
                at = pl.ds(((f + n) * rows + r) * pairs, pairs)
                store(f + n, r, [stage[k, at, :].astype(BF16) for k in range(3)])


def norm_kernel(swap, mask, block, gain, normed, *rest):
    sent, stage = rest[:-1], rest[-1]
    rows, pairs = normed.shape[1], normed.shape[2]

    def store(f, r, parts):
        for k in range(3):
            normed[f, r, :, k * LANES : (k + 1) * LANES] = parts[k]

    norm_block(block, twice(gain), mask[...] > 0.5, stage, store, pairs)
    if swap:
        first = (rows - 2) * (1 - lax.axis_index("space"))
        sent[0][...] = normed[:, pl.ds(first, 2)]
    else:
        sent[0][...] = normed[:, rows - 2 :]
        sent[1][...] = normed[:, :2]


def dot(left, right):
    return jnp.dot(
        jnp.concatenate(left, axis=1), jnp.concatenate(right, axis=0), preferred_element_type=F32
    )


def products(parts, rims, channels):
    lead = jnp.zeros((2 * LANES - channels, channels), BF16)
    mine = (
        dot(parts, [w[channels:] for w in rims]),
        dot(parts, [w[: 2 * channels] for w in rims]),
    )
    high = [x[:, LANES:] for x in parts]
    low = [x[:, : 2 * LANES] for x in parts]
    moved = (
        dot(high, [x for w in rims for x in (lead, w[:channels])]),
        dot(low, [x for w in rims for x in (w[2 * channels :], lead)]),
    )
    return mine, moved


def conv(window, weight, source, frames, rows, times, channels):
    pairs, wide = window[0].shape[1:]
    taps = [(a, b) for a in times for b in range(3)]

    def patch(a, b):
        at = source + a - times[0]
        rows_of = [window[f][b : b + rows].reshape(rows * pairs, wide) for f in range(at, at + frames)]
        return jnp.concatenate(rows_of, axis=0)

    parts = [patch(a, b) for a, b in taps]
    return add_moved(*products(parts, [weight[a, b] for a, b in taps], channels), pairs)


def add_moved(mine, moved, pairs):
    place = lax.broadcasted_iota(jnp.int32, mine[0].shape, 0) % pairs
    count = mine[0].shape[0]
    left = jnp.where(place == 0, 0.0, pltpu.roll(moved[0], 1, 0))
    right = jnp.where(place == pairs - 1, 0.0, pltpu.roll(moved[1], count - 1, 0))
    return mine[0] + left, mine[1] + right


def own_kernel(bands, deep, count, normed, weight, total, window):
    frames, rows, pairs, wide = normed.shape
    tm, space = lax.axis_index("tm"), lax.axis_index("space")
    nothing = jnp.zeros((pairs, wide), BF16)
    top = clear_rims(window, bands, space, rows, range(1, frames + 1))
    window[0] = jnp.zeros(window.shape[1:], BF16)
    for f in range(frames):
        good = tm * frames + f < count[0]
        for r in range(rows):
            window[f + 1, top + r] = jnp.where(good, normed[f, r], nothing)
    late = conv([window.at[f] for f in range(frames + 1)], weight, 1, frames - 2, deep, (0, 1, 2), wide // 2)
    soon = conv([window.at[f] for f in range(frames + 1)], weight, 0, 2, deep, (1, 2), wide // 2)
    for q in range(2):
        total[q, 0:2] = soon[q].reshape(2, *total.shape[2:])
        total[q, 2:] = late[q].reshape(frames - 2, *total.shape[2:])


def clear_rims(window, bands, space, rows, at):
    nothing = jnp.zeros(window.shape[2:], BF16)
    for f in at:
        if bands == 2:
            window[f, (rows + 2) * space] = nothing
            for r in range(2):
                window[f, (rows + 1) * (1 - space) + r] = nothing
        else:
            for r in range(2):
                window[f, r] = nothing
                window[f, rows + 2 + r] = nothing
    return 1 + space if bands == 2 else 2


def earlier_kernel(
    bands, deep, count, mask, earlier, gain, weight, after, total, window, stage
):
    frames, rows = earlier.shape[0], earlier.shape[1]
    pairs, wide = window.shape[2], window.shape[3]
    tm, space = lax.axis_index("tm"), lax.axis_index("space")

    @pl.when(tm > 0)
    def _():
        top = clear_rims(window, bands, space, rows, range(frames))
        window[frames] = jnp.zeros(window.shape[1:], BF16)

        def store(f, r, parts):
            good = (tm - 1) * frames + f < count[0]
            for k in range(3):
                part = jnp.where(good, parts[k], jnp.zeros_like(parts[k]))
                window[f, top + r, :, k * LANES : (k + 1) * LANES] = part

        norm_block(earlier, twice(gain), mask[...] > 0.5, stage, store, pairs)
        soon = conv([window.at[f] for f in range(frames + 1)], weight, 0, frames - 2, deep, (0, 1, 2), wide // 2)
        late = conv([window.at[f] for f in range(frames + 1)], weight, frames - 2, 2, deep, (0, 1), wide // 2)
        for q in range(2):
            total[q, 0 : frames - 2] = soon[q].reshape(frames - 2, *total.shape[2:])
            total[q, frames - 2 :] = late[q].reshape(2, *total.shape[2:])


def add_rims(total, near, far, weight, side, keep, channels):
    frames, pairs, wide = near.shape[0], near.shape[2], near.shape[3]
    deep = total.shape[2]
    low = (deep - 2) * side
    halo = (deep - 1) * side
    nothing = jnp.zeros((pairs, wide), BF16)

    def row(f, r):
        ref, at = (far, f) if f < frames else (near, f - frames)
        return jnp.where(keep(f), ref[at, r], nothing)

    rows = [[row(f, r) for r in range(2)] for f in range(2 * frames)]
    inner = [row(f, 1 - side) for f in range(2 * frames)]
    span = frames + 2
    parts = [
        jnp.concatenate([x for f in range(span) for x in rows[f + a]], axis=0) for a in range(3)
    ]
    added = add_moved(*products(parts, [weight[a, 2 * side] for a in range(3)], channels), pairs)
    for q in range(2):
        total[q, :, pl.ds(low, 2)] += added[q].reshape(span, 2, pairs, channels)
    parts = [jnp.concatenate([inner[f + a] for f in range(span)], axis=0) for a in range(3)]
    added = add_moved(*products(parts, [weight[a, 1] for a in range(3)], channels), pairs)
    for q in range(2):
        total[q, :, halo] += added[q].reshape(span, pairs, channels)


def finish(bands, count, own, near, far, bias, weight, gain_two, bias_two, weight_two, out, total, hidden, final):
    frames, rows, pairs, wide = near[0].shape[0], own.shape[1], near[0].shape[2], near[0].shape[3]
    channels = wide // 2
    deep = total.shape[2]
    tm, space = lax.axis_index("tm"), lax.axis_index("space")
    fill = deep * pairs

    def valid(f):
        at = (tm - 1) * frames + f
        return (at >= 0) & (at < count[0])

    if bands == 2:
        add_rims(total, near[0], far[0], weight, 1 - space, valid, channels)
    else:
        above = lambda f: valid(f) & (space > 0)
        below = lambda f: valid(f) & (space < bands - 1)
        add_rims(total, near[0], far[0], weight, 0, above, channels)
        add_rims(total, near[1], far[1], weight, 1, below, channels)

    start = (1 - space) if bands == 2 else 0
    row = lax.broadcasted_iota(jnp.int32, (fill, 1), 0) // pairs + (space * rows - 1 + start)
    row_ok = (row >= 0) & (row < bands * rows)
    bias_wide, gain_wide = twice(bias), twice(gain_two)
    first_lanes = lax.broadcasted_iota(jnp.int32, (fill, wide), 1) < channels

    def norm_hidden(h):
        good = row_ok & valid(frames + h - 2)
        t = jnp.concatenate([total[q, h].reshape(fill, channels) for q in range(2)], axis=1)
        t = jnp.where(good, t + bias_wide, 0.0).astype(BF16).astype(F32)
        y = norm_silu_pair(t, gain_wide, first_lanes, channels).astype(BF16)
        hidden[h][0] = jnp.zeros((pairs, wide), BF16)
        hidden[h][rows + 1] = jnp.zeros((pairs, wide), BF16)
        for r in range(deep):
            hidden[h][start + r] = y[r * pairs : (r + 1) * pairs]

    def second_conv(f):
        both = conv(hidden, weight_two, f, 2, rows, (0, 1, 2), channels)
        both = jnp.concatenate(both, axis=1) + bias_two_wide
        for k in range(3):
            final[f // 2][k] = both[:, k * LANES : (k + 1) * LANES]

    def emit(f):
        good = [valid(frames + f + n) for n in range(2)]
        for p in range(pairs):
            for k in range(3):
                block = final[f // 2][k, pl.ds(p, 2 * rows, stride=pairs), :]
                lanes = pl.ds(p * wide + k * LANES, LANES)
                for n in range(2):
                    value = own[f + n, :, lanes].astype(F32) + block[n * rows : (n + 1) * rows]
                    out[f + n, :, lanes] = jnp.where(good[n], value, 0.0).astype(BF16)

    bias_two_wide = twice(bias_two)
    for h in range(4):
        norm_hidden(h)
    second_conv(0)
    for f in range(2, frames, 2):
        norm_hidden(f + 2)
        norm_hidden(f + 3)
        emit(f - 2)
        second_conv(f)
    emit(frames - 2)


def first_block_kernel(
    bands, count, own, above, below, from_own, bias, weight, gain_two, bias_two, weight_two,
    out, total, *scratch,
):
    frames = own.shape[0]
    hidden, final = scratch[: frames + 2], scratch[frames + 2 :]

    @pl.when(lax.axis_index("tm") == 0)
    def _():
        total[:, :2] = jnp.zeros((2, 2, *total.shape[2:]), F32)
        total[:, 2:] = from_own[...]
        near = (above, below)
        finish(
            bands, count, own, near, near, bias, weight, gain_two, bias_two, weight_two,
            out, total, hidden, final,
        )


def last_kernel(
    bands, count, own, above, below, far_above, far_below, from_own, from_earlier, first_out, bias,
    weight, gain_two, bias_two, weight_two, out, total, *scratch,
):
    frames = own.shape[0]
    hidden, final = scratch[: frames + 2], scratch[frames + 2 :]
    tm = lax.axis_index("tm")

    @pl.when(tm == 0)
    def _():
        out[...] = first_out[...]

    @pl.when(tm > 0)
    def _():
        total[:, :2] = from_earlier[:, :2]
        total[:, 2:frames] = from_own[:, : frames - 2] + from_earlier[:, 2:]
        total[:, frames:] = from_own[:, frames - 2 :]
        finish(
            bands, count, own, (above, below), (far_above, far_below), bias, weight, gain_two,
            bias_two, weight_two, out, total, hidden, final,
        )


def shards(latents, counts, gain_first, bias_first, weight_first, gain_second, bias_second, weight_second):
    channels = gain_first.shape[0]
    frames, rows, flat = latents.shape[1:]
    wide = 2 * channels
    pairs = flat // wide
    blocks, bands = lax.axis_size("tm"), lax.axis_size("space")
    block = latents.reshape(frames, rows, flat)

    def shift(sent, step, along):
        pairs_of = [
            (t * bands + s, (t + along) % blocks * bands + (s + step * (t + along < blocks)) % bands)
            for t in range(blocks)
            for s in range(bands)
        ]
        return lax.ppermute(sent, ("tm", "space"), pairs_of)

    vmem = pl.BlockSpec(memory_space=pltpu.VMEM)
    smem = pl.BlockSpec(memory_space=pltpu.SMEM)
    params = pltpu.CompilerParams(vmem_limit_bytes=24 << 20)
    swap = bands == 2
    rims = 1 if swap else 2
    rim = jax.ShapeDtypeStruct((frames, 2, pairs, wide), BF16)
    mask = pl.pallas_call(
        functools.partial(mask_kernel, channels),
        out_shape=jax.ShapeDtypeStruct((2 * rows, wide), F32),
        out_specs=vmem,
        compiler_params=params,
        cost_estimate=pl.CostEstimate(flops=4 << 30, bytes_accessed=1 << 16, transcendentals=0),
        name="lane_mask",
    )()
    normed, *sent = pl.pallas_call(
        functools.partial(norm_kernel, swap),
        out_shape=[jax.ShapeDtypeStruct((frames, rows, pairs, wide), BF16)] + [rim] * rims,
        in_specs=[vmem] * 3,
        out_specs=[vmem] * (1 + rims),
        scratch_shapes=[pltpu.VMEM((3, frames * rows * pairs, LANES), F32)],
        compiler_params=params,
        cost_estimate=pl.CostEstimate(flops=4 << 30, bytes_accessed=1 << 20, transcendentals=0),
        name="norm_and_cut",
    )(mask, block, gain_first.reshape(1, channels))
    earlier = shift(block, 0, 1)
    if swap:
        near = (shift(sent[0], 1, 0),) * 2
        far = (shift(sent[0], 1, 1),) * 2
        deep = rows + 1
    else:
        near = (shift(sent[0], 1, 0), shift(sent[1], -1, 0))
        far = (shift(sent[0], 1, 1), shift(sent[1], -1, 1))
        deep = rows + 2

    first_weight = weight_first.reshape(3, 3, 3 * channels, channels)
    second_weight = weight_second.reshape(3, 3, 3 * channels, channels)
    share = (2, frames, deep, pairs, channels)
    window = pltpu.VMEM((frames + 1, deep + 2, pairs, wide), BF16)
    stage = pltpu.VMEM((3, frames * rows * pairs, LANES), F32)
    cost = pl.CostEstimate(flops=1 << 20, bytes_accessed=1 << 16, transcendentals=0)
    from_own = pl.pallas_call(
        functools.partial(own_kernel, bands, deep),
        out_shape=jax.ShapeDtypeStruct(share, F32),
        in_specs=[smem] + [vmem] * 2,
        out_specs=vmem,
        scratch_shapes=[window],
        compiler_params=params,
        cost_estimate=cost,
        name="conv_one_own",
    )(counts, normed, first_weight)
    constants = (
        bias_first.reshape(1, channels), first_weight,
        gain_second.reshape(1, channels), bias_second.reshape(1, channels), second_weight,
    )
    result = jax.ShapeDtypeStruct((frames, rows, flat), BF16)
    scratch = [
        pltpu.VMEM((2, frames + 2, deep, pairs, channels), F32),
        *[pltpu.VMEM((rows + 2, pairs, wide), BF16)] * (frames + 2),
        *[pltpu.VMEM((3, 2 * rows * pairs, LANES), F32)] * (frames // 2),
    ]
    first_out = pl.pallas_call(
        functools.partial(first_block_kernel, bands),
        out_shape=result,
        in_specs=[smem] + [vmem] * 9,
        out_specs=vmem,
        scratch_shapes=scratch,
        compiler_params=params,
        cost_estimate=cost,
        name="first_block",
    )(counts, block, *near, from_own, *constants)
    from_earlier = pl.pallas_call(
        functools.partial(earlier_kernel, bands, deep),
        out_shape=jax.ShapeDtypeStruct(share, F32),
        in_specs=[smem] + [vmem] * 5,
        out_specs=vmem,
        scratch_shapes=[window, stage],
        compiler_params=params,
        cost_estimate=cost,
        name="conv_one_earlier",
    )(counts, mask, earlier, gain_first.reshape(1, channels), first_weight, first_out)
    out = pl.pallas_call(
        functools.partial(last_kernel, bands),
        out_shape=result,
        in_specs=[smem] + [vmem] * 13,
        out_specs=vmem,
        scratch_shapes=scratch,
        compiler_params=params,
        cost_estimate=pl.CostEstimate(flops=4 << 30, bytes_accessed=6 << 20, transcendentals=0),
        name="last",
    )(counts, block, *near, *far, from_own, from_earlier, first_out, *constants)
    return out.reshape(1, frames, rows, flat)


def solution(mesh):
    spread = P(("groups", "clip"), "tm", "space", None)
    return jax.shard_map(
        shards,
        mesh=mesh,
        in_specs=(spread, P(("groups", "clip")), P(), P(), P(), P(), P(), P()),
        out_specs=spread,
        check_vma=False,
    )
```

```python
import functools

import jax
import jax.numpy as jnp
from jax import lax
from jax.experimental import pallas as pl
from jax.experimental.pallas import tpu as pltpu
from jax.sharding import PartitionSpec as P

F32 = jnp.float32
BF16 = jnp.bfloat16
LANES = 128


def mask_kernel(channels, mask):
    lane = lax.broadcasted_iota(jnp.int32, mask.shape, 1)
    mask[...] = jnp.where(lane < channels, 1.0, 0.0)


def norm_silu_pair(t, gain, first, channels):
    square = t * t
    left = jnp.sum(jnp.where(first, square, 0.0), axis=1, keepdims=True)
    right = jnp.sum(jnp.where(first, 0.0, square), axis=1, keepdims=True)
    left = lax.rsqrt(left * (1.0 / channels) + 1e-06)
    right = lax.rsqrt(right * (1.0 / channels) + 1e-06)
    y = t * jnp.where(first, left, right) * gain
    return y * (0.5 + 0.5 * jnp.tanh(0.5 * y))


def twice(ref):
    return jnp.concatenate([ref[...], ref[...]], axis=1)


def norm_block(block, gain_wide, first, stage, store, pairs):
    frames, rows = block.shape[0], block.shape[1]
    wide = gain_wide.shape[1]
    for f in range(0, frames, 2):
        for p in range(pairs):
            lanes = pl.ds(p * wide, wide)
            t = jnp.concatenate([block[f + n, :, lanes].astype(F32) for n in range(2)], axis=0)
            y = norm_silu_pair(t, gain_wide, first, wide // 2)
            for k in range(3):
                at = pl.ds(f * rows * pairs + p, 2 * rows, stride=pairs)
                stage[k, at, :] = y[:, k * LANES : (k + 1) * LANES]
        for n in range(2):
            for r in range(rows):
                at = pl.ds(((f + n) * rows + r) * pairs, pairs)
                store(f + n, r, [stage[k, at, :].astype(BF16) for k in range(3)])


def norm_kernel(swap, mask, block, gain, normed, *rest):
    sent, stage = rest[:-1], rest[-1]
    rows, pairs = normed.shape[1], normed.shape[2]

    def store(f, r, parts):
        for k in range(3):
            normed[f, r, :, k * LANES : (k + 1) * LANES] = parts[k]

    norm_block(block, twice(gain), mask[...] > 0.5, stage, store, pairs)
    if swap:
        first = (rows - 2) * (1 - lax.axis_index("space"))
        sent[0][...] = normed[:, pl.ds(first, 2)]
    else:
        sent[0][...] = normed[:, rows - 2 :]
        sent[1][...] = normed[:, :2]


def dot(left, right):
    return jnp.dot(
        jnp.concatenate(left, axis=1), jnp.concatenate(right, axis=0), preferred_element_type=F32
    )


def products(parts, rims, channels):
    lead = jnp.zeros((2 * LANES - channels, channels), BF16)
    mine = (
        dot(parts, [w[channels:] for w in rims]),
        dot(parts, [w[: 2 * channels] for w in rims]),
    )
    high = [x[:, LANES:] for x in parts]
    low = [x[:, : 2 * LANES] for x in parts]
    moved = (
        dot(high, [x for w in rims for x in (lead, w[:channels])]),
        dot(low, [x for w in rims for x in (w[2 * channels :], lead)]),
    )
    return mine, moved


def conv(window, weight, source, frames, rows, times, channels):
    pairs, wide = window[0].shape[1:]
    taps = [(a, b) for a in times for b in range(3)]

    def patch(a, b):
        at = source + a - times[0]
        rows_of = [window[f][b : b + rows].reshape(rows * pairs, wide) for f in range(at, at + frames)]
        return jnp.concatenate(rows_of, axis=0)

    parts = [patch(a, b) for a, b in taps]
    return add_moved(*products(parts, [weight[a, b] for a, b in taps], channels), pairs)


def add_moved(mine, moved, pairs):
    place = lax.broadcasted_iota(jnp.int32, mine[0].shape, 0) % pairs
    count = mine[0].shape[0]
    left = jnp.where(place == 0, 0.0, pltpu.roll(moved[0], 1, 0))
    right = jnp.where(place == pairs - 1, 0.0, pltpu.roll(moved[1], count - 1, 0))
    return mine[0] + left, mine[1] + right


def own_kernel(bands, deep, count, normed, weight, *rest):
    number = (len(rest) - 2) // 2
    sent, total, later, window = rest[:number], rest[number], rest[number + 1 : -1], rest[-1]
    for old, new in zip(sent, later):
        new[...] = old[...]
    frames, rows, pairs, wide = normed.shape
    tm, space = lax.axis_index("tm"), lax.axis_index("space")
    nothing = jnp.zeros((pairs, wide), BF16)
    top = clear_rims(window, bands, space, rows, range(1, frames + 1))
    window[0] = jnp.zeros(window.shape[1:], BF16)
    for f in range(frames):
        good = tm * frames + f < count[0]
        for r in range(rows):
            window[f + 1, top + r] = jnp.where(good, normed[f, r], nothing)
    late = conv([window.at[f] for f in range(frames + 1)], weight, 1, frames - 2, deep, (0, 1, 2), wide // 2)
    soon = conv([window.at[f] for f in range(frames + 1)], weight, 0, 2, deep, (1, 2), wide // 2)
    for q in range(2):
        total[q, 0:2] = soon[q].reshape(2, *total.shape[2:])
        total[q, 2:] = late[q].reshape(frames - 2, *total.shape[2:])


def clear_rims(window, bands, space, rows, at):
    nothing = jnp.zeros(window.shape[2:], BF16)
    for f in at:
        if bands == 2:
            window[f, (rows + 2) * space] = nothing
            for r in range(2):
                window[f, (rows + 1) * (1 - space) + r] = nothing
        else:
            for r in range(2):
                window[f, r] = nothing
                window[f, rows + 2 + r] = nothing
    return 1 + space if bands == 2 else 2


def earlier_kernel(
    bands, deep, count, mask, earlier, gain, weight, after, total, window, stage
):
    frames, rows = earlier.shape[0], earlier.shape[1]
    pairs, wide = window.shape[2], window.shape[3]
    tm, space = lax.axis_index("tm"), lax.axis_index("space")

    @pl.when(tm > 0)
    def _():
        top = clear_rims(window, bands, space, rows, range(frames))
        window[frames] = jnp.zeros(window.shape[1:], BF16)

        def store(f, r, parts):
            good = (tm - 1) * frames + f < count[0]
            for k in range(3):
                part = jnp.where(good, parts[k], jnp.zeros_like(parts[k]))
                window[f, top + r, :, k * LANES : (k + 1) * LANES] = part

        norm_block(earlier, twice(gain), mask[...] > 0.5, stage, store, pairs)
        soon = conv([window.at[f] for f in range(frames + 1)], weight, 0, frames - 2, deep, (0, 1, 2), wide // 2)
        late = conv([window.at[f] for f in range(frames + 1)], weight, frames - 2, 2, deep, (0, 1), wide // 2)
        for q in range(2):
            total[q, 0 : frames - 2] = soon[q].reshape(frames - 2, *total.shape[2:])
            total[q, frames - 2 :] = late[q].reshape(2, *total.shape[2:])


def add_rims(total, near, far, weight, side, keep, channels):
    frames, pairs, wide = near.shape[0], near.shape[2], near.shape[3]
    deep = total.shape[2]
    low = (deep - 2) * side
    halo = (deep - 1) * side
    nothing = jnp.zeros((pairs, wide), BF16)

    def row(f, r):
        ref, at = (far, f) if f < frames else (near, f - frames)
        return jnp.where(keep(f), ref[at, r], nothing)

    rows = [[row(f, r) for r in range(2)] for f in range(2 * frames)]
    inner = [row(f, 1 - side) for f in range(2 * frames)]
    span = frames + 2
    parts = [
        jnp.concatenate([x for f in range(span) for x in rows[f + a]], axis=0) for a in range(3)
    ]
    added = add_moved(*products(parts, [weight[a, 2 * side] for a in range(3)], channels), pairs)
    for q in range(2):
        total[q, :, pl.ds(low, 2)] += added[q].reshape(span, 2, pairs, channels)
    parts = [jnp.concatenate([inner[f + a] for f in range(span)], axis=0) for a in range(3)]
    added = add_moved(*products(parts, [weight[a, 1] for a in range(3)], channels), pairs)
    for q in range(2):
        total[q, :, halo] += added[q].reshape(span, pairs, channels)


def finish(bands, count, own, near, far, bias, weight, gain_two, bias_two, weight_two, out, total, hidden, final):
    frames, rows, pairs, wide = near[0].shape[0], own.shape[1], near[0].shape[2], near[0].shape[3]
    channels = wide // 2
    deep = total.shape[2]
    tm, space = lax.axis_index("tm"), lax.axis_index("space")
    fill = deep * pairs

    def valid(f):
        at = (tm - 1) * frames + f
        return (at >= 0) & (at < count[0])

    if bands == 2:
        add_rims(total, near[0], far[0], weight, 1 - space, valid, channels)
    else:
        above = lambda f: valid(f) & (space > 0)
        below = lambda f: valid(f) & (space < bands - 1)
        add_rims(total, near[0], far[0], weight, 0, above, channels)
        add_rims(total, near[1], far[1], weight, 1, below, channels)

    start = (1 - space) if bands == 2 else 0
    row = lax.broadcasted_iota(jnp.int32, (fill, 1), 0) // pairs + (space * rows - 1 + start)
    row_ok = (row >= 0) & (row < bands * rows)
    bias_wide, gain_wide = twice(bias), twice(gain_two)
    first_lanes = lax.broadcasted_iota(jnp.int32, (fill, wide), 1) < channels

    def norm_hidden(h):
        good = row_ok & valid(frames + h - 2)
        t = jnp.concatenate([total[q, h].reshape(fill, channels) for q in range(2)], axis=1)
        t = jnp.where(good, t + bias_wide, 0.0).astype(BF16).astype(F32)
        y = norm_silu_pair(t, gain_wide, first_lanes, channels).astype(BF16)
        hidden[h][0] = jnp.zeros((pairs, wide), BF16)
        hidden[h][rows + 1] = jnp.zeros((pairs, wide), BF16)
        for r in range(deep):
            hidden[h][start + r] = y[r * pairs : (r + 1) * pairs]

    def second_conv(f):
        both = conv(hidden, weight_two, f, 2, rows, (0, 1, 2), channels)
        both = jnp.concatenate(both, axis=1) + bias_two_wide
        for k in range(3):
            final[f // 2][k] = both[:, k * LANES : (k + 1) * LANES]

    def emit(f):
        good = [valid(frames + f + n) for n in range(2)]
        for p in range(pairs):
            for k in range(3):
                block = final[f // 2][k, pl.ds(p, 2 * rows, stride=pairs), :]
                lanes = pl.ds(p * wide + k * LANES, LANES)
                for n in range(2):
                    value = own[f + n, :, lanes].astype(F32) + block[n * rows : (n + 1) * rows]
                    out[f + n, :, lanes] = jnp.where(good[n], value, 0.0).astype(BF16)

    bias_two_wide = twice(bias_two)
    for h in range(4):
        norm_hidden(h)
    second_conv(0)
    for f in range(2, frames, 2):
        norm_hidden(f + 2)
        norm_hidden(f + 3)
        emit(f - 2)
        second_conv(f)
    emit(frames - 2)


def first_block_kernel(
    bands, count, own, above, below, from_own, bias, weight, gain_two, bias_two, weight_two,
    out, total, *scratch,
):
    frames = own.shape[0]
    hidden, final = scratch[: frames + 2], scratch[frames + 2 :]

    @pl.when(lax.axis_index("tm") == 0)
    def _():
        total[:, :2] = jnp.zeros((2, 2, *total.shape[2:]), F32)
        total[:, 2:] = from_own[...]
        near = (above, below)
        finish(
            bands, count, own, near, near, bias, weight, gain_two, bias_two, weight_two,
            out, total, hidden, final,
        )


def last_kernel(
    bands, count, own, above, below, far_above, far_below, from_own, from_earlier, first_out, bias,
    weight, gain_two, bias_two, weight_two, out, total, *scratch,
):
    frames = own.shape[0]
    hidden, final = scratch[: frames + 2], scratch[frames + 2 :]
    tm = lax.axis_index("tm")

    @pl.when(tm == 0)
    def _():
        out[...] = first_out[...]

    @pl.when(tm > 0)
    def _():
        total[:, :2] = from_earlier[:, :2]
        total[:, 2:frames] = from_own[:, : frames - 2] + from_earlier[:, 2:]
        total[:, frames:] = from_own[:, frames - 2 :]
        finish(
            bands, count, own, (above, below), (far_above, far_below), bias, weight, gain_two,
            bias_two, weight_two, out, total, hidden, final,
        )


def shards(latents, counts, gain_first, bias_first, weight_first, gain_second, bias_second, weight_second):
    channels = gain_first.shape[0]
    frames, rows, flat = latents.shape[1:]
    wide = 2 * channels
    pairs = flat // wide
    blocks, bands = lax.axis_size("tm"), lax.axis_size("space")
    block = latents.reshape(frames, rows, flat)

    def shift(sent, step, along):
        pairs_of = [
            (t * bands + s, (t + along) % blocks * bands + (s + step * (t + along < blocks)) % bands)
            for t in range(blocks)
            for s in range(bands)
        ]
        return lax.ppermute(sent, ("tm", "space"), pairs_of)

    vmem = pl.BlockSpec(memory_space=pltpu.VMEM)
    smem = pl.BlockSpec(memory_space=pltpu.SMEM)
    params = pltpu.CompilerParams(vmem_limit_bytes=24 << 20)
    swap = bands == 2
    rims = 1 if swap else 2
    rim = jax.ShapeDtypeStruct((frames, 2, pairs, wide), BF16)
    mask = pl.pallas_call(
        functools.partial(mask_kernel, channels),
        out_shape=jax.ShapeDtypeStruct((2 * rows, wide), F32),
        out_specs=vmem,
        compiler_params=params,
        cost_estimate=pl.CostEstimate(flops=4 << 30, bytes_accessed=1 << 16, transcendentals=0),
        name="lane_mask",
    )()
    normed, *sent = pl.pallas_call(
        functools.partial(norm_kernel, swap),
        out_shape=[jax.ShapeDtypeStruct((frames, rows, pairs, wide), BF16)] + [rim] * rims,
        in_specs=[vmem] * 3,
        out_specs=[vmem] * (1 + rims),
        scratch_shapes=[pltpu.VMEM((3, frames * rows * pairs, LANES), F32)],
        compiler_params=params,
        cost_estimate=pl.CostEstimate(flops=4 << 30, bytes_accessed=1 << 20, transcendentals=0),
        name="norm_and_cut",
    )(mask, block, gain_first.reshape(1, channels))
    earlier = shift(block, 0, 1)
    if swap:
        near = (shift(sent[0], 1, 0),) * 2
        deep = rows + 1
    else:
        near = (shift(sent[0], 1, 0), shift(sent[1], -1, 0))
        deep = rows + 2

    first_weight = weight_first.reshape(3, 3, 3 * channels, channels)
    second_weight = weight_second.reshape(3, 3, 3 * channels, channels)
    share = (2, frames, deep, pairs, channels)
    window = pltpu.VMEM((frames + 1, deep + 2, pairs, wide), BF16)
    stage = pltpu.VMEM((3, frames * rows * pairs, LANES), F32)
    cost = pl.CostEstimate(flops=1 << 20, bytes_accessed=1 << 16, transcendentals=0)
    from_own, *later = pl.pallas_call(
        functools.partial(own_kernel, bands, deep),
        out_shape=[jax.ShapeDtypeStruct(share, F32)] + [rim] * rims,
        in_specs=[smem] + [vmem] * (2 + rims),
        out_specs=[vmem] * (1 + rims),
        scratch_shapes=[window],
        compiler_params=params,
        cost_estimate=cost,
        name="conv_one_own",
    )(counts, normed, first_weight, *sent)
    if swap:
        far = (shift(later[0], 1, 1),) * 2
    else:
        far = (shift(later[0], 1, 1), shift(later[1], -1, 1))
    constants = (
        bias_first.reshape(1, channels), first_weight,
        gain_second.reshape(1, channels), bias_second.reshape(1, channels), second_weight,
    )
    result = jax.ShapeDtypeStruct((frames, rows, flat), BF16)
    scratch = [
        pltpu.VMEM((2, frames + 2, deep, pairs, channels), F32),
        *[pltpu.VMEM((rows + 2, pairs, wide), BF16)] * (frames + 2),
        *[pltpu.VMEM((3, 2 * rows * pairs, LANES), F32)] * (frames // 2),
    ]
    first_out = pl.pallas_call(
        functools.partial(first_block_kernel, bands),
        out_shape=result,
        in_specs=[smem] + [vmem] * 9,
        out_specs=vmem,
        scratch_shapes=scratch,
        compiler_params=params,
        cost_estimate=cost,
        name="first_block",
    )(counts, block, *near, from_own, *constants)
    from_earlier = pl.pallas_call(
        functools.partial(earlier_kernel, bands, deep),
        out_shape=jax.ShapeDtypeStruct(share, F32),
        in_specs=[smem] + [vmem] * 5,
        out_specs=vmem,
        scratch_shapes=[window, stage],
        compiler_params=params,
        cost_estimate=cost,
        name="conv_one_earlier",
    )(counts, mask, earlier, gain_first.reshape(1, channels), first_weight, first_out)
    out = pl.pallas_call(
        functools.partial(last_kernel, bands),
        out_shape=result,
        in_specs=[smem] + [vmem] * 13,
        out_specs=vmem,
        scratch_shapes=scratch,
        compiler_params=params,
        cost_estimate=pl.CostEstimate(flops=4 << 30, bytes_accessed=6 << 20, transcendentals=0),
        name="last",
    )(counts, block, *near, *far, from_own, from_earlier, first_out, *constants)
    return out.reshape(1, frames, rows, flat)


def solution(mesh):
    spread = P(("groups", "clip"), "tm", "space", None)
    return jax.shard_map(
        shards,
        mesh=mesh,
        in_specs=(spread, P(("groups", "clip")), P(), P(), P(), P(), P(), P()),
        out_specs=spread,
        check_vma=False,
    )
```

```python
import functools

import jax
import jax.numpy as jnp
from jax import lax
from jax.experimental import pallas as pl
from jax.experimental.pallas import tpu as pltpu
from jax.sharding import PartitionSpec as P

F32 = jnp.float32
BF16 = jnp.bfloat16
LANES = 128


def sums_kernel(channels, sums):
    lane = lax.broadcasted_iota(jnp.int32, sums.shape, 0) < channels
    half = lax.broadcasted_iota(jnp.int32, sums.shape, 1) < LANES
    sums[...] = jnp.where(lane == half, 1.0, 0.0).astype(BF16)


def norm_silu_pair(t, half_gain, sums, channels):
    squares = jnp.dot((t * t).astype(BF16), sums, preferred_element_type=F32)
    scale = lax.rsqrt(squares * (1.0 / channels) + 1e-06)
    left, right = scale[:, :LANES], scale[:, LANES:]
    first = lax.broadcasted_iota(jnp.int32, left.shape, 1) < channels - LANES
    scale = jnp.concatenate([left, jnp.where(first, left, right), right], axis=1)
    h = t * scale * half_gain
    return h + h * jnp.tanh(h)


def twice(ref):
    return jnp.concatenate([ref[...], ref[...]], axis=1)


def norm_block(block, half_gain, sums, stage, store, pairs):
    frames, rows = block.shape[0], block.shape[1]
    wide = half_gain.shape[1]
    tall = 2 * rows
    for f in range(0, frames, 2):
        parts = []
        for p in range(pairs):
            lanes = pl.ds(p * wide, wide)
            parts += [block[f + n, :, lanes].astype(F32) for n in range(2)]
        y = norm_silu_pair(jnp.concatenate(parts, axis=0), half_gain, sums, wide // 2)
        for p in range(pairs):
            for k in range(3):
                at = pl.ds(f * rows * pairs + p, tall, stride=pairs)
                stage[k, at, :] = y[p * tall : (p + 1) * tall, k * LANES : (k + 1) * LANES]
        for n in range(2):
            for r in range(rows):
                at = pl.ds(((f + n) * rows + r) * pairs, pairs)
                store(f + n, r, [stage[k, at, :].astype(BF16) for k in range(3)])


def norm_kernel(swap, sums, block, gain, normed, *rest):
    sent, stage = rest[:-1], rest[-1]
    rows, pairs = normed.shape[1], normed.shape[2]

    def store(f, r, parts):
        for k in range(3):
            normed[f, r, :, k * LANES : (k + 1) * LANES] = parts[k]

    norm_block(block, twice(gain) * 0.5, sums[...], stage, store, pairs)
    if swap:
        first = (rows - 2) * (1 - lax.axis_index("space"))
        sent[0][...] = normed[:, pl.ds(first, 2)]
    else:
        sent[0][...] = normed[:, rows - 2 :]
        sent[1][...] = normed[:, :2]


def dot(left, right):
    return jnp.dot(
        jnp.concatenate(left, axis=1), jnp.concatenate(right, axis=0), preferred_element_type=F32
    )


def products(parts, rims, channels):
    lead = jnp.zeros((2 * LANES - channels, channels), BF16)
    mine = (
        dot(parts, [w[channels:] for w in rims]),
        dot(parts, [w[: 2 * channels] for w in rims]),
    )
    high = [x[:, LANES:] for x in parts]
    low = [x[:, : 2 * LANES] for x in parts]
    moved = (
        dot(high, [x for w in rims for x in (lead, w[:channels])]),
        dot(low, [x for w in rims for x in (w[2 * channels :], lead)]),
    )
    return mine, moved


def conv(window, weight, source, frames, rows, times, channels):
    pairs, wide = window[0].shape[1:]
    taps = [(a, b) for a in times for b in range(3)]

    def patch(a, b):
        at = source + a - times[0]
        rows_of = [window[f][b : b + rows].reshape(rows * pairs, wide) for f in range(at, at + frames)]
        return jnp.concatenate(rows_of, axis=0)

    parts = [patch(a, b) for a, b in taps]
    return add_moved(*products(parts, [weight[a, b] for a, b in taps], channels), pairs)


def add_moved(mine, moved, pairs):
    place = lax.broadcasted_iota(jnp.int32, mine[0].shape, 0) % pairs
    count = mine[0].shape[0]
    left = jnp.where(place == 0, 0.0, pltpu.roll(moved[0], 1, 0))
    right = jnp.where(place == pairs - 1, 0.0, pltpu.roll(moved[1], count - 1, 0))
    return mine[0] + left, mine[1] + right


def own_kernel(bands, deep, count, normed, weight, total, window):
    frames, rows, pairs, wide = normed.shape
    tm, space = lax.axis_index("tm"), lax.axis_index("space")
    nothing = jnp.zeros((pairs, wide), BF16)
    top = clear_rims(window, bands, space, rows, range(1, frames + 1))
    window[0] = jnp.zeros(window.shape[1:], BF16)
    for f in range(frames):
        good = tm * frames + f < count[0]
        for r in range(rows):
            window[f + 1, top + r] = jnp.where(good, normed[f, r], nothing)
    late = conv([window.at[f] for f in range(frames + 1)], weight, 1, frames - 2, deep, (0, 1, 2), wide // 2)
    soon = conv([window.at[f] for f in range(frames + 1)], weight, 0, 2, deep, (1, 2), wide // 2)
    for q in range(2):
        total[q, 0:2] = soon[q].reshape(2, *total.shape[2:])
        total[q, 2:] = late[q].reshape(frames - 2, *total.shape[2:])


def clear_rims(window, bands, space, rows, at):
    nothing = jnp.zeros(window.shape[2:], BF16)
    for f in at:
        if bands == 2:
            window[f, (rows + 2) * space] = nothing
            for r in range(2):
                window[f, (rows + 1) * (1 - space) + r] = nothing
        else:
            for r in range(2):
                window[f, r] = nothing
                window[f, rows + 2 + r] = nothing
    return 1 + space if bands == 2 else 2


def earlier_kernel(
    bands, deep, count, sums, earlier, gain, weight, after, total, window, stage
):
    frames, rows = earlier.shape[0], earlier.shape[1]
    pairs, wide = window.shape[2], window.shape[3]
    tm, space = lax.axis_index("tm"), lax.axis_index("space")

    @pl.when(tm > 0)
    def _():
        top = clear_rims(window, bands, space, rows, range(frames))
        window[frames] = jnp.zeros(window.shape[1:], BF16)

        def store(f, r, parts):
            good = (tm - 1) * frames + f < count[0]
            for k in range(3):
                part = jnp.where(good, parts[k], jnp.zeros_like(parts[k]))
                window[f, top + r, :, k * LANES : (k + 1) * LANES] = part

        norm_block(earlier, twice(gain) * 0.5, sums[...], stage, store, pairs)
        soon = conv([window.at[f] for f in range(frames + 1)], weight, 0, frames - 2, deep, (0, 1, 2), wide // 2)
        late = conv([window.at[f] for f in range(frames + 1)], weight, frames - 2, 2, deep, (0, 1), wide // 2)
        for q in range(2):
            total[q, 0 : frames - 2] = soon[q].reshape(frames - 2, *total.shape[2:])
            total[q, frames - 2 :] = late[q].reshape(2, *total.shape[2:])


def add_rims(total, near, far, weight, side, keep, channels):
    frames, pairs, wide = near.shape[0], near.shape[2], near.shape[3]
    deep = total.shape[2]
    low = (deep - 2) * side
    halo = (deep - 1) * side
    nothing = jnp.zeros((pairs, wide), BF16)

    def row(f, r):
        ref, at = (far, f) if f < frames else (near, f - frames)
        return jnp.where(keep(f), ref[at, r], nothing)

    rows = [[row(f, r) for r in range(2)] for f in range(2 * frames)]
    inner = [row(f, 1 - side) for f in range(2 * frames)]
    span = frames + 2
    parts = [
        jnp.concatenate([x for f in range(span) for x in rows[f + a]], axis=0) for a in range(3)
    ]
    added = add_moved(*products(parts, [weight[a, 2 * side] for a in range(3)], channels), pairs)
    for q in range(2):
        total[q, :, pl.ds(low, 2)] += added[q].reshape(span, 2, pairs, channels)
    parts = [jnp.concatenate([inner[f + a] for f in range(span)], axis=0) for a in range(3)]
    added = add_moved(*products(parts, [weight[a, 1] for a in range(3)], channels), pairs)
    for q in range(2):
        total[q, :, halo] += added[q].reshape(span, pairs, channels)


def finish(bands, count, sums, own, near, far, bias, weight, gain_two, bias_two, weight_two, out, total, hidden, final):
    frames, rows, pairs, wide = near[0].shape[0], own.shape[1], near[0].shape[2], near[0].shape[3]
    channels = wide // 2
    deep = total.shape[2]
    tm, space = lax.axis_index("tm"), lax.axis_index("space")
    fill = deep * pairs

    def valid(f):
        at = (tm - 1) * frames + f
        return (at >= 0) & (at < count[0])

    if bands == 2:
        add_rims(total, near[0], far[0], weight, 1 - space, valid, channels)
    else:
        above = lambda f: valid(f) & (space > 0)
        below = lambda f: valid(f) & (space < bands - 1)
        add_rims(total, near[0], far[0], weight, 0, above, channels)
        add_rims(total, near[1], far[1], weight, 1, below, channels)

    start = (1 - space) if bands == 2 else 0
    row = lax.broadcasted_iota(jnp.int32, (fill, 1), 0) // pairs + (space * rows - 1 + start)
    row_ok = (row >= 0) & (row < bands * rows)
    bias_wide, gain_wide = twice(bias), twice(gain_two) * 0.5

    def norm_hidden(h):
        good = row_ok & valid(frames + h - 2)
        t = jnp.concatenate([total[q, h].reshape(fill, channels) for q in range(2)], axis=1)
        t = jnp.where(good, t + bias_wide, 0.0).astype(BF16).astype(F32)
        y = norm_silu_pair(t, gain_wide, sums[...], channels).astype(BF16)
        hidden[h][0] = jnp.zeros((pairs, wide), BF16)
        hidden[h][rows + 1] = jnp.zeros((pairs, wide), BF16)
        for r in range(deep):
            hidden[h][start + r] = y[r * pairs : (r + 1) * pairs]

    def second_conv(f):
        both = conv(hidden, weight_two, f, 2, rows, (0, 1, 2), channels)
        both = jnp.concatenate(both, axis=1) + bias_two_wide
        for k in range(3):
            final[f // 2][k] = both[:, k * LANES : (k + 1) * LANES]

    def emit(f):
        good = [valid(frames + f + n) for n in range(2)]
        for p in range(pairs):
            for k in range(3):
                block = final[f // 2][k, pl.ds(p, 2 * rows, stride=pairs), :]
                lanes = pl.ds(p * wide + k * LANES, LANES)
                for n in range(2):
                    value = own[f + n, :, lanes].astype(F32) + block[n * rows : (n + 1) * rows]
                    out[f + n, :, lanes] = jnp.where(good[n], value, 0.0).astype(BF16)

    bias_two_wide = twice(bias_two)
    for h in range(4):
        norm_hidden(h)
    second_conv(0)
    for f in range(2, frames, 2):
        norm_hidden(f + 2)
        norm_hidden(f + 3)
        emit(f - 2)
        second_conv(f)
    emit(frames - 2)


def first_block_kernel(
    bands, count, sums, own, above, below, from_own, bias, weight, gain_two, bias_two, weight_two,
    out, total, *scratch,
):
    frames = own.shape[0]
    hidden, final = scratch[: frames + 2], scratch[frames + 2 :]

    @pl.when(lax.axis_index("tm") == 0)
    def _():
        total[:, :2] = jnp.zeros((2, 2, *total.shape[2:]), F32)
        total[:, 2:] = from_own[...]
        near = (above, below)
        finish(
            bands, count, sums, own, near, near, bias, weight, gain_two, bias_two, weight_two,
            out, total, hidden, final,
        )


def last_kernel(
    bands, count, sums, own, above, below, far_above, far_below, from_own, from_earlier, first_out, bias,
    weight, gain_two, bias_two, weight_two, out, total, *scratch,
):
    frames = own.shape[0]
    hidden, final = scratch[: frames + 2], scratch[frames + 2 :]
    tm = lax.axis_index("tm")

    @pl.when(tm == 0)
    def _():
        out[...] = first_out[...]

    @pl.when(tm > 0)
    def _():
        total[:, :2] = from_earlier[:, :2]
        total[:, 2:frames] = from_own[:, : frames - 2] + from_earlier[:, 2:]
        total[:, frames:] = from_own[:, frames - 2 :]
        finish(
            bands, count, sums, own, (above, below), (far_above, far_below), bias, weight, gain_two,
            bias_two, weight_two, out, total, hidden, final,
        )


def shards(latents, counts, gain_first, bias_first, weight_first, gain_second, bias_second, weight_second):
    channels = gain_first.shape[0]
    frames, rows, flat = latents.shape[1:]
    wide = 2 * channels
    pairs = flat // wide
    blocks, bands = lax.axis_size("tm"), lax.axis_size("space")
    block = latents.reshape(frames, rows, flat)

    def shift(sent, step, along):
        pairs_of = [
            (t * bands + s, (t + along) % blocks * bands + (s + step * (t + along < blocks)) % bands)
            for t in range(blocks)
            for s in range(bands)
        ]
        return lax.ppermute(sent, ("tm", "space"), pairs_of)

    vmem = pl.BlockSpec(memory_space=pltpu.VMEM)
    smem = pl.BlockSpec(memory_space=pltpu.SMEM)
    params = pltpu.CompilerParams(vmem_limit_bytes=24 << 20)
    swap = bands == 2
    rims = 1 if swap else 2
    rim = jax.ShapeDtypeStruct((frames, 2, pairs, wide), BF16)
    sums = pl.pallas_call(
        functools.partial(sums_kernel, channels),
        out_shape=jax.ShapeDtypeStruct((wide, 2 * LANES), BF16),
        out_specs=vmem,
        compiler_params=params,
        cost_estimate=pl.CostEstimate(flops=4 << 30, bytes_accessed=1 << 16, transcendentals=0),
        name="sum_matrix",
    )()
    normed, *sent = pl.pallas_call(
        functools.partial(norm_kernel, swap),
        out_shape=[jax.ShapeDtypeStruct((frames, rows, pairs, wide), BF16)] + [rim] * rims,
        in_specs=[vmem] * 3,
        out_specs=[vmem] * (1 + rims),
        scratch_shapes=[pltpu.VMEM((3, frames * rows * pairs, LANES), F32)],
        compiler_params=params,
        cost_estimate=pl.CostEstimate(flops=4 << 30, bytes_accessed=1 << 20, transcendentals=0),
        name="norm_and_cut",
    )(sums, block, gain_first.reshape(1, channels))
    earlier = shift(block, 0, 1)
    if swap:
        near = (shift(sent[0], 1, 0),) * 2
        far = (shift(sent[0], 1, 1),) * 2
        deep = rows + 1
    else:
        near = (shift(sent[0], 1, 0), shift(sent[1], -1, 0))
        far = (shift(sent[0], 1, 1), shift(sent[1], -1, 1))
        deep = rows + 2

    first_weight = weight_first.reshape(3, 3, 3 * channels, channels)
    second_weight = weight_second.reshape(3, 3, 3 * channels, channels)
    share = (2, frames, deep, pairs, channels)
    window = pltpu.VMEM((frames + 1, deep + 2, pairs, wide), BF16)
    stage = pltpu.VMEM((3, frames * rows * pairs, LANES), F32)
    cost = pl.CostEstimate(flops=1 << 20, bytes_accessed=1 << 16, transcendentals=0)
    from_own = pl.pallas_call(
        functools.partial(own_kernel, bands, deep),
        out_shape=jax.ShapeDtypeStruct(share, F32),
        in_specs=[smem] + [vmem] * 2,
        out_specs=vmem,
        scratch_shapes=[window],
        compiler_params=params,
        cost_estimate=cost,
        name="conv_one_own",
    )(counts, normed, first_weight)
    constants = (
        bias_first.reshape(1, channels), first_weight,
        gain_second.reshape(1, channels), bias_second.reshape(1, channels), second_weight,
    )
    result = jax.ShapeDtypeStruct((frames, rows, flat), BF16)
    scratch = [
        pltpu.VMEM((2, frames + 2, deep, pairs, channels), F32),
        *[pltpu.VMEM((rows + 2, pairs, wide), BF16)] * (frames + 2),
        *[pltpu.VMEM((3, 2 * rows * pairs, LANES), F32)] * (frames // 2),
    ]
    first_out = pl.pallas_call(
        functools.partial(first_block_kernel, bands),
        out_shape=result,
        in_specs=[smem] + [vmem] * 10,
        out_specs=vmem,
        scratch_shapes=scratch,
        compiler_params=params,
        cost_estimate=cost,
        name="first_block",
    )(counts, sums, block, *near, from_own, *constants)
    from_earlier = pl.pallas_call(
        functools.partial(earlier_kernel, bands, deep),
        out_shape=jax.ShapeDtypeStruct(share, F32),
        in_specs=[smem] + [vmem] * 5,
        out_specs=vmem,
        scratch_shapes=[window, stage],
        compiler_params=params,
        cost_estimate=cost,
        name="conv_one_earlier",
    )(counts, sums, earlier, gain_first.reshape(1, channels), first_weight, first_out)
    out = pl.pallas_call(
        functools.partial(last_kernel, bands),
        out_shape=result,
        in_specs=[smem] + [vmem] * 14,
        out_specs=vmem,
        scratch_shapes=scratch,
        compiler_params=params,
        cost_estimate=pl.CostEstimate(flops=4 << 30, bytes_accessed=6 << 20, transcendentals=0),
        name="last",
    )(counts, sums, block, *near, *far, from_own, from_earlier, first_out, *constants)
    return out.reshape(1, frames, rows, flat)


def solution(mesh):
    spread = P(("groups", "clip"), "tm", "space", None)
    return jax.shard_map(
        shards,
        mesh=mesh,
        in_specs=(spread, P(("groups", "clip")), P(), P(), P(), P(), P(), P()),
        out_specs=spread,
        check_vma=False,
    )
```

```python
import functools

import jax
import jax.numpy as jnp
from jax import lax
from jax.experimental import pallas as pl
from jax.experimental.pallas import tpu as pltpu
from jax.sharding import PartitionSpec as P

F32 = jnp.float32
BF16 = jnp.bfloat16
LANES = 128


def mask_kernel(channels, mask):
    lane = lax.broadcasted_iota(jnp.int32, mask.shape, 1)
    mask[...] = jnp.where(lane < channels, 1.0, 0.0)


def norm_silu_pair(t, gain, first, channels):
    square = t * t
    left = jnp.sum(jnp.where(first, square, 0.0), axis=1, keepdims=True)
    right = jnp.sum(jnp.where(first, 0.0, square), axis=1, keepdims=True)
    left = lax.rsqrt(left * (1.0 / channels) + 1e-06)
    right = lax.rsqrt(right * (1.0 / channels) + 1e-06)
    y = t * jnp.where(first, left, right) * gain
    return y * (0.5 + 0.5 * jnp.tanh(0.5 * y))


def twice(ref):
    return jnp.concatenate([ref[...], ref[...]], axis=1)


def norm_block(block, gain_wide, first, stage, store, pairs):
    frames, rows = block.shape[0], block.shape[1]
    wide = gain_wide.shape[1]
    for f in range(0, frames, 2):
        for p in range(pairs):
            lanes = pl.ds(p * wide, wide)
            t = jnp.concatenate([block[f + n, :, lanes].astype(F32) for n in range(2)], axis=0)
            y = norm_silu_pair(t, gain_wide, first, wide // 2)
            for k in range(3):
                at = pl.ds(f * rows * pairs + p, 2 * rows, stride=pairs)
                stage[k, at, :] = y[:, k * LANES : (k + 1) * LANES]
        for n in range(2):
            for r in range(rows):
                at = pl.ds(((f + n) * rows + r) * pairs, pairs)
                store(f + n, r, [stage[k, at, :].astype(BF16) for k in range(3)])


def norm_kernel(swap, mask, block, gain, normed, *rest):
    sent, stage = rest[:-1], rest[-1]
    rows, pairs = normed.shape[1], normed.shape[2]

    def store(f, r, parts):
        for k in range(3):
            normed[f, r, :, k * LANES : (k + 1) * LANES] = parts[k]

    norm_block(block, twice(gain), mask[...] > 0.5, stage, store, pairs)
    if swap:
        first = (rows - 2) * (1 - lax.axis_index("space"))
        sent[0][...] = normed[:, pl.ds(first, 2)]
    else:
        sent[0][...] = normed[:, rows - 2 :]
        sent[1][...] = normed[:, :2]


def dot(left, right):
    return jnp.dot(
        jnp.concatenate(left, axis=1), jnp.concatenate(right, axis=0), preferred_element_type=F32
    )


def products(parts, rims, channels):
    lead = jnp.zeros((2 * LANES - channels, channels), BF16)
    mine = (
        dot(parts, [w[channels:] for w in rims]),
        dot(parts, [w[: 2 * channels] for w in rims]),
    )
    high = [x[:, LANES:] for x in parts]
    low = [x[:, : 2 * LANES] for x in parts]
    moved = (
        dot(high, [x for w in rims for x in (lead, w[:channels])]),
        dot(low, [x for w in rims for x in (w[2 * channels :], lead)]),
    )
    return mine, moved


def conv(window, weight, source, frames, rows, times, channels):
    pairs, wide = window.shape[2], window.shape[3]
    taps = [(a, b) for a in times for b in range(3)]
    parts = [
        window[pl.ds(source + a - times[0], frames), b : b + rows].reshape(
            frames * rows * pairs, wide
        )
        for a, b in taps
    ]
    return add_moved(*products(parts, [weight[a, b] for a, b in taps], channels), pairs)


def add_moved(mine, moved, pairs):
    place = lax.broadcasted_iota(jnp.int32, mine[0].shape, 0) % pairs
    count = mine[0].shape[0]
    left = jnp.where(place == 0, 0.0, pltpu.roll(moved[0], 1, 0))
    right = jnp.where(place == pairs - 1, 0.0, pltpu.roll(moved[1], count - 1, 0))
    return mine[0] + left, mine[1] + right


def own_kernel(bands, deep, count, normed, weight, total, window):
    frames, rows, pairs, wide = normed.shape
    tm, space = lax.axis_index("tm"), lax.axis_index("space")
    nothing = jnp.zeros((pairs, wide), BF16)
    top = clear_rims(window, bands, space, rows, range(1, frames + 1))
    window[0] = jnp.zeros(window.shape[1:], BF16)
    for f in range(frames):
        good = tm * frames + f < count[0]
        for r in range(rows):
            window[f + 1, top + r] = jnp.where(good, normed[f, r], nothing)
    late = conv(window, weight, 1, frames - 2, deep, (0, 1, 2), wide // 2)
    soon = conv(window, weight, 0, 2, deep, (1, 2), wide // 2)
    for q in range(2):
        total[q, 0:2] = soon[q].reshape(2, *total.shape[2:])
        total[q, 2:] = late[q].reshape(frames - 2, *total.shape[2:])


def clear_rims(window, bands, space, rows, at):
    nothing = jnp.zeros(window.shape[2:], BF16)
    for f in at:
        if bands == 2:
            window[f, (rows + 2) * space] = nothing
            for r in range(2):
                window[f, (rows + 1) * (1 - space) + r] = nothing
        else:
            for r in range(2):
                window[f, r] = nothing
                window[f, rows + 2 + r] = nothing
    return 1 + space if bands == 2 else 2


def earlier_kernel(
    bands, deep, count, mask, earlier, gain, weight, after, total, window, stage
):
    frames, rows = earlier.shape[0], earlier.shape[1]
    pairs, wide = window.shape[2], window.shape[3]
    tm, space = lax.axis_index("tm"), lax.axis_index("space")

    @pl.when(tm > 0)
    def _():
        top = clear_rims(window, bands, space, rows, range(frames))
        window[frames] = jnp.zeros(window.shape[1:], BF16)

        def store(f, r, parts):
            good = (tm - 1) * frames + f < count[0]
            for k in range(3):
                part = jnp.where(good, parts[k], jnp.zeros_like(parts[k]))
                window[f, top + r, :, k * LANES : (k + 1) * LANES] = part

        norm_block(earlier, twice(gain), mask[...] > 0.5, stage, store, pairs)
        soon = conv(window, weight, 0, frames - 2, deep, (0, 1, 2), wide // 2)
        late = conv(window, weight, frames - 2, 2, deep, (0, 1), wide // 2)
        for q in range(2):
            total[q, 0 : frames - 2] = soon[q].reshape(frames - 2, *total.shape[2:])
            total[q, frames - 2 :] = late[q].reshape(2, *total.shape[2:])


def add_rims(total, near, far, weight, side, keep, channels):
    frames, pairs, wide = near.shape[0], near.shape[2], near.shape[3]
    deep = total.shape[2]
    low = (deep - 2) * side
    halo = (deep - 1) * side
    nothing = jnp.zeros((pairs, wide), BF16)

    def row(f, r):
        ref, at = (far, f) if f < frames else (near, f - frames)
        return jnp.where(keep(f), ref[at, r], nothing)

    rows = [[row(f, r) for r in range(2)] for f in range(2 * frames)]
    inner = [row(f, 1 - side) for f in range(2 * frames)]
    span = frames + 2
    parts = [
        jnp.concatenate([x for f in range(span) for x in rows[f + a]], axis=0) for a in range(3)
    ]
    added = add_moved(*products(parts, [weight[a, 2 * side] for a in range(3)], channels), pairs)
    for q in range(2):
        total[q, :, pl.ds(low, 2)] += added[q].reshape(span, 2, pairs, channels)
    parts = [jnp.concatenate([inner[f + a] for f in range(span)], axis=0) for a in range(3)]
    added = add_moved(*products(parts, [weight[a, 1] for a in range(3)], channels), pairs)
    for q in range(2):
        total[q, :, halo] += added[q].reshape(span, pairs, channels)


def finish(bands, count, own, near, far, bias, weight, gain_two, bias_two, weight_two, out, total, hidden, final):
    frames, rows, pairs, wide = near[0].shape[0], own.shape[1], near[0].shape[2], near[0].shape[3]
    channels = wide // 2
    deep = total.shape[2]
    tm, space = lax.axis_index("tm"), lax.axis_index("space")
    fill = deep * pairs

    def valid(f):
        at = (tm - 1) * frames + f
        return (at >= 0) & (at < count[0])

    if bands == 2:
        add_rims(total, near[0], far[0], weight, 1 - space, valid, channels)
    else:
        above = lambda f: valid(f) & (space > 0)
        below = lambda f: valid(f) & (space < bands - 1)
        add_rims(total, near[0], far[0], weight, 0, above, channels)
        add_rims(total, near[1], far[1], weight, 1, below, channels)

    start = (1 - space) if bands == 2 else 0
    row = lax.broadcasted_iota(jnp.int32, (fill, 1), 0) // pairs + (space * rows - 1 + start)
    row_ok = (row >= 0) & (row < bands * rows)
    bias_wide, gain_wide = twice(bias), twice(gain_two)
    first_lanes = lax.broadcasted_iota(jnp.int32, (fill, wide), 1) < channels

    bias_two_wide = twice(bias_two)

    def norm_hidden(h, _):
        good = row_ok & valid(frames + h - 2)
        t = jnp.concatenate([total[q, h].reshape(fill, channels) for q in range(2)], axis=1)
        t = jnp.where(good, t + bias_wide, 0.0).astype(BF16).astype(F32)
        y = norm_silu_pair(t, gain_wide, first_lanes, channels).astype(BF16)
        hidden[h, 0] = jnp.zeros((pairs, wide), BF16)
        hidden[h, rows + 1] = jnp.zeros((pairs, wide), BF16)
        for r in range(deep):
            hidden[h, start + r] = y[r * pairs : (r + 1) * pairs]
        return 0

    def second_conv(i, _):
        both = conv(hidden, weight_two, 2 * i, 2, rows, (0, 1, 2), channels)
        both = jnp.concatenate(both, axis=1) + bias_two_wide
        for k in range(3):
            final[i, k] = both[:, k * LANES : (k + 1) * LANES]
        return 0

    def emit(i, _):
        good = [valid(frames + 2 * i + n) for n in range(2)]
        for p in range(pairs):
            for k in range(3):
                block = final[i, k, pl.ds(p, 2 * rows, stride=pairs), :]
                lanes = pl.ds(p * wide + k * LANES, LANES)
                for n in range(2):
                    f = 2 * i + n
                    value = own[f, :, lanes].astype(F32) + block[n * rows : (n + 1) * rows]
                    out[f, :, lanes] = jnp.where(good[n], value, 0.0).astype(BF16)
        return 0

    lax.fori_loop(0, frames + 2, norm_hidden, 0)
    lax.fori_loop(0, frames // 2, second_conv, 0)
    lax.fori_loop(0, frames // 2, emit, 0)


def first_block_kernel(
    bands, count, own, above, below, from_own, bias, weight, gain_two, bias_two, weight_two,
    out, total, hidden, final,
):
    frames = own.shape[0]

    @pl.when(lax.axis_index("tm") == 0)
    def _():
        total[:, :2] = jnp.zeros((2, 2, *total.shape[2:]), F32)
        total[:, 2:] = from_own[...]
        near = (above, below)
        finish(
            bands, count, own, near, near, bias, weight, gain_two, bias_two, weight_two,
            out, total, hidden, final,
        )


def last_kernel(
    bands, count, own, above, below, far_above, far_below, from_own, from_earlier, first_out, bias,
    weight, gain_two, bias_two, weight_two, out, total, hidden, final,
):
    frames = own.shape[0]
    tm = lax.axis_index("tm")

    @pl.when(tm == 0)
    def _():
        out[...] = first_out[...]

    @pl.when(tm > 0)
    def _():
        total[:, :2] = from_earlier[:, :2]
        total[:, 2:frames] = from_own[:, : frames - 2] + from_earlier[:, 2:]
        total[:, frames:] = from_own[:, frames - 2 :]
        finish(
            bands, count, own, (above, below), (far_above, far_below), bias, weight, gain_two,
            bias_two, weight_two, out, total, hidden, final,
        )


def shards(latents, counts, gain_first, bias_first, weight_first, gain_second, bias_second, weight_second):
    channels = gain_first.shape[0]
    frames, rows, flat = latents.shape[1:]
    wide = 2 * channels
    pairs = flat // wide
    blocks, bands = lax.axis_size("tm"), lax.axis_size("space")
    block = latents.reshape(frames, rows, flat)

    def shift(sent, step, along):
        pairs_of = [
            (t * bands + s, (t + along) % blocks * bands + (s + step * (t + along < blocks)) % bands)
            for t in range(blocks)
            for s in range(bands)
        ]
        return lax.ppermute(sent, ("tm", "space"), pairs_of)

    vmem = pl.BlockSpec(memory_space=pltpu.VMEM)
    smem = pl.BlockSpec(memory_space=pltpu.SMEM)
    params = pltpu.CompilerParams(vmem_limit_bytes=24 << 20)
    swap = bands == 2
    rims = 1 if swap else 2
    rim = jax.ShapeDtypeStruct((frames, 2, pairs, wide), BF16)
    mask = pl.pallas_call(
        functools.partial(mask_kernel, channels),
        out_shape=jax.ShapeDtypeStruct((2 * rows, wide), F32),
        out_specs=vmem,
        compiler_params=params,
        cost_estimate=pl.CostEstimate(flops=4 << 30, bytes_accessed=1 << 16, transcendentals=0),
        name="lane_mask",
    )()
    normed, *sent = pl.pallas_call(
        functools.partial(norm_kernel, swap),
        out_shape=[jax.ShapeDtypeStruct((frames, rows, pairs, wide), BF16)] + [rim] * rims,
        in_specs=[vmem] * 3,
        out_specs=[vmem] * (1 + rims),
        scratch_shapes=[pltpu.VMEM((3, frames * rows * pairs, LANES), F32)],
        compiler_params=params,
        cost_estimate=pl.CostEstimate(flops=4 << 30, bytes_accessed=1 << 20, transcendentals=0),
        name="norm_and_cut",
    )(mask, block, gain_first.reshape(1, channels))
    earlier = shift(block, 0, 1)
    if swap:
        near = (shift(sent[0], 1, 0),) * 2
        far = (shift(sent[0], 1, 1),) * 2
        deep = rows + 1
    else:
        near = (shift(sent[0], 1, 0), shift(sent[1], -1, 0))
        far = (shift(sent[0], 1, 1), shift(sent[1], -1, 1))
        deep = rows + 2

    first_weight = weight_first.reshape(3, 3, 3 * channels, channels)
    second_weight = weight_second.reshape(3, 3, 3 * channels, channels)
    share = (2, frames, deep, pairs, channels)
    window = pltpu.VMEM((frames + 1, deep + 2, pairs, wide), BF16)
    stage = pltpu.VMEM((3, frames * rows * pairs, LANES), F32)
    cost = pl.CostEstimate(flops=1 << 20, bytes_accessed=1 << 16, transcendentals=0)
    from_own = pl.pallas_call(
        functools.partial(own_kernel, bands, deep),
        out_shape=jax.ShapeDtypeStruct(share, F32),
        in_specs=[smem] + [vmem] * 2,
        out_specs=vmem,
        scratch_shapes=[window],
        compiler_params=params,
        cost_estimate=cost,
        name="conv_one_own",
    )(counts, normed, first_weight)
    constants = (
        bias_first.reshape(1, channels), first_weight,
        gain_second.reshape(1, channels), bias_second.reshape(1, channels), second_weight,
    )
    result = jax.ShapeDtypeStruct((frames, rows, flat), BF16)
    scratch = [
        pltpu.VMEM((2, frames + 2, deep, pairs, channels), F32),
        pltpu.VMEM((frames + 2, rows + 2, pairs, wide), BF16),
        pltpu.VMEM((frames // 2, 3, 2 * rows * pairs, LANES), F32),
    ]
    first_out = pl.pallas_call(
        functools.partial(first_block_kernel, bands),
        out_shape=result,
        in_specs=[smem] + [vmem] * 9,
        out_specs=vmem,
        scratch_shapes=scratch,
        compiler_params=params,
        cost_estimate=cost,
        name="first_block",
    )(counts, block, *near, from_own, *constants)
    from_earlier = pl.pallas_call(
        functools.partial(earlier_kernel, bands, deep),
        out_shape=jax.ShapeDtypeStruct(share, F32),
        in_specs=[smem] + [vmem] * 5,
        out_specs=vmem,
        scratch_shapes=[window, stage],
        compiler_params=params,
        cost_estimate=cost,
        name="conv_one_earlier",
    )(counts, mask, earlier, gain_first.reshape(1, channels), first_weight, first_out)
    out = pl.pallas_call(
        functools.partial(last_kernel, bands),
        out_shape=result,
        in_specs=[smem] + [vmem] * 13,
        out_specs=vmem,
        scratch_shapes=scratch,
        compiler_params=params,
        cost_estimate=pl.CostEstimate(flops=4 << 30, bytes_accessed=6 << 20, transcendentals=0),
        name="last",
    )(counts, block, *near, *far, from_own, from_earlier, first_out, *constants)
    return out.reshape(1, frames, rows, flat)


def solution(mesh):
    spread = P(("groups", "clip"), "tm", "space", None)
    return jax.shard_map(
        shards,
        mesh=mesh,
        in_specs=(spread, P(("groups", "clip")), P(), P(), P(), P(), P(), P()),
        out_specs=spread,
        check_vma=False,
    )
```

```python
import functools

import jax
import jax.numpy as jnp
from jax import lax
from jax.experimental import pallas as pl
from jax.experimental.pallas import tpu as pltpu
from jax.sharding import PartitionSpec as P

F32 = jnp.float32
BF16 = jnp.bfloat16
LANES = 128


def mask_kernel(channels, mask):
    lane = lax.broadcasted_iota(jnp.int32, mask.shape, 1)
    mask[...] = jnp.where(lane < channels, 1.0, 0.0)


def norm_silu_pair(t, gain, first, channels):
    square = t * t
    left = jnp.sum(jnp.where(first, square, 0.0), axis=1, keepdims=True)
    right = jnp.sum(jnp.where(first, 0.0, square), axis=1, keepdims=True)
    left = lax.rsqrt(left * (1.0 / channels) + 1e-06)
    right = lax.rsqrt(right * (1.0 / channels) + 1e-06)
    y = t * jnp.where(first, left, right) * gain
    return y * (0.5 + 0.5 * jnp.tanh(0.5 * y))


def twice(ref):
    return jnp.concatenate([ref[...], ref[...]], axis=1)


def norm_frames(block, f, gain_wide, first, stage, store, pairs):
    rows = block.shape[1]
    wide = gain_wide.shape[1]
    for p in range(pairs):
        lanes = pl.ds(p * wide, wide)
        t = jnp.concatenate([block[f + n, :, lanes].astype(F32) for n in range(2)], axis=0)
        y = norm_silu_pair(t, gain_wide, first, wide // 2)
        for k in range(3):
            stage[k, pl.ds(p, 2 * rows, stride=pairs), :] = y[:, k * LANES : (k + 1) * LANES]
    for n in range(2):
        for r in range(rows):
            at = pl.ds((n * rows + r) * pairs, pairs)
            store(f + n, r, [stage[k, at, :].astype(BF16) for k in range(3)])


def norm_kernel(swap, mask, block, gain, normed, *rest):
    frames, rows, pairs, _ = normed.shape
    sent, stages = rest[: -(frames // 2)], rest[-(frames // 2) :]

    def store(f, r, parts):
        for k in range(3):
            normed[f, r, :, k * LANES : (k + 1) * LANES] = parts[k]

    for f in range(0, frames, 2):
        norm_frames(block, f, twice(gain), mask[...] > 0.5, stages[f // 2], store, pairs)
    if swap:
        first = (rows - 2) * (1 - lax.axis_index("space"))
        sent[0][...] = normed[:, pl.ds(first, 2)]
    else:
        sent[0][...] = normed[:, rows - 2 :]
        sent[1][...] = normed[:, :2]


def dot(left, right):
    return jnp.dot(
        jnp.concatenate(left, axis=1), jnp.concatenate(right, axis=0), preferred_element_type=F32
    )


def products(parts, rims, channels):
    lead = jnp.zeros((2 * LANES - channels, channels), BF16)
    mine = (
        dot(parts, [w[channels:] for w in rims]),
        dot(parts, [w[: 2 * channels] for w in rims]),
    )
    high = [x[:, LANES:] for x in parts]
    low = [x[:, : 2 * LANES] for x in parts]
    moved = (
        dot(high, [x for w in rims for x in (lead, w[:channels])]),
        dot(low, [x for w in rims for x in (w[2 * channels :], lead)]),
    )
    return mine, moved


def conv(window, weight, source, frames, rows, times, channels):
    pairs, wide = window[0].shape[1:]
    taps = [(a, b) for a in times for b in range(3)]

    def patch(a, b):
        at = source + a - times[0]
        rows_of = [window[f][b : b + rows].reshape(rows * pairs, wide) for f in range(at, at + frames)]
        return jnp.concatenate(rows_of, axis=0)

    parts = [patch(a, b) for a, b in taps]
    return add_moved(*products(parts, [weight[a, b] for a, b in taps], channels), pairs)


def add_moved(mine, moved, pairs):
    place = lax.broadcasted_iota(jnp.int32, mine[0].shape, 0) % pairs
    count = mine[0].shape[0]
    left = jnp.where(place == 0, 0.0, pltpu.roll(moved[0], 1, 0))
    right = jnp.where(place == pairs - 1, 0.0, pltpu.roll(moved[1], count - 1, 0))
    return mine[0] + left, mine[1] + right


def own_kernel(bands, deep, count, normed, weight, total, *window):
    frames, rows, pairs, wide = normed.shape
    tm, space = lax.axis_index("tm"), lax.axis_index("space")
    nothing = jnp.zeros((pairs, wide), BF16)
    top = clear_rims(window[1:], bands, space, rows)
    window[0][...] = jnp.zeros(window[0].shape, BF16)
    for f in range(frames):
        good = tm * frames + f < count[0]
        for r in range(rows):
            window[f + 1][top + r] = jnp.where(good, normed[f, r], nothing)
    late = conv(window, weight, 1, frames - 2, deep, (0, 1, 2), wide // 2)
    soon = conv(window, weight, 0, 2, deep, (1, 2), wide // 2)
    for q in range(2):
        total[q, 0:2] = soon[q].reshape(2, *total.shape[2:])
        total[q, 2:] = late[q].reshape(frames - 2, *total.shape[2:])


def clear_rims(window, bands, space, rows):
    for part in window:
        nothing = jnp.zeros(part.shape[1:], BF16)
        if bands == 2:
            part[(rows + 2) * space] = nothing
            for r in range(2):
                part[(rows + 1) * (1 - space) + r] = nothing
        else:
            for r in range(2):
                part[r] = nothing
                part[rows + 2 + r] = nothing
    return 1 + space if bands == 2 else 2


def earlier_kernel(bands, deep, count, mask, earlier, gain, weight, after, total, *scratch):
    frames, rows = earlier.shape[0], earlier.shape[1]
    window, stages = scratch[: frames + 1], scratch[frames + 1 :]
    pairs, wide = window[0].shape[1:]
    tm, space = lax.axis_index("tm"), lax.axis_index("space")

    @pl.when(tm > 0)
    def _():
        top = clear_rims(window[:frames], bands, space, rows)
        window[frames][...] = jnp.zeros(window[frames].shape, BF16)

        def store(f, r, parts):
            good = (tm - 1) * frames + f < count[0]
            for k in range(3):
                part = jnp.where(good, parts[k], jnp.zeros_like(parts[k]))
                window[f][top + r, :, k * LANES : (k + 1) * LANES] = part

        def norm(f):
            norm_frames(earlier, f, twice(gain), mask[...] > 0.5, stages[f // 2], store, pairs)

        norm(frames - 2)
        late = conv(window, weight, frames - 2, 2, deep, (0, 1), wide // 2)
        for f in range(0, frames - 2, 2):
            norm(f)
        for q in range(2):
            total[q, frames - 2 :] = late[q].reshape(2, *total.shape[2:])
        soon = conv(window, weight, 0, frames - 2, deep, (0, 1, 2), wide // 2)
        for q in range(2):
            total[q, 0 : frames - 2] = soon[q].reshape(frames - 2, *total.shape[2:])


def add_rims(total, near, far, weight, side, keep, channels, wanted):
    frames, pairs, wide = near.shape[0], near.shape[2], near.shape[3]
    deep = total[0].shape[1]
    low = (deep - 2) * side
    halo = (deep - 1) * side
    nothing = jnp.zeros((pairs, wide), BF16)

    def row(f, r):
        ref, at = (far, f) if f < frames else (near, f - frames)
        return jnp.where(keep(f), ref[at, r], nothing)

    span = len(wanted)
    rows = {f: [row(f, r) for r in range(2)] for f in range(wanted[0], wanted[-1] + 3)}
    inner = {f: row(f, 1 - side) for f in rows}
    parts = [jnp.concatenate([x for h in wanted for x in rows[h + a]], axis=0) for a in range(3)]
    added = add_moved(*products(parts, [weight[a, 2 * side] for a in range(3)], channels), pairs)
    for q in range(2):
        both = added[q].reshape(span, 2, pairs, channels)
        for n, h in enumerate(wanted):
            total[h][q, pl.ds(low, 2)] += both[n]
    parts = [jnp.concatenate([inner[h + a] for h in wanted], axis=0) for a in range(3)]
    added = add_moved(*products(parts, [weight[a, 1] for a in range(3)], channels), pairs)
    for q in range(2):
        one = added[q].reshape(span, pairs, channels)
        for n, h in enumerate(wanted):
            total[h][q, halo] += one[n]


def finish(bands, count, own, near, far, bias, weight, gain_two, bias_two, weight_two, out, total, hidden, final, ready):
    frames, rows, pairs, wide = near[0].shape[0], own.shape[1], near[0].shape[2], near[0].shape[3]
    channels = wide // 2
    deep = total[0].shape[1]
    tm, space = lax.axis_index("tm"), lax.axis_index("space")
    fill = deep * pairs

    def valid(f):
        at = (tm - 1) * frames + f
        return (at >= 0) & (at < count[0])

    def rims(wanted):
        if bands == 2:
            add_rims(total, near[0], far[0], weight, 1 - space, valid, channels, wanted)
        else:
            above = lambda f: valid(f) & (space > 0)
            below = lambda f: valid(f) & (space < bands - 1)
            add_rims(total, near[0], far[0], weight, 0, above, channels, wanted)
            add_rims(total, near[1], far[1], weight, 1, below, channels, wanted)

    start = (1 - space) if bands == 2 else 0
    row = lax.broadcasted_iota(jnp.int32, (fill, 1), 0) // pairs + (space * rows - 1 + start)
    row_ok = (row >= 0) & (row < bands * rows)
    bias_wide, gain_wide = twice(bias), twice(gain_two)
    first_lanes = lax.broadcasted_iota(jnp.int32, (fill, wide), 1) < channels

    def norm_hidden(h):
        good = row_ok & valid(frames + h - 2)
        t = jnp.concatenate([total[h][q].reshape(fill, channels) for q in range(2)], axis=1)
        t = jnp.where(good, t + bias_wide, 0.0).astype(BF16).astype(F32)
        y = norm_silu_pair(t, gain_wide, first_lanes, channels).astype(BF16)
        hidden[h][0] = jnp.zeros((pairs, wide), BF16)
        hidden[h][rows + 1] = jnp.zeros((pairs, wide), BF16)
        for r in range(deep):
            hidden[h][start + r] = y[r * pairs : (r + 1) * pairs]

    def second_conv(f):
        both = conv(hidden, weight_two, f, 2, rows, (0, 1, 2), channels)
        both = jnp.concatenate(both, axis=1) + bias_two_wide
        for k in range(3):
            final[f // 2][k] = both[:, k * LANES : (k + 1) * LANES]

    def emit(f):
        good = [valid(frames + f + n) for n in range(2)]
        for p in range(pairs):
            for k in range(3):
                block = final[f // 2][k, pl.ds(p, 2 * rows, stride=pairs), :]
                lanes = pl.ds(p * wide + k * LANES, LANES)
                for n in range(2):
                    value = own[f + n, :, lanes].astype(F32) + block[n * rows : (n + 1) * rows]
                    out[f + n, :, lanes] = jnp.where(good[n], value, 0.0).astype(BF16)

    bias_two_wide = twice(bias_two)
    rims(range(4))
    for f in range(2, frames, 2):
        rims(range(f + 2, f + 4))
    for h in range(4):
        norm_hidden(h)
    second_conv(0)
    for f in range(2, frames, 2):
        norm_hidden(f + 2)
        norm_hidden(f + 3)
        emit(f - 2)
        ready(f - 2)
        second_conv(f)
    emit(frames - 2)
    ready(frames - 2)


def first_block_kernel(
    bands, count, own, above, below, from_own, bias, weight, gain_two, bias_two, weight_two,
    out, *scratch,
):
    total, hidden, final = split(scratch, own.shape[0])

    @pl.when(lax.axis_index("tm") == 0)
    def _():
        for h, part in enumerate(total):
            part[...] = jnp.zeros(part.shape, F32) if h < 2 else from_own[:, h - 2]
        near = (above, below)
        finish(
            bands, count, own, near, near, bias, weight, gain_two, bias_two, weight_two,
            out, total, hidden, final, lambda f: None,
        )


def split(scratch, frames):
    return scratch[: frames + 2], scratch[frames + 2 : 2 * frames + 4], scratch[2 * frames + 4 :]


def last_kernel(
    bands, count, own, above, below, far_above, far_below, from_own, from_earlier, first_out, bias,
    weight, gain_two, bias_two, weight_two, out, result, sems, *scratch,
):
    frames = own.shape[0]
    total, hidden, final = split(scratch, frames)
    tm = lax.axis_index("tm")

    @pl.when(tm == 0)
    def _():
        copy = pltpu.make_async_copy(first_out, out, sems.at[0])
        copy.start()
        copy.wait()

    @pl.when(tm > 0)
    def _():
        for h, part in enumerate(total):
            if h < 2:
                part[...] = from_earlier[:, h]
            elif h < frames:
                part[...] = from_own[:, h - 2] + from_earlier[:, h]
            else:
                part[...] = from_own[:, h - 2]
        copies = [
            pltpu.make_async_copy(result.at[pl.ds(f, 2)], out.at[pl.ds(f, 2)], sems.at[f // 2])
            for f in range(0, frames, 2)
        ]
        finish(
            bands, count, own, (above, below), (far_above, far_below), bias, weight, gain_two,
            bias_two, weight_two, result, total, hidden, final, lambda f: copies[f // 2].start(),
        )
        for copy in copies:
            copy.wait()


def shards(latents, counts, gain_first, bias_first, weight_first, gain_second, bias_second, weight_second):
    channels = gain_first.shape[0]
    frames, rows, flat = latents.shape[1:]
    wide = 2 * channels
    pairs = flat // wide
    blocks, bands = lax.axis_size("tm"), lax.axis_size("space")
    block = latents.reshape(frames, rows, flat)

    def shift(sent, step, along):
        pairs_of = [
            (t * bands + s, (t + along) % blocks * bands + (s + step * (t + along < blocks)) % bands)
            for t in range(blocks)
            for s in range(bands)
        ]
        return lax.ppermute(sent, ("tm", "space"), pairs_of)

    vmem = pl.BlockSpec(memory_space=pltpu.VMEM)
    smem = pl.BlockSpec(memory_space=pltpu.SMEM)
    params = pltpu.CompilerParams(vmem_limit_bytes=24 << 20)
    swap = bands == 2
    rims = 1 if swap else 2
    rim = jax.ShapeDtypeStruct((frames, 2, pairs, wide), BF16)
    stages = [pltpu.VMEM((3, 2 * rows * pairs, LANES), F32)] * (frames // 2)
    mask = pl.pallas_call(
        functools.partial(mask_kernel, channels),
        out_shape=jax.ShapeDtypeStruct((2 * rows, wide), F32),
        out_specs=vmem,
        compiler_params=params,
        cost_estimate=pl.CostEstimate(flops=4 << 30, bytes_accessed=1 << 16, transcendentals=0),
        name="lane_mask",
    )()
    normed, *sent = pl.pallas_call(
        functools.partial(norm_kernel, swap),
        out_shape=[jax.ShapeDtypeStruct((frames, rows, pairs, wide), BF16)] + [rim] * rims,
        in_specs=[vmem] * 3,
        out_specs=[vmem] * (1 + rims),
        scratch_shapes=stages,
        compiler_params=params,
        cost_estimate=pl.CostEstimate(flops=4 << 30, bytes_accessed=1 << 20, transcendentals=0),
        name="norm_and_cut",
    )(mask, block, gain_first.reshape(1, channels))
    earlier = shift(block, 0, 1)
    if swap:
        near = (shift(sent[0], 1, 0),) * 2
        far = (shift(sent[0], 1, 1),) * 2
        deep = rows + 1
    else:
        near = (shift(sent[0], 1, 0), shift(sent[1], -1, 0))
        far = (shift(sent[0], 1, 1), shift(sent[1], -1, 1))
        deep = rows + 2

    first_weight = weight_first.reshape(3, 3, 3 * channels, channels)
    second_weight = weight_second.reshape(3, 3, 3 * channels, channels)
    share = (2, frames, deep, pairs, channels)
    window = [pltpu.VMEM((deep + 2, pairs, wide), BF16)] * (frames + 1)
    cost = pl.CostEstimate(flops=1 << 20, bytes_accessed=1 << 16, transcendentals=0)
    from_own = pl.pallas_call(
        functools.partial(own_kernel, bands, deep),
        out_shape=jax.ShapeDtypeStruct(share, F32),
        in_specs=[smem] + [vmem] * 2,
        out_specs=vmem,
        scratch_shapes=window,
        compiler_params=params,
        cost_estimate=cost,
        name="conv_one_own",
    )(counts, normed, first_weight)
    constants = (
        bias_first.reshape(1, channels), first_weight,
        gain_second.reshape(1, channels), bias_second.reshape(1, channels), second_weight,
    )
    result = jax.ShapeDtypeStruct((frames, rows, flat), BF16)
    scratch = (
        [pltpu.VMEM((2, deep, pairs, channels), F32)] * (frames + 2)
        + [pltpu.VMEM((rows + 2, pairs, wide), BF16)] * (frames + 2)
        + stages
    )
    first_out = pl.pallas_call(
        functools.partial(first_block_kernel, bands),
        out_shape=result,
        in_specs=[smem] + [vmem] * 9,
        out_specs=vmem,
        scratch_shapes=scratch,
        compiler_params=params,
        cost_estimate=cost,
        name="first_block",
    )(counts, block, *near, from_own, *constants)
    from_earlier = pl.pallas_call(
        functools.partial(earlier_kernel, bands, deep),
        out_shape=jax.ShapeDtypeStruct(share, F32),
        in_specs=[smem] + [vmem] * 5,
        out_specs=vmem,
        scratch_shapes=window + stages,
        compiler_params=params,
        cost_estimate=cost,
        name="conv_one_earlier",
    )(counts, mask, earlier, gain_first.reshape(1, channels), first_weight, first_out)
    out = pl.pallas_call(
        functools.partial(last_kernel, bands),
        out_shape=result,
        in_specs=[smem] + [vmem] * 13,
        out_specs=pl.BlockSpec(memory_space=pl.ANY),
        scratch_shapes=[
            pltpu.VMEM((frames, rows, flat), BF16), pltpu.SemaphoreType.DMA((frames // 2,))
        ] + scratch,
        compiler_params=params,
        cost_estimate=pl.CostEstimate(flops=4 << 30, bytes_accessed=6 << 20, transcendentals=0),
        name="last",
    )(counts, block, *near, *far, from_own, from_earlier, first_out, *constants)
    return out.reshape(1, frames, rows, flat)


def solution(mesh):
    spread = P(("groups", "clip"), "tm", "space", None)
    return jax.shard_map(
        shards,
        mesh=mesh,
        in_specs=(spread, P(("groups", "clip")), P(), P(), P(), P(), P(), P()),
        out_specs=spread,
        check_vma=False,
    )
```

```python
import functools

import jax
import jax.numpy as jnp
from jax import lax
from jax.experimental import pallas as pl
from jax.experimental.pallas import tpu as pltpu
from jax.sharding import PartitionSpec as P

F32 = jnp.float32
BF16 = jnp.bfloat16
LANES = 128


def mask_kernel(channels, mask):
    lane = lax.broadcasted_iota(jnp.int32, mask.shape, 1)
    mask[...] = jnp.where(lane < channels, 1.0, 0.0)


def norm_silu_pair(t, gain, first, channels):
    square = t * t
    left = jnp.sum(jnp.where(first, square, 0.0), axis=1, keepdims=True)
    right = jnp.sum(jnp.where(first, 0.0, square), axis=1, keepdims=True)
    left = lax.rsqrt(left * (1.0 / channels) + 1e-06)
    right = lax.rsqrt(right * (1.0 / channels) + 1e-06)
    y = t * jnp.where(first, left, right) * gain
    return y * (0.5 + 0.5 * jnp.tanh(0.5 * y))


def twice(ref):
    return jnp.concatenate([ref[...], ref[...]], axis=1)


def norm_frames(block, f, gain_wide, first, stage, store, pairs):
    rows = block.shape[1]
    wide = gain_wide.shape[1]
    for p in range(pairs):
        lanes = pl.ds(p * wide, wide)
        t = jnp.concatenate([block[f + n, :, lanes].astype(F32) for n in range(2)], axis=0)
        y = norm_silu_pair(t, gain_wide, first, wide // 2)
        for k in range(3):
            stage[k, pl.ds(p, 2 * rows, stride=pairs), :] = y[:, k * LANES : (k + 1) * LANES]
    for n in range(2):
        for r in range(rows):
            at = pl.ds((n * rows + r) * pairs, pairs)
            store(f + n, r, [stage[k, at, :].astype(BF16) for k in range(3)])


def norm_kernel(swap, mask, block, gain, normed, *rest):
    frames, rows, pairs, _ = normed.shape
    sent, stages = rest[: -(frames // 2)], rest[-(frames // 2) :]

    def store(f, r, parts):
        for k in range(3):
            normed[f, r, :, k * LANES : (k + 1) * LANES] = parts[k]

    for f in range(0, frames, 2):
        norm_frames(block, f, twice(gain), mask[...] > 0.5, stages[f // 2], store, pairs)
    if swap:
        first = (rows - 2) * (1 - lax.axis_index("space"))
        sent[0][...] = normed[:, pl.ds(first, 2)]
    else:
        sent[0][...] = normed[:, rows - 2 :]
        sent[1][...] = normed[:, :2]


def dot(left, right):
    return jnp.dot(
        jnp.concatenate(left, axis=1), jnp.concatenate(right, axis=0), preferred_element_type=F32
    )


def products(parts, rims, channels):
    lead = jnp.zeros((2 * LANES - channels, channels), BF16)
    mine = (
        dot(parts, [w[channels:] for w in rims]),
        dot(parts, [w[: 2 * channels] for w in rims]),
    )
    high = [x[:, LANES:] for x in parts]
    low = [x[:, : 2 * LANES] for x in parts]
    moved = (
        dot(high, [x for w in rims for x in (lead, w[:channels])]),
        dot(low, [x for w in rims for x in (w[2 * channels :], lead)]),
    )
    return mine, moved


def mix(frames, mixed):
    d = [frame[...] for frame in frames]
    for ref, value in zip(mixed, (d[0] - d[2], d[1] + d[2], d[2] - d[1], d[1] - d[3])):
        ref[...] = value


def mix_weights(weight, mixed):
    for b in range(3):
        g = [weight[a, b].astype(F32) for a in range(3)]
        both = (g[0] + g[1] + g[2]) * -0.5
        mixed[0, b] = both.astype(BF16)
        mixed[1, b] = (both + g[1]).astype(BF16)


def conv_pairs(mixed, weight, weight_mixed, rows, channels):
    pairs, wide = mixed[0][0].shape[1:]
    mine, moved = [], []
    for i in range(4):
        parts = [
            jnp.concatenate([m[i][b : b + rows].reshape(rows * pairs, wide) for m in mixed], axis=0)
            for b in range(3)
        ]
        rims = [(weight[0, b], weight_mixed[0, b], weight_mixed[1, b], weight[2, b])[i] for b in range(3)]
        own, other = products(parts, rims, channels)
        mine.append(own)
        moved.append(other)

    def outputs(m):
        soon = [m[0][q] - m[1][q] - m[2][q] for q in range(2)]
        late = [m[2][q] - m[1][q] - m[3][q] for q in range(2)]
        return soon, late

    return [add_moved(x, y, pairs) for x, y in zip(outputs(mine), outputs(moved))]


def put_pairs(total, results, first):
    _, _, deep, pairs, channels = total.shape
    for n, both in enumerate(results):
        for q in range(2):
            value = both[q].reshape(-1, deep, pairs, channels)
            for m in range(value.shape[0]):
                total[q, first + 2 * m + n] = value[m]


def add_moved(mine, moved, pairs):
    place = lax.broadcasted_iota(jnp.int32, mine[0].shape, 0) % pairs
    count = mine[0].shape[0]
    left = jnp.where(place == 0, 0.0, pltpu.roll(moved[0], 1, 0))
    right = jnp.where(place == pairs - 1, 0.0, pltpu.roll(moved[1], count - 1, 0))
    return mine[0] + left, mine[1] + right


def own_window(window, normed, source, count, bands):
    frames, rows, pairs, wide = normed.shape
    tm, space = lax.axis_index("tm"), lax.axis_index("space")
    nothing = jnp.zeros((pairs, wide), BF16)
    top = clear_rims(window, bands, space, rows)
    for n, part in enumerate(window):
        good = tm * frames + source + n < count[0]
        for r in range(rows):
            part[top + r] = jnp.where(good, normed[source + n, r], nothing)


def own_kernel(
    bands, deep, count, normed, weight, weight_two, gain_two, bias, bias_two, total, mixed_one,
    mixed_two, *scratch,
):
    channels = normed.shape[3] // 2
    window, mixed = scratch[:4], scratch[4:]
    mix_weights(weight, mixed_one)
    own_window(window, normed, 0, count, bands)
    mix(window, mixed)
    put_pairs(total, conv_pairs([mixed], weight, mixed_one, deep, channels), 0)
    mix_weights(weight_two, mixed_two)


def clear_rims(window, bands, space, rows):
    for part in window:
        nothing = jnp.zeros(part.shape[1:], BF16)
        if bands == 2:
            part[(rows + 2) * space] = nothing
            for r in range(2):
                part[(rows + 1) * (1 - space) + r] = nothing
        else:
            for r in range(2):
                part[r] = nothing
                part[rows + 2 + r] = nothing
    return 1 + space if bands == 2 else 2


def earlier_kernel(
    bands, deep, count, mask, earlier, normed, gain, weight, mixed_one, after, total, *scratch
):
    frames, rows = earlier.shape[0], earlier.shape[1]
    window, scratch = scratch[: frames + 2], scratch[frames + 2 :]
    mixed, stages = (scratch[:4], scratch[4:8]), scratch[8:]
    pairs, wide = window[0].shape[1:]
    tm, space = lax.axis_index("tm"), lax.axis_index("space")

    @pl.when(tm > 0)
    def _():
        top = clear_rims(window[:frames], bands, space, rows)
        own_window(window[frames:], normed, 0, count, bands)

        def store(f, r, parts):
            good = (tm - 1) * frames + f < count[0]
            for k in range(3):
                part = jnp.where(good, parts[k], jnp.zeros_like(parts[k]))
                window[f][top + r, :, k * LANES : (k + 1) * LANES] = part

        for f in range(0, frames, 2):
            norm_frames(earlier, f, twice(gain), mask[...] > 0.5, stages[f // 2], store, pairs)
        for n in range(2):
            mix(window[2 * n : 2 * n + 4], mixed[n])
        put_pairs(total, conv_pairs(mixed, weight, mixed_one, deep, wide // 2), 0)


def add_rims(total, near, far, weight, side, keep, channels, wanted):
    frames, pairs, wide = near.shape[0], near.shape[2], near.shape[3]
    deep = total[0].shape[1]
    low = (deep - 2) * side
    halo = (deep - 1) * side
    nothing = jnp.zeros((pairs, wide), BF16)

    def row(f, r):
        ref, at = (far, f) if f < frames else (near, f - frames)
        return jnp.where(keep(f), ref[at, r], nothing)

    span = len(wanted)
    rows = {f: [row(f, r) for r in range(2)] for f in range(wanted[0], wanted[-1] + 3)}
    inner = {f: row(f, 1 - side) for f in rows}
    parts = [jnp.concatenate([x for h in wanted for x in rows[h + a]], axis=0) for a in range(3)]
    added = add_moved(*products(parts, [weight[a, 2 * side] for a in range(3)], channels), pairs)
    for q in range(2):
        both = added[q].reshape(span, 2, pairs, channels)
        for n, h in enumerate(wanted):
            total[h][q, pl.ds(low, 2)] += both[n]
    parts = [jnp.concatenate([inner[h + a] for h in wanted], axis=0) for a in range(3)]
    added = add_moved(*products(parts, [weight[a, 1] for a in range(3)], channels), pairs)
    for q in range(2):
        one = added[q].reshape(span, pairs, channels)
        for n, h in enumerate(wanted):
            total[h][q, halo] += one[n]


def finish(bands, count, own, near, far, bias, weight, gain_two, bias_two, weight_two, mixed_two, out, total, hidden, mixed, final, ready):
    frames, rows, pairs, wide = near[0].shape[0], own.shape[1], near[0].shape[2], near[0].shape[3]
    channels = wide // 2
    deep = total[0].shape[1]
    tm, space = lax.axis_index("tm"), lax.axis_index("space")
    fill = deep * pairs

    def valid(f):
        at = (tm - 1) * frames + f
        return (at >= 0) & (at < count[0])

    def rims(wanted):
        if bands == 2:
            add_rims(total, near[0], far[0], weight, 1 - space, valid, channels, wanted)
        else:
            above = lambda f: valid(f) & (space > 0)
            below = lambda f: valid(f) & (space < bands - 1)
            add_rims(total, near[0], far[0], weight, 0, above, channels, wanted)
            add_rims(total, near[1], far[1], weight, 1, below, channels, wanted)

    start = (1 - space) if bands == 2 else 0
    row = lax.broadcasted_iota(jnp.int32, (fill, 1), 0) // pairs + (space * rows - 1 + start)
    row_ok = (row >= 0) & (row < bands * rows)
    bias_wide, gain_wide = twice(bias), twice(gain_two)
    first_lanes = lax.broadcasted_iota(jnp.int32, (fill, wide), 1) < channels

    def norm_hidden(h):
        good = row_ok & valid(frames + h - 2)
        t = jnp.concatenate([total[h][q].reshape(fill, channels) for q in range(2)], axis=1)
        t = jnp.where(good, t + bias_wide, 0.0).astype(BF16).astype(F32)
        y = norm_silu_pair(t, gain_wide, first_lanes, channels).astype(BF16)
        hidden[h][0] = jnp.zeros((pairs, wide), BF16)
        hidden[h][rows + 1] = jnp.zeros((pairs, wide), BF16)
        for r in range(deep):
            hidden[h][start + r] = y[r * pairs : (r + 1) * pairs]

    def second_conv():
        for n, parts in enumerate(mixed):
            mix(hidden[2 * n : 2 * n + 4], parts)
        results = conv_pairs(mixed, weight_two, mixed_two, rows, channels)
        for n, both in enumerate(results):
            both = jnp.concatenate(both, axis=1) + bias_two_wide
            for m in range(frames // 2):
                at = pl.ds(n * rows * pairs, rows * pairs)
                part = both[m * rows * pairs : (m + 1) * rows * pairs]
                for k in range(3):
                    final[m][k, at, :] = part[:, k * LANES : (k + 1) * LANES]

    def emit(f):
        good = [valid(frames + f + n) for n in range(2)]
        for p in range(pairs):
            for k in range(3):
                block = final[f // 2][k, pl.ds(p, 2 * rows, stride=pairs), :]
                lanes = pl.ds(p * wide + k * LANES, LANES)
                for n in range(2):
                    value = own[f + n, :, lanes].astype(F32) + block[n * rows : (n + 1) * rows]
                    out[f + n, :, lanes] = jnp.where(good[n], value, 0.0).astype(BF16)

    bias_two_wide = twice(bias_two)
    rims(range(4))
    for f in range(2, frames, 2):
        rims(range(f + 2, f + 4))
    for h in range(frames + 2):
        norm_hidden(h)
    second_conv()
    for f in range(0, frames, 2):
        emit(f)
        ready(f)


def split(scratch, frames):
    total, hidden, rest = scratch[: frames + 2], scratch[frames + 2 : 2 * frames + 4], scratch[2 * frames + 4 :]
    half = frames // 2
    return total, hidden, [rest[4 * n : 4 * n + 4] for n in range(half)], rest[4 * half : 5 * half]


def first_block_kernel(
    bands, count, own, normed, above, below, from_own, mixed_one, mixed_two, bias, weight,
    gain_two, bias_two, weight_two, out, *scratch,
):
    frames = own.shape[0]
    window, blend, scratch = scratch[:4], scratch[4:8], scratch[8:]
    parts = split(scratch, frames)
    total = parts[0]

    @pl.when(lax.axis_index("tm") == 0)
    def _():
        for part in window[:2]:
            part[...] = jnp.zeros(part.shape, BF16)
        own_window(window[2:], normed, 0, count, bands)
        mix(window, blend)
        deep, pairs, channels = total[0].shape[1:]
        results = conv_pairs([blend], weight, mixed_one, deep, channels)
        for h, part in enumerate(total):
            if h < 2:
                part[...] = jnp.zeros(part.shape, F32)
            elif h < 4:
                for q in range(2):
                    part[q] = results[h - 2][q].reshape(deep, pairs, channels)
            else:
                part[...] = from_own[:, h - 4]
        near = (above, below)
        finish(
            bands, count, own, near, near, bias, weight, gain_two, bias_two, weight_two, mixed_two,
            out, *parts, lambda f: None,
        )


def last_kernel(
    bands, count, own, above, below, far_above, far_below, from_own, from_earlier, first_out,
    mixed_two, bias, weight, gain_two, bias_two, weight_two, out, result, sems, *scratch,
):
    frames = own.shape[0]
    parts = split(scratch, frames)
    tm = lax.axis_index("tm")

    @pl.when(tm == 0)
    def _():
        copy = pltpu.make_async_copy(first_out, out, sems.at[0])
        copy.start()
        copy.wait()

    @pl.when(tm > 0)
    def _():
        for h, part in enumerate(parts[0]):
            part[...] = from_earlier[:, h] if h < frames else from_own[:, h - frames]
        copies = [
            pltpu.make_async_copy(result.at[pl.ds(f, 2)], out.at[pl.ds(f, 2)], sems.at[f // 2])
            for f in range(0, frames, 2)
        ]
        finish(
            bands, count, own, (above, below), (far_above, far_below), bias, weight, gain_two,
            bias_two, weight_two, mixed_two, result, *parts, lambda f: copies[f // 2].start(),
        )
        for copy in copies:
            copy.wait()


def shards(latents, counts, gain_first, bias_first, weight_first, gain_second, bias_second, weight_second):
    channels = gain_first.shape[0]
    frames, rows, flat = latents.shape[1:]
    wide = 2 * channels
    pairs = flat // wide
    blocks, bands = lax.axis_size("tm"), lax.axis_size("space")
    block = latents.reshape(frames, rows, flat)

    def shift(sent, step, along):
        pairs_of = [
            (t * bands + s, (t + along) % blocks * bands + (s + step * (t + along < blocks)) % bands)
            for t in range(blocks)
            for s in range(bands)
        ]
        return lax.ppermute(sent, ("tm", "space"), pairs_of)

    vmem = pl.BlockSpec(memory_space=pltpu.VMEM)
    smem = pl.BlockSpec(memory_space=pltpu.SMEM)
    params = pltpu.CompilerParams(vmem_limit_bytes=24 << 20)
    swap = bands == 2
    rims = 1 if swap else 2
    rim = jax.ShapeDtypeStruct((frames, 2, pairs, wide), BF16)
    stages = [pltpu.VMEM((3, 2 * rows * pairs, LANES), F32)] * (frames // 2)
    mask = pl.pallas_call(
        functools.partial(mask_kernel, channels),
        out_shape=jax.ShapeDtypeStruct((2 * rows, wide), F32),
        out_specs=vmem,
        compiler_params=params,
        cost_estimate=pl.CostEstimate(flops=4 << 30, bytes_accessed=1 << 16, transcendentals=0),
        name="lane_mask",
    )()
    normed, *sent = pl.pallas_call(
        functools.partial(norm_kernel, swap),
        out_shape=[jax.ShapeDtypeStruct((frames, rows, pairs, wide), BF16)] + [rim] * rims,
        in_specs=[vmem] * 3,
        out_specs=[vmem] * (1 + rims),
        scratch_shapes=stages,
        compiler_params=params,
        cost_estimate=pl.CostEstimate(flops=4 << 30, bytes_accessed=1 << 20, transcendentals=0),
        name="norm_and_cut",
    )(mask, block, gain_first.reshape(1, channels))
    earlier = shift(block, 0, 1)
    if swap:
        near = (shift(sent[0], 1, 0),) * 2
        far = (shift(sent[0], 1, 1),) * 2
        deep = rows + 1
    else:
        near = (shift(sent[0], 1, 0), shift(sent[1], -1, 0))
        far = (shift(sent[0], 1, 1), shift(sent[1], -1, 1))
        deep = rows + 2

    first_weight = weight_first.reshape(3, 3, 3 * channels, channels)
    second_weight = weight_second.reshape(3, 3, 3 * channels, channels)
    row_window = pltpu.VMEM((deep + 2, pairs, wide), BF16)
    taps = jax.ShapeDtypeStruct((2, *first_weight.shape[1:]), BF16)
    cost = pl.CostEstimate(flops=1 << 20, bytes_accessed=1 << 16, transcendentals=0)
    from_own, mixed_one, mixed_two = pl.pallas_call(
        functools.partial(own_kernel, bands, deep),
        out_shape=[jax.ShapeDtypeStruct((2, 2, deep, pairs, channels), F32), taps, taps],
        in_specs=[smem] + [vmem] * 6,
        out_specs=[vmem] * 3,
        scratch_shapes=[row_window] * 8,
        compiler_params=params,
        cost_estimate=cost,
        name="conv_one_own",
    )(
        counts, normed, first_weight, second_weight, gain_second.reshape(1, channels),
        bias_first.reshape(1, channels), bias_second.reshape(1, channels),
    )
    constants = (
        bias_first.reshape(1, channels), first_weight,
        gain_second.reshape(1, channels), bias_second.reshape(1, channels), second_weight,
    )
    result = jax.ShapeDtypeStruct((frames, rows, flat), BF16)
    scratch = (
        [pltpu.VMEM((2, deep, pairs, channels), F32)] * (frames + 2)
        + [pltpu.VMEM((rows + 2, pairs, wide), BF16)] * (frames + 2 + 2 * frames)
        + stages
    )
    first_out = pl.pallas_call(
        functools.partial(first_block_kernel, bands),
        out_shape=result,
        in_specs=[smem] + [vmem] * 12,
        out_specs=vmem,
        scratch_shapes=[row_window] * 8 + scratch,
        compiler_params=params,
        cost_estimate=cost,
        name="first_block",
    )(counts, block, normed, *near, from_own, mixed_one, mixed_two, *constants)
    from_earlier = pl.pallas_call(
        functools.partial(earlier_kernel, bands, deep),
        out_shape=jax.ShapeDtypeStruct((2, frames, deep, pairs, channels), F32),
        in_specs=[smem] + [vmem] * 7,
        out_specs=vmem,
        scratch_shapes=[row_window] * (frames + 2 + 8) + stages,
        compiler_params=params,
        cost_estimate=cost,
        name="conv_one_earlier",
    )(
        counts, mask, earlier, normed, gain_first.reshape(1, channels), first_weight, mixed_one,
        first_out,
    )
    out = pl.pallas_call(
        functools.partial(last_kernel, bands),
        out_shape=result,
        in_specs=[smem] + [vmem] * 14,
        out_specs=pl.BlockSpec(memory_space=pl.ANY),
        scratch_shapes=[
            pltpu.VMEM((frames, rows, flat), BF16), pltpu.SemaphoreType.DMA((frames // 2,))
        ] + scratch,
        compiler_params=params,
        cost_estimate=pl.CostEstimate(flops=4 << 30, bytes_accessed=6 << 20, transcendentals=0),
        name="last",
    )(counts, block, *near, *far, from_own, from_earlier, first_out, mixed_two, *constants)
    return out.reshape(1, frames, rows, flat)


def solution(mesh):
    spread = P(("groups", "clip"), "tm", "space", None)
    return jax.shard_map(
        shards,
        mesh=mesh,
        in_specs=(spread, P(("groups", "clip")), P(), P(), P(), P(), P(), P()),
        out_specs=spread,
        check_vma=False,
    )
```

```python
import functools

import jax
import jax.numpy as jnp
from jax import lax
from jax.experimental import pallas as pl
from jax.experimental.pallas import tpu as pltpu
from jax.sharding import PartitionSpec as P

F32 = jnp.float32
BF16 = jnp.bfloat16
LANES = 128


def mask_kernel(channels, mask):
    lane = lax.broadcasted_iota(jnp.int32, mask.shape, 1)
    mask[...] = jnp.where(lane < channels, 1.0, 0.0)


def norm_silu_pair(t, gain, first, channels):
    square = t * t
    left = jnp.sum(jnp.where(first, square, 0.0), axis=1, keepdims=True)
    right = jnp.sum(jnp.where(first, 0.0, square), axis=1, keepdims=True)
    left = lax.rsqrt(left * (1.0 / channels) + 1e-06)
    right = lax.rsqrt(right * (1.0 / channels) + 1e-06)
    y = t * jnp.where(first, left, right) * gain
    return y * (0.5 + 0.5 * jnp.tanh(0.5 * y))


def twice(ref):
    return jnp.concatenate([ref[...], ref[...]], axis=1)


def norm_frames(block, f, gain_wide, first, stage, store, pairs):
    rows = block.shape[1]
    wide = gain_wide.shape[1]
    for p in range(pairs):
        lanes = pl.ds(p * wide, wide)
        t = jnp.concatenate([block[f + n, :, lanes].astype(F32) for n in range(2)], axis=0)
        y = norm_silu_pair(t, gain_wide, first, wide // 2)
        for k in range(3):
            stage[k, pl.ds(p, 2 * rows, stride=pairs), :] = y[:, k * LANES : (k + 1) * LANES]
    for n in range(2):
        for r in range(rows):
            at = pl.ds((n * rows + r) * pairs, pairs)
            store(f + n, r, [stage[k, at, :].astype(BF16) for k in range(3)])


def norm_kernel(swap, mask, block, gain, normed, *rest):
    frames, rows, pairs, _ = normed.shape
    sent, stages = rest[: -(frames // 2)], rest[-(frames // 2) :]

    def store(f, r, parts):
        for k in range(3):
            normed[f, r, :, k * LANES : (k + 1) * LANES] = parts[k]

    for f in range(0, frames, 2):
        norm_frames(block, f, twice(gain), mask[...] > 0.5, stages[f // 2], store, pairs)
    if swap:
        first = (rows - 2) * (1 - lax.axis_index("space"))
        sent[0][...] = normed[:, pl.ds(first, 2)]
    else:
        sent[0][...] = normed[:, rows - 2 :]
        sent[1][...] = normed[:, :2]


def dot(left, right):
    return jnp.dot(
        jnp.concatenate(left, axis=1), jnp.concatenate(right, axis=0), preferred_element_type=F32
    )


def products(parts, rims, channels):
    lead = jnp.zeros((2 * LANES - channels, channels), BF16)
    mine = (
        dot(parts, [w[channels:] for w in rims]),
        dot(parts, [w[: 2 * channels] for w in rims]),
    )
    high = [x[:, LANES:] for x in parts]
    low = [x[:, : 2 * LANES] for x in parts]
    moved = (
        dot(high, [x for w in rims for x in (lead, w[:channels])]),
        dot(low, [x for w in rims for x in (w[2 * channels :], lead)]),
    )
    return mine, moved


def conv(window, weight, source, frames, rows, times, channels):
    pairs, wide = window[0].shape[1:]
    taps = [(a, b) for a in times for b in range(3)]

    def patch(a, b):
        at = source + a - times[0]
        rows_of = [window[f][b : b + rows].reshape(rows * pairs, wide) for f in range(at, at + frames)]
        return jnp.concatenate(rows_of, axis=0)

    parts = [patch(a, b) for a, b in taps]
    return add_moved(*products(parts, [weight[a, b] for a, b in taps], channels), pairs)


def mix_weights(weight, mixed):
    for b in range(3):
        outer = weight[0, b] + weight[2, b]
        mixed[0, b] = (outer + weight[1, b]) * -0.5
        mixed[1, b] = (outer - weight[1, b]) * -0.5


def mix(frames, i, out):
    if i == 1:
        out[...] = frames[1][...] + frames[2][...]
    else:
        one, other = ((0, 2), None, (2, 1), (1, 3))[i]
        out[...] = frames[one][...] - frames[other][...]


def mixed_product(mixed, taps, rows, channels):
    pairs, wide = mixed[0].shape[1:]
    parts = [
        jnp.concatenate([m[b : b + rows].reshape(rows * pairs, wide) for m in mixed], axis=0)
        for b in range(3)
    ]
    mine, moved = products(parts, taps, channels)
    return [*mine, *moved]


def add_moved(mine, moved, pairs):
    place = lax.broadcasted_iota(jnp.int32, mine[0].shape, 0) % pairs
    count = mine[0].shape[0]
    left = jnp.where(place == 0, 0.0, pltpu.roll(moved[0], 1, 0))
    right = jnp.where(place == pairs - 1, 0.0, pltpu.roll(moved[1], count - 1, 0))
    return mine[0] + left, mine[1] + right


def own_kernel(
    bands, deep, count, normed, weight, weight_two, gain_two, bias, bias_two, total, mixed_two, *window
):
    frames, rows, pairs, wide = normed.shape
    tm, space = lax.axis_index("tm"), lax.axis_index("space")
    nothing = jnp.zeros((pairs, wide), BF16)
    top = clear_rims(window[1:], bands, space, rows)
    window[0][...] = jnp.zeros(window[0].shape, BF16)
    for f in range(frames):
        good = tm * frames + f < count[0]
        for r in range(rows):
            window[f + 1][top + r] = jnp.where(good, normed[f, r], nothing)
    late = conv(window, weight, 1, frames - 2, deep, (0, 1, 2), wide // 2)
    soon = conv(window, weight, 0, 2, deep, (1, 2), wide // 2)
    mix_weights(weight_two, mixed_two)
    for q in range(2):
        total[q, 0:2] = soon[q].reshape(2, *total.shape[2:])
        total[q, 2:] = late[q].reshape(frames - 2, *total.shape[2:])


def clear_rims(window, bands, space, rows):
    for part in window:
        nothing = jnp.zeros(part.shape[1:], BF16)
        if bands == 2:
            part[(rows + 2) * space] = nothing
            for r in range(2):
                part[(rows + 1) * (1 - space) + r] = nothing
        else:
            for r in range(2):
                part[r] = nothing
                part[rows + 2 + r] = nothing
    return 1 + space if bands == 2 else 2


def earlier_kernel(bands, deep, count, mask, earlier, gain, weight, after, total, *scratch):
    frames, rows = earlier.shape[0], earlier.shape[1]
    window, stages = scratch[: frames + 1], scratch[frames + 1 :]
    pairs, wide = window[0].shape[1:]
    tm, space = lax.axis_index("tm"), lax.axis_index("space")

    @pl.when(tm > 0)
    def _():
        top = clear_rims(window[:frames], bands, space, rows)
        window[frames][...] = jnp.zeros(window[frames].shape, BF16)

        def store(f, r, parts):
            good = (tm - 1) * frames + f < count[0]
            for k in range(3):
                part = jnp.where(good, parts[k], jnp.zeros_like(parts[k]))
                window[f][top + r, :, k * LANES : (k + 1) * LANES] = part

        def norm(f):
            norm_frames(earlier, f, twice(gain), mask[...] > 0.5, stages[f // 2], store, pairs)

        norm(frames - 2)
        late = conv(window, weight, frames - 2, 2, deep, (0, 1), wide // 2)
        for f in range(0, frames - 2, 2):
            norm(f)
        for q in range(2):
            total[q, frames - 2 :] = late[q].reshape(2, *total.shape[2:])
        soon = conv(window, weight, 0, frames - 2, deep, (0, 1, 2), wide // 2)
        for q in range(2):
            total[q, 0 : frames - 2] = soon[q].reshape(frames - 2, *total.shape[2:])


def add_rims(total, near, far, weight, side, keep, channels, wanted):
    frames, pairs, wide = near.shape[0], near.shape[2], near.shape[3]
    deep = total[0].shape[1]
    low = (deep - 2) * side
    halo = (deep - 1) * side
    nothing = jnp.zeros((pairs, wide), BF16)

    def row(f, r):
        ref, at = (far, f) if f < frames else (near, f - frames)
        return jnp.where(keep(f), ref[at, r], nothing)

    span = len(wanted)
    rows = {f: [row(f, r) for r in range(2)] for f in range(wanted[0], wanted[-1] + 3)}
    inner = {f: row(f, 1 - side) for f in rows}
    parts = [jnp.concatenate([x for h in wanted for x in rows[h + a]], axis=0) for a in range(3)]
    added = add_moved(*products(parts, [weight[a, 2 * side] for a in range(3)], channels), pairs)
    for q in range(2):
        both = added[q].reshape(span, 2, pairs, channels)
        for n, h in enumerate(wanted):
            total[h][q, pl.ds(low, 2)] += both[n]
    parts = [jnp.concatenate([inner[h + a] for h in wanted], axis=0) for a in range(3)]
    added = add_moved(*products(parts, [weight[a, 1] for a in range(3)], channels), pairs)
    for q in range(2):
        one = added[q].reshape(span, pairs, channels)
        for n, h in enumerate(wanted):
            total[h][q, halo] += one[n]


def finish(bands, count, own, near, far, bias, weight, gain_two, bias_two, weight_two, mixed_two, out, total, hidden, mixed, final, ready):
    frames, rows, pairs, wide = near[0].shape[0], own.shape[1], near[0].shape[2], near[0].shape[3]
    channels = wide // 2
    deep = total[0].shape[1]
    tm, space = lax.axis_index("tm"), lax.axis_index("space")
    fill = deep * pairs

    def valid(f):
        at = (tm - 1) * frames + f
        return (at >= 0) & (at < count[0])

    def rims(wanted):
        if bands == 2:
            add_rims(total, near[0], far[0], weight, 1 - space, valid, channels, wanted)
        else:
            above = lambda f: valid(f) & (space > 0)
            below = lambda f: valid(f) & (space < bands - 1)
            add_rims(total, near[0], far[0], weight, 0, above, channels, wanted)
            add_rims(total, near[1], far[1], weight, 1, below, channels, wanted)

    start = (1 - space) if bands == 2 else 0
    row = lax.broadcasted_iota(jnp.int32, (fill, 1), 0) // pairs + (space * rows - 1 + start)
    row_ok = (row >= 0) & (row < bands * rows)
    bias_wide, gain_wide = twice(bias), twice(gain_two)
    first_lanes = lax.broadcasted_iota(jnp.int32, (fill, wide), 1) < channels

    def norm_hidden(h):
        good = row_ok & valid(frames + h - 2)
        t = jnp.concatenate([total[h][q].reshape(fill, channels) for q in range(2)], axis=1)
        t = jnp.where(good, t + bias_wide, 0.0).astype(BF16).astype(F32)
        y = norm_silu_pair(t, gain_wide, first_lanes, channels).astype(BF16)
        hidden[h][0] = jnp.zeros((pairs, wide), BF16)
        hidden[h][rows + 1] = jnp.zeros((pairs, wide), BF16)
        for r in range(deep):
            hidden[h][start + r] = y[r * pairs : (r + 1) * pairs]

    def product(i):
        for n in range(half):
            mix(hidden[2 * n : 2 * n + 4], i, mixed[half * i + n])
        taps = [(weight_two[0, b], mixed_two[0, b], mixed_two[1, b], weight_two[2, b])[i] for b in range(3)]
        return mixed_product(mixed[half * i : half * (i + 1)], taps, rows, channels)

    def emit(n, result):
        both = add_moved(result[:2], result[2:], pairs)
        both = jnp.concatenate(both, axis=1) + bias_two_wide
        for k in range(3):
            final[n][k] = both[:, k * LANES : (k + 1) * LANES]
        for m in range(0, half, 2):
            good = [valid(frames + n + 2 * (m + j)) for j in range(2)]
            for p in range(pairs):
                for k in range(3):
                    at = pl.ds(m * rows * pairs + p, 2 * rows, stride=pairs)
                    block = final[n][k, at, :]
                    lanes = pl.ds(p * wide + k * LANES, LANES)
                    for j in range(2):
                        f = n + 2 * (m + j)
                        value = own[f, :, lanes].astype(F32) + block[j * rows : (j + 1) * rows]
                        out[f, :, lanes] = jnp.where(good[j], value, 0.0).astype(BF16)
        for m in range(half):
            ready(n + 2 * m)

    half = frames // 2
    bias_two_wide = twice(bias_two)
    rims(range(4))
    for f in range(2, frames, 2):
        rims(range(f + 2, f + 4))
    for h in range(1, frames + 1):
        norm_hidden(h)
    one = product(1)
    two = product(2)
    norm_hidden(0)
    zero = product(0)
    norm_hidden(frames + 1)
    three = product(3)
    emit(0, [x - y - z for x, y, z in zip(zero, one, two)])
    emit(1, [z - y - x for x, y, z in zip(three, one, two)])


def first_block_kernel(
    bands, count, own, above, below, from_own, mixed_two, bias, weight, gain_two, bias_two,
    weight_two, out, *scratch,
):
    parts = split(scratch, own.shape[0])

    @pl.when(lax.axis_index("tm") == 0)
    def _():
        for h, part in enumerate(parts[0]):
            part[...] = jnp.zeros(part.shape, F32) if h < 2 else from_own[:, h - 2]
        near = (above, below)
        finish(
            bands, count, own, near, near, bias, weight, gain_two, bias_two, weight_two,
            mixed_two, out, *parts, lambda f: None,
        )


def split(scratch, frames):
    rest = scratch[2 * frames + 4 :]
    return scratch[: frames + 2], scratch[frames + 2 : 2 * frames + 4], rest[: 2 * frames], rest[2 * frames :]


def last_kernel(
    bands, count, own, above, below, far_above, far_below, from_own, from_earlier, first_out,
    mixed_two, bias, weight, gain_two, bias_two, weight_two, out, result, sems, *scratch,
):
    frames = own.shape[0]
    parts = split(scratch, frames)
    tm = lax.axis_index("tm")

    @pl.when(tm == 0)
    def _():
        copy = pltpu.make_async_copy(first_out, out, sems.at[0])
        copy.start()
        copy.wait()

    @pl.when(tm > 0)
    def _():
        for h, part in enumerate(parts[0]):
            if h < 2:
                part[...] = from_earlier[:, h]
            elif h < frames:
                part[...] = from_own[:, h - 2] + from_earlier[:, h]
            else:
                part[...] = from_own[:, h - 2]
        copies = [
            pltpu.make_async_copy(result.at[f], out.at[f], sems.at[f]) for f in range(frames)
        ]
        finish(
            bands, count, own, (above, below), (far_above, far_below), bias, weight, gain_two,
            bias_two, weight_two, mixed_two, result, *parts, lambda f: copies[f].start(),
        )
        for copy in copies:
            copy.wait()


def shards(latents, counts, gain_first, bias_first, weight_first, gain_second, bias_second, weight_second):
    channels = gain_first.shape[0]
    frames, rows, flat = latents.shape[1:]
    wide = 2 * channels
    pairs = flat // wide
    blocks, bands = lax.axis_size("tm"), lax.axis_size("space")
    block = latents.reshape(frames, rows, flat)

    def shift(sent, step, along):
        pairs_of = [
            (t * bands + s, (t + along) % blocks * bands + (s + step * (t + along < blocks)) % bands)
            for t in range(blocks)
            for s in range(bands)
        ]
        return lax.ppermute(sent, ("tm", "space"), pairs_of)

    vmem = pl.BlockSpec(memory_space=pltpu.VMEM)
    smem = pl.BlockSpec(memory_space=pltpu.SMEM)
    params = pltpu.CompilerParams(vmem_limit_bytes=24 << 20)
    swap = bands == 2
    rims = 1 if swap else 2
    rim = jax.ShapeDtypeStruct((frames, 2, pairs, wide), BF16)
    stages = [pltpu.VMEM((3, 2 * rows * pairs, LANES), F32)] * (frames // 2)
    mask = pl.pallas_call(
        functools.partial(mask_kernel, channels),
        out_shape=jax.ShapeDtypeStruct((2 * rows, wide), F32),
        out_specs=vmem,
        compiler_params=params,
        cost_estimate=pl.CostEstimate(flops=4 << 30, bytes_accessed=1 << 16, transcendentals=0),
        name="lane_mask",
    )()
    normed, *sent = pl.pallas_call(
        functools.partial(norm_kernel, swap),
        out_shape=[jax.ShapeDtypeStruct((frames, rows, pairs, wide), BF16)] + [rim] * rims,
        in_specs=[vmem] * 3,
        out_specs=[vmem] * (1 + rims),
        scratch_shapes=stages,
        compiler_params=params,
        cost_estimate=pl.CostEstimate(flops=4 << 30, bytes_accessed=1 << 20, transcendentals=0),
        name="norm_and_cut",
    )(mask, block, gain_first.reshape(1, channels))
    earlier = shift(block, 0, 1)
    if swap:
        near = (shift(sent[0], 1, 0),) * 2
        far = (shift(sent[0], 1, 1),) * 2
        deep = rows + 1
    else:
        near = (shift(sent[0], 1, 0), shift(sent[1], -1, 0))
        far = (shift(sent[0], 1, 1), shift(sent[1], -1, 1))
        deep = rows + 2

    first_weight = weight_first.reshape(3, 3, 3 * channels, channels)
    second_weight = weight_second.reshape(3, 3, 3 * channels, channels)
    share = (2, frames, deep, pairs, channels)
    window = [pltpu.VMEM((deep + 2, pairs, wide), BF16)] * (frames + 1)
    cost = pl.CostEstimate(flops=1 << 20, bytes_accessed=1 << 16, transcendentals=0)
    taps = jax.ShapeDtypeStruct((2, *first_weight.shape[1:]), BF16)
    from_own, mixed_two = pl.pallas_call(
        functools.partial(own_kernel, bands, deep),
        out_shape=[jax.ShapeDtypeStruct(share, F32), taps],
        in_specs=[smem] + [vmem] * 6,
        out_specs=[vmem] * 2,
        scratch_shapes=window,
        compiler_params=params,
        cost_estimate=cost,
        name="conv_one_own",
    )(
        counts, normed, first_weight, second_weight, gain_second.reshape(1, channels),
        bias_first.reshape(1, channels), bias_second.reshape(1, channels),
    )
    constants = (
        bias_first.reshape(1, channels), first_weight,
        gain_second.reshape(1, channels), bias_second.reshape(1, channels), second_weight,
    )
    result = jax.ShapeDtypeStruct((frames, rows, flat), BF16)
    scratch = (
        [pltpu.VMEM((2, deep, pairs, channels), F32)] * (frames + 2)
        + [pltpu.VMEM((rows + 2, pairs, wide), BF16)] * (frames + 2 + 2 * frames)
        + [pltpu.VMEM((3, frames // 2 * rows * pairs, LANES), F32)] * 2
    )
    first_out = pl.pallas_call(
        functools.partial(first_block_kernel, bands),
        out_shape=result,
        in_specs=[smem] + [vmem] * 10,
        out_specs=vmem,
        scratch_shapes=scratch,
        compiler_params=params,
        cost_estimate=cost,
        name="first_block",
    )(counts, block, *near, from_own, mixed_two, *constants)
    from_earlier = pl.pallas_call(
        functools.partial(earlier_kernel, bands, deep),
        out_shape=jax.ShapeDtypeStruct(share, F32),
        in_specs=[smem] + [vmem] * 5,
        out_specs=vmem,
        scratch_shapes=window + stages,
        compiler_params=params,
        cost_estimate=cost,
        name="conv_one_earlier",
    )(counts, mask, earlier, gain_first.reshape(1, channels), first_weight, first_out)
    out = pl.pallas_call(
        functools.partial(last_kernel, bands),
        out_shape=result,
        in_specs=[smem] + [vmem] * 14,
        out_specs=pl.BlockSpec(memory_space=pl.ANY),
        scratch_shapes=[
            pltpu.VMEM((frames, rows, flat), BF16), pltpu.SemaphoreType.DMA((frames,))
        ] + scratch,
        compiler_params=params,
        cost_estimate=pl.CostEstimate(flops=4 << 30, bytes_accessed=6 << 20, transcendentals=0),
        name="last",
    )(counts, block, *near, *far, from_own, from_earlier, first_out, mixed_two, *constants)
    return out.reshape(1, frames, rows, flat)


def solution(mesh):
    spread = P(("groups", "clip"), "tm", "space", None)
    return jax.shard_map(
        shards,
        mesh=mesh,
        in_specs=(spread, P(("groups", "clip")), P(), P(), P(), P(), P(), P()),
        out_specs=spread,
        check_vma=False,
    )
```

```python
import functools

import jax
import jax.numpy as jnp
from jax import lax
from jax.experimental import pallas as pl
from jax.experimental.pallas import tpu as pltpu
from jax.sharding import PartitionSpec as P

F32 = jnp.float32
BF16 = jnp.bfloat16
LANES = 128


def mask_kernel(channels, mask):
    lane = lax.broadcasted_iota(jnp.int32, mask.shape, 1)
    mask[...] = jnp.where(lane < channels, 1.0, 0.0)


def norm_silu_pair(t, gain, first, channels):
    square = t * t
    left = jnp.sum(jnp.where(first, square, 0.0), axis=1, keepdims=True)
    right = jnp.sum(jnp.where(first, 0.0, square), axis=1, keepdims=True)
    left = lax.rsqrt(left * (1.0 / channels) + 1e-06)
    right = lax.rsqrt(right * (1.0 / channels) + 1e-06)
    y = t * jnp.where(first, left, right) * gain
    return y * (0.5 + 0.5 * jnp.tanh(0.5 * y))


def twice(ref):
    return jnp.concatenate([ref[...], ref[...]], axis=1)


def norm_frames(block, f, gain_wide, first, stage, store, pairs):
    rows = block.shape[1]
    wide = gain_wide.shape[1]
    for p in range(pairs):
        lanes = pl.ds(p * wide, wide)
        t = jnp.concatenate([block[f + n, :, lanes].astype(F32) for n in range(2)], axis=0)
        y = norm_silu_pair(t, gain_wide, first, wide // 2)
        for k in range(3):
            stage[k, pl.ds(p, 2 * rows, stride=pairs), :] = y[:, k * LANES : (k + 1) * LANES]
    for n in range(2):
        for r in range(rows):
            at = pl.ds((n * rows + r) * pairs, pairs)
            store(f + n, r, [stage[k, at, :].astype(BF16) for k in range(3)])


def norm_kernel(swap, mask, block, gain, normed, *rest):
    frames, rows, pairs, _ = normed.shape
    sent, stages = rest[: -(frames // 2)], rest[-(frames // 2) :]

    def store(f, r, parts):
        for k in range(3):
            normed[f, r, :, k * LANES : (k + 1) * LANES] = parts[k]

    for f in range(0, frames, 2):
        norm_frames(block, f, twice(gain), mask[...] > 0.5, stages[f // 2], store, pairs)
    if swap:
        first = (rows - 2) * (1 - lax.axis_index("space"))
        sent[0][...] = normed[:, pl.ds(first, 2)]
    else:
        sent[0][...] = normed[:, rows - 2 :]
        sent[1][...] = normed[:, :2]


def dot(left, right):
    return jnp.dot(
        jnp.concatenate(left, axis=1), jnp.concatenate(right, axis=0), preferred_element_type=F32
    )


def products(parts, rims, channels):
    lead = jnp.zeros((2 * LANES - channels, channels), BF16)
    mine = (
        dot(parts, [w[channels:] for w in rims]),
        dot(parts, [w[: 2 * channels] for w in rims]),
    )
    high = [x[:, LANES:] for x in parts]
    low = [x[:, : 2 * LANES] for x in parts]
    moved = (
        dot(high, [x for w in rims for x in (lead, w[:channels])]),
        dot(low, [x for w in rims for x in (w[2 * channels :], lead)]),
    )
    return mine, moved


def conv(window, weight, source, frames, rows, times, channels):
    pairs, wide = window[0].shape[1:]
    taps = [(a, b) for a in times for b in range(3)]

    def patch(a, b):
        at = source + a - times[0]
        rows_of = [window[f][b : b + rows].reshape(rows * pairs, wide) for f in range(at, at + frames)]
        return jnp.concatenate(rows_of, axis=0)

    parts = [patch(a, b) for a, b in taps]
    return add_moved(*products(parts, [weight[a, b] for a, b in taps], channels), pairs)


def mix_weights(weight, mixed):
    for b in range(3):
        outer = weight[0, b] + weight[2, b]
        mixed[0, b] = outer + weight[1, b]
        mixed[1, b] = outer - weight[1, b]


def mix(frames, i, out):
    if i == 1:
        out[...] = (frames[1][...] + frames[2][...]) * -0.5
    elif i == 2:
        out[...] = (frames[1][...] - frames[2][...]) * 0.5
    else:
        one, other = (0, 2) if i == 0 else (1, 3)
        out[...] = frames[one][...] - frames[other][...]


def mixed_product(mixed, taps, rows, channels):
    pairs, wide = mixed[0].shape[1:]
    parts = [
        jnp.concatenate([m[b : b + rows].reshape(rows * pairs, wide) for m in mixed], axis=0)
        for b in range(3)
    ]
    mine, moved = products(parts, taps, channels)
    return [*mine, *moved]


def add_moved(mine, moved, pairs):
    place = lax.broadcasted_iota(jnp.int32, mine[0].shape, 0) % pairs
    count = mine[0].shape[0]
    left = jnp.where(place == 0, 0.0, pltpu.roll(moved[0], 1, 0))
    right = jnp.where(place == pairs - 1, 0.0, pltpu.roll(moved[1], count - 1, 0))
    return mine[0] + left, mine[1] + right


def own_kernel(
    bands, deep, count, normed, weight, weight_two, gain_two, bias, bias_two, total, mixed_two, *window
):
    frames, rows, pairs, wide = normed.shape
    tm, space = lax.axis_index("tm"), lax.axis_index("space")
    nothing = jnp.zeros((pairs, wide), BF16)
    top = clear_rims(window[1:], bands, space, rows)
    window[0][...] = jnp.zeros(window[0].shape, BF16)
    for f in range(frames):
        good = tm * frames + f < count[0]
        for r in range(rows):
            window[f + 1][top + r] = jnp.where(good, normed[f, r], nothing)
    late = conv(window, weight, 1, frames - 2, deep, (0, 1, 2), wide // 2)
    soon = conv(window, weight, 0, 2, deep, (1, 2), wide // 2)
    mix_weights(weight_two, mixed_two)
    for q in range(2):
        total[q, 0:2] = soon[q].reshape(2, *total.shape[2:])
        total[q, 2:] = late[q].reshape(frames - 2, *total.shape[2:])


def clear_rims(window, bands, space, rows):
    for part in window:
        nothing = jnp.zeros(part.shape[1:], BF16)
        if bands == 2:
            part[(rows + 2) * space] = nothing
            for r in range(2):
                part[(rows + 1) * (1 - space) + r] = nothing
        else:
            for r in range(2):
                part[r] = nothing
                part[rows + 2 + r] = nothing
    return 1 + space if bands == 2 else 2


def earlier_kernel(bands, deep, count, mask, earlier, gain, weight, after, total, *scratch):
    frames, rows = earlier.shape[0], earlier.shape[1]
    window, stages = scratch[: frames + 1], scratch[frames + 1 :]
    pairs, wide = window[0].shape[1:]
    tm, space = lax.axis_index("tm"), lax.axis_index("space")

    @pl.when(tm > 0)
    def _():
        top = clear_rims(window[:frames], bands, space, rows)
        window[frames][...] = jnp.zeros(window[frames].shape, BF16)

        def store(f, r, parts):
            good = (tm - 1) * frames + f < count[0]
            for k in range(3):
                part = jnp.where(good, parts[k], jnp.zeros_like(parts[k]))
                window[f][top + r, :, k * LANES : (k + 1) * LANES] = part

        def norm(f):
            norm_frames(earlier, f, twice(gain), mask[...] > 0.5, stages[f // 2], store, pairs)

        norm(frames - 2)
        late = conv(window, weight, frames - 2, 2, deep, (0, 1), wide // 2)
        for f in range(0, frames - 2, 2):
            norm(f)
        for q in range(2):
            total[q, frames - 2 :] = late[q].reshape(2, *total.shape[2:])
        soon = conv(window, weight, 0, frames - 2, deep, (0, 1, 2), wide // 2)
        for q in range(2):
            total[q, 0 : frames - 2] = soon[q].reshape(frames - 2, *total.shape[2:])


def add_rims(total, near, far, weight, side, keep, channels, wanted):
    frames, pairs, wide = near.shape[0], near.shape[2], near.shape[3]
    deep = total[0].shape[1]
    low = (deep - 2) * side
    halo = (deep - 1) * side
    nothing = jnp.zeros((pairs, wide), BF16)

    def row(f, r):
        ref, at = (far, f) if f < frames else (near, f - frames)
        return jnp.where(keep(f), ref[at, r], nothing)

    span = len(wanted)
    rows = {f: [row(f, r) for r in range(2)] for f in range(wanted[0], wanted[-1] + 3)}
    inner = {f: row(f, 1 - side) for f in rows}
    parts = [jnp.concatenate([x for h in wanted for x in rows[h + a]], axis=0) for a in range(3)]
    added = add_moved(*products(parts, [weight[a, 2 * side] for a in range(3)], channels), pairs)
    for q in range(2):
        both = added[q].reshape(span, 2, pairs, channels)
        for n, h in enumerate(wanted):
            total[h][q, pl.ds(low, 2)] += both[n]
    parts = [jnp.concatenate([inner[h + a] for h in wanted], axis=0) for a in range(3)]
    added = add_moved(*products(parts, [weight[a, 1] for a in range(3)], channels), pairs)
    for q in range(2):
        one = added[q].reshape(span, pairs, channels)
        for n, h in enumerate(wanted):
            total[h][q, halo] += one[n]


def finish(bands, count, own, near, far, bias, weight, gain_two, bias_two, weight_two, mixed_two, out, total, hidden, mixed, final, ready):
    frames, rows, pairs, wide = near[0].shape[0], own.shape[1], near[0].shape[2], near[0].shape[3]
    channels = wide // 2
    deep = total[0].shape[1]
    tm, space = lax.axis_index("tm"), lax.axis_index("space")
    fill = deep * pairs

    def valid(f):
        at = (tm - 1) * frames + f
        return (at >= 0) & (at < count[0])

    def rims(wanted):
        if bands == 2:
            add_rims(total, near[0], far[0], weight, 1 - space, valid, channels, wanted)
        else:
            above = lambda f: valid(f) & (space > 0)
            below = lambda f: valid(f) & (space < bands - 1)
            add_rims(total, near[0], far[0], weight, 0, above, channels, wanted)
            add_rims(total, near[1], far[1], weight, 1, below, channels, wanted)

    start = (1 - space) if bands == 2 else 0
    row = lax.broadcasted_iota(jnp.int32, (fill, 1), 0) // pairs + (space * rows - 1 + start)
    row_ok = (row >= 0) & (row < bands * rows)
    bias_wide, gain_wide = twice(bias), twice(gain_two)
    first_lanes = lax.broadcasted_iota(jnp.int32, (fill, wide), 1) < channels

    def norm_hidden(h):
        good = row_ok & valid(frames + h - 2)
        t = jnp.concatenate([total[h][q].reshape(fill, channels) for q in range(2)], axis=1)
        t = jnp.where(good, t + bias_wide, 0.0).astype(BF16).astype(F32)
        y = norm_silu_pair(t, gain_wide, first_lanes, channels).astype(BF16)
        hidden[h][0] = jnp.zeros((pairs, wide), BF16)
        hidden[h][rows + 1] = jnp.zeros((pairs, wide), BF16)
        for r in range(deep):
            hidden[h][start + r] = y[r * pairs : (r + 1) * pairs]

    def product(i):
        for n in range(half):
            mix(hidden[2 * n : 2 * n + 4], i, mixed[half * i + n])
        taps = [(weight_two[0, b], mixed_two[0, b], mixed_two[1, b], weight_two[2, b])[i] for b in range(3)]
        return mixed_product(mixed[half * i : half * (i + 1)], taps, rows, channels)

    def emit(n, result):
        both = add_moved(result[:2], result[2:], pairs)
        both = jnp.concatenate(both, axis=1) + bias_two_wide
        for k in range(3):
            final[n][k] = both[:, k * LANES : (k + 1) * LANES]
        for m in range(0, half, 2):
            good = [valid(frames + n + 2 * (m + j)) for j in range(2)]
            for p in range(pairs):
                for k in range(3):
                    at = pl.ds(m * rows * pairs + p, 2 * rows, stride=pairs)
                    block = final[n][k, at, :]
                    lanes = pl.ds(p * wide + k * LANES, LANES)
                    for j in range(2):
                        f = n + 2 * (m + j)
                        value = own[f, :, lanes].astype(F32) + block[j * rows : (j + 1) * rows]
                        out[f, :, lanes] = jnp.where(good[j], value, 0.0).astype(BF16)
        for m in range(half):
            ready(n + 2 * m)

    half = frames // 2
    bias_two_wide = twice(bias_two)
    rims(range(frames + 2))
    for h in range(1, frames + 1):
        norm_hidden(h)
    one = product(1)
    two = product(2)
    norm_hidden(0)
    zero = product(0)
    norm_hidden(frames + 1)
    three = product(3)
    emit(0, [x - y - z for x, y, z in zip(zero, one, two)])
    emit(1, [z - y - x for x, y, z in zip(three, one, two)])


def first_block_kernel(
    bands, count, own, above, below, from_own, mixed_two, bias, weight, gain_two, bias_two,
    weight_two, out, *scratch,
):
    parts = split(scratch, own.shape[0])

    @pl.when(lax.axis_index("tm") == 0)
    def _():
        for h, part in enumerate(parts[0]):
            part[...] = jnp.zeros(part.shape, F32) if h < 2 else from_own[:, h - 2]
        near = (above, below)
        finish(
            bands, count, own, near, near, bias, weight, gain_two, bias_two, weight_two,
            mixed_two, out, *parts, lambda f: None,
        )


def split(scratch, frames):
    rest = scratch[2 * frames + 4 :]
    return scratch[: frames + 2], scratch[frames + 2 : 2 * frames + 4], rest[: 2 * frames], rest[2 * frames :]


def last_kernel(
    bands, count, own, above, below, far_above, far_below, from_own, from_earlier, first_out,
    mixed_two, bias, weight, gain_two, bias_two, weight_two, out, result, sems, *scratch,
):
    frames = own.shape[0]
    parts = split(scratch, frames)
    tm = lax.axis_index("tm")

    @pl.when(tm == 0)
    def _():
        copy = pltpu.make_async_copy(first_out, out, sems.at[0])
        copy.start()
        copy.wait()

    @pl.when(tm > 0)
    def _():
        for h, part in enumerate(parts[0]):
            if h < 2:
                part[...] = from_earlier[:, h]
            elif h < frames:
                part[...] = from_own[:, h - 2] + from_earlier[:, h]
            else:
                part[...] = from_own[:, h - 2]
        copies = [
            pltpu.make_async_copy(result.at[f], out.at[f], sems.at[f]) for f in range(frames)
        ]
        finish(
            bands, count, own, (above, below), (far_above, far_below), bias, weight, gain_two,
            bias_two, weight_two, mixed_two, result, *parts, lambda f: copies[f].start(),
        )
        for copy in copies:
            copy.wait()


def shards(latents, counts, gain_first, bias_first, weight_first, gain_second, bias_second, weight_second):
    channels = gain_first.shape[0]
    frames, rows, flat = latents.shape[1:]
    wide = 2 * channels
    pairs = flat // wide
    blocks, bands = lax.axis_size("tm"), lax.axis_size("space")
    block = latents.reshape(frames, rows, flat)

    def shift(sent, step, along):
        pairs_of = [
            (t * bands + s, (t + along) % blocks * bands + (s + step * (t + along < blocks)) % bands)
            for t in range(blocks)
            for s in range(bands)
        ]
        return lax.ppermute(sent, ("tm", "space"), pairs_of)

    vmem = pl.BlockSpec(memory_space=pltpu.VMEM)
    smem = pl.BlockSpec(memory_space=pltpu.SMEM)
    params = pltpu.CompilerParams(vmem_limit_bytes=24 << 20)
    swap = bands == 2
    rims = 1 if swap else 2
    rim = jax.ShapeDtypeStruct((frames, 2, pairs, wide), BF16)
    stages = [pltpu.VMEM((3, 2 * rows * pairs, LANES), F32)] * (frames // 2)
    mask = pl.pallas_call(
        functools.partial(mask_kernel, channels),
        out_shape=jax.ShapeDtypeStruct((2 * rows, wide), F32),
        out_specs=vmem,
        compiler_params=params,
        cost_estimate=pl.CostEstimate(flops=4 << 30, bytes_accessed=1 << 16, transcendentals=0),
        name="lane_mask",
    )()
    normed, *sent = pl.pallas_call(
        functools.partial(norm_kernel, swap),
        out_shape=[jax.ShapeDtypeStruct((frames, rows, pairs, wide), BF16)] + [rim] * rims,
        in_specs=[vmem] * 3,
        out_specs=[vmem] * (1 + rims),
        scratch_shapes=stages,
        compiler_params=params,
        cost_estimate=pl.CostEstimate(flops=4 << 30, bytes_accessed=1 << 20, transcendentals=0),
        name="norm_and_cut",
    )(mask, block, gain_first.reshape(1, channels))
    earlier = shift(block, 0, 1)
    if swap:
        near = (shift(sent[0], 1, 0),) * 2
        far = (shift(sent[0], 1, 1),) * 2
        deep = rows + 1
    else:
        near = (shift(sent[0], 1, 0), shift(sent[1], -1, 0))
        far = (shift(sent[0], 1, 1), shift(sent[1], -1, 1))
        deep = rows + 2

    first_weight = weight_first.reshape(3, 3, 3 * channels, channels)
    second_weight = weight_second.reshape(3, 3, 3 * channels, channels)
    share = (2, frames, deep, pairs, channels)
    window = [pltpu.VMEM((deep + 2, pairs, wide), BF16)] * (frames + 1)
    cost = pl.CostEstimate(flops=1 << 20, bytes_accessed=1 << 16, transcendentals=0)
    taps = jax.ShapeDtypeStruct((2, *first_weight.shape[1:]), BF16)
    from_own, mixed_two = pl.pallas_call(
        functools.partial(own_kernel, bands, deep),
        out_shape=[jax.ShapeDtypeStruct(share, F32), taps],
        in_specs=[smem] + [vmem] * 6,
        out_specs=[vmem] * 2,
        scratch_shapes=window,
        compiler_params=params,
        cost_estimate=cost,
        name="conv_one_own",
    )(
        counts, normed, first_weight, second_weight, gain_second.reshape(1, channels),
        bias_first.reshape(1, channels), bias_second.reshape(1, channels),
    )
    constants = (
        bias_first.reshape(1, channels), first_weight,
        gain_second.reshape(1, channels), bias_second.reshape(1, channels), second_weight,
    )
    result = jax.ShapeDtypeStruct((frames, rows, flat), BF16)
    scratch = (
        [pltpu.VMEM((2, deep, pairs, channels), F32)] * (frames + 2)
        + [pltpu.VMEM((rows + 2, pairs, wide), BF16)] * (frames + 2 + 2 * frames)
        + [pltpu.VMEM((3, frames // 2 * rows * pairs, LANES), F32)] * 2
    )
    first_out = pl.pallas_call(
        functools.partial(first_block_kernel, bands),
        out_shape=result,
        in_specs=[smem] + [vmem] * 10,
        out_specs=vmem,
        scratch_shapes=scratch,
        compiler_params=params,
        cost_estimate=cost,
        name="first_block",
    )(counts, block, *near, from_own, mixed_two, *constants)
    from_earlier = pl.pallas_call(
        functools.partial(earlier_kernel, bands, deep),
        out_shape=jax.ShapeDtypeStruct(share, F32),
        in_specs=[smem] + [vmem] * 5,
        out_specs=vmem,
        scratch_shapes=window + stages,
        compiler_params=params,
        cost_estimate=cost,
        name="conv_one_earlier",
    )(counts, mask, earlier, gain_first.reshape(1, channels), first_weight, first_out)
    out = pl.pallas_call(
        functools.partial(last_kernel, bands),
        out_shape=result,
        in_specs=[smem] + [vmem] * 14,
        out_specs=pl.BlockSpec(memory_space=pl.ANY),
        scratch_shapes=[
            pltpu.VMEM((frames, rows, flat), BF16), pltpu.SemaphoreType.DMA((frames,))
        ] + scratch,
        compiler_params=params,
        cost_estimate=pl.CostEstimate(flops=4 << 30, bytes_accessed=6 << 20, transcendentals=0),
        name="last",
    )(counts, block, *near, *far, from_own, from_earlier, first_out, mixed_two, *constants)
    return out.reshape(1, frames, rows, flat)


def solution(mesh):
    spread = P(("groups", "clip"), "tm", "space", None)
    return jax.shard_map(
        shards,
        mesh=mesh,
        in_specs=(spread, P(("groups", "clip")), P(), P(), P(), P(), P(), P()),
        out_specs=spread,
        check_vma=False,
    )
```

```python
import functools

import jax
import jax.numpy as jnp
from jax import lax
from jax.experimental import pallas as pl
from jax.experimental.pallas import tpu as pltpu
from jax.sharding import PartitionSpec as P

F32 = jnp.float32
BF16 = jnp.bfloat16
LANES = 128


def mask_kernel(channels, mask):
    lane = lax.broadcasted_iota(jnp.int32, mask.shape, 1)
    mask[...] = jnp.where(lane < channels, 1.0, 0.0)


def norm_silu_pair(t, gain, first, channels):
    square = t * t
    left = jnp.sum(jnp.where(first, square, 0.0), axis=1, keepdims=True)
    right = jnp.sum(jnp.where(first, 0.0, square), axis=1, keepdims=True)
    left = lax.rsqrt(left * (1.0 / channels) + 1e-06)
    right = lax.rsqrt(right * (1.0 / channels) + 1e-06)
    y = t * jnp.where(first, left, right) * gain
    return y * (0.5 + 0.5 * jnp.tanh(0.5 * y))


def twice(ref):
    return jnp.concatenate([ref[...], ref[...]], axis=1)


def norm_frames(block, f, gain_wide, first, stage, store, pairs):
    rows = block.shape[1]
    wide = gain_wide.shape[1]
    for p in range(pairs):
        lanes = pl.ds(p * wide, wide)
        t = jnp.concatenate([block[f + n, :, lanes].astype(F32) for n in range(2)], axis=0)
        y = norm_silu_pair(t, gain_wide, first, wide // 2)
        for k in range(3):
            stage[k, pl.ds(p, 2 * rows, stride=pairs), :] = y[:, k * LANES : (k + 1) * LANES]
    for n in range(2):
        for r in range(rows):
            at = pl.ds((n * rows + r) * pairs, pairs)
            store(f + n, r, [stage[k, at, :].astype(BF16) for k in range(3)])


def norm_kernel(swap, mask, block, gain, normed, *rest):
    frames, rows, pairs, _ = normed.shape
    sent, stages = rest[: -(frames // 2)], rest[-(frames // 2) :]

    def store(f, r, parts):
        for k in range(3):
            normed[f, r, :, k * LANES : (k + 1) * LANES] = parts[k]

    for f in range(0, frames, 2):
        norm_frames(block, f, twice(gain), mask[...] > 0.5, stages[f // 2], store, pairs)
    if swap:
        first = (rows - 2) * (1 - lax.axis_index("space"))
        sent[0][...] = normed[:, pl.ds(first, 2)]
    else:
        sent[0][...] = normed[:, rows - 2 :]
        sent[1][...] = normed[:, :2]


def dot(left, right):
    return jnp.dot(
        jnp.concatenate(left, axis=1), jnp.concatenate(right, axis=0), preferred_element_type=F32
    )


def products(parts, rims, channels):
    lead = jnp.zeros((2 * LANES - channels, channels), BF16)
    mine = (
        dot(parts, [w[channels:] for w in rims]),
        dot(parts, [w[: 2 * channels] for w in rims]),
    )
    high = [x[:, LANES:] for x in parts]
    low = [x[:, : 2 * LANES] for x in parts]
    moved = (
        dot(high, [x for w in rims for x in (lead, w[:channels])]),
        dot(low, [x for w in rims for x in (w[2 * channels :], lead)]),
    )
    return mine, moved


def conv(window, weight, source, frames, rows, times, channels):
    pairs, wide = window[0].shape[1:]
    taps = [(a, b) for a in times for b in range(3)]

    def patch(a, b):
        at = source + a - times[0]
        rows_of = [window[f][b : b + rows].reshape(rows * pairs, wide) for f in range(at, at + frames)]
        return jnp.concatenate(rows_of, axis=0)

    parts = [patch(a, b) for a, b in taps]
    return add_moved(*products(parts, [weight[a, b] for a, b in taps], channels), pairs)


def mix_weights(weight, mixed):
    for b in range(3):
        outer = weight[0, b] + weight[2, b]
        mixed[0, b] = outer + weight[1, b]
        mixed[1, b] = outer - weight[1, b]


def mix(frames, i, out):
    if i == 1:
        out[...] = (frames[1][...] + frames[2][...]) * -0.5
    elif i == 2:
        out[...] = (frames[1][...] - frames[2][...]) * 0.5
    else:
        one, other = (0, 2) if i == 0 else (1, 3)
        out[...] = frames[one][...] - frames[other][...]


def mixed_product(mixed, taps, rows, channels):
    pairs, wide = mixed[0].shape[1:]
    parts = [
        jnp.concatenate([m[b : b + rows].reshape(rows * pairs, wide) for m in mixed], axis=0)
        for b in range(3)
    ]
    mine, moved = products(parts, taps, channels)
    return [*mine, *moved]


def add_moved(mine, moved, pairs):
    place = lax.broadcasted_iota(jnp.int32, mine[0].shape, 0) % pairs
    count = mine[0].shape[0]
    left = jnp.where(place == 0, 0.0, pltpu.roll(moved[0], 1, 0))
    right = jnp.where(place == pairs - 1, 0.0, pltpu.roll(moved[1], count - 1, 0))
    return mine[0] + left, mine[1] + right


def own_kernel(
    bands, deep, count, normed, weight, weight_two, gain_two, bias, bias_two, total, mixed_two, *window
):
    frames, rows, pairs, wide = normed.shape
    tm, space = lax.axis_index("tm"), lax.axis_index("space")
    nothing = jnp.zeros((pairs, wide), BF16)
    top = clear_rims(window[1:], bands, space, rows)
    window[0][...] = jnp.zeros(window[0].shape, BF16)
    for f in range(frames):
        good = tm * frames + f < count[0]
        for r in range(rows):
            window[f + 1][top + r] = jnp.where(good, normed[f, r], nothing)
    late = conv(window, weight, 1, frames - 2, deep, (0, 1, 2), wide // 2)
    soon = conv(window, weight, 0, 2, deep, (1, 2), wide // 2)
    mix_weights(weight_two, mixed_two)
    for q in range(2):
        total[q, 0:2] = soon[q].reshape(2, *total.shape[2:])
        total[q, 2:] = late[q].reshape(frames - 2, *total.shape[2:])


def clear_rims(window, bands, space, rows):
    for part in window:
        nothing = jnp.zeros(part.shape[1:], BF16)
        if bands == 2:
            part[(rows + 2) * space] = nothing
            for r in range(2):
                part[(rows + 1) * (1 - space) + r] = nothing
        else:
            for r in range(2):
                part[r] = nothing
                part[rows + 2 + r] = nothing
    return 1 + space if bands == 2 else 2


def earlier_kernel(bands, deep, count, mask, earlier, gain, weight, after, total, *scratch):
    frames, rows = earlier.shape[0], earlier.shape[1]
    window, stages = scratch[: frames + 1], scratch[frames + 1 :]
    pairs, wide = window[0].shape[1:]
    tm, space = lax.axis_index("tm"), lax.axis_index("space")

    @pl.when(tm > 0)
    def _():
        top = clear_rims(window[:frames], bands, space, rows)
        window[frames][...] = jnp.zeros(window[frames].shape, BF16)

        def store(f, r, parts):
            good = (tm - 1) * frames + f < count[0]
            for k in range(3):
                part = jnp.where(good, parts[k], jnp.zeros_like(parts[k]))
                window[f][top + r, :, k * LANES : (k + 1) * LANES] = part

        def norm(f):
            norm_frames(earlier, f, twice(gain), mask[...] > 0.5, stages[f // 2], store, pairs)

        norm(frames - 2)
        late = conv(window, weight, frames - 2, 2, deep, (0, 1), wide // 2)
        for f in range(0, frames - 2, 2):
            norm(f)
        for q in range(2):
            total[q, frames - 2 :] = late[q].reshape(2, *total.shape[2:])
        soon = conv(window, weight, 0, frames - 2, deep, (0, 1, 2), wide // 2)
        for q in range(2):
            total[q, 0 : frames - 2] = soon[q].reshape(frames - 2, *total.shape[2:])


def rim_sums(near, far, weight, side, keep, channels, frames):
    pairs, wide = near.shape[2], near.shape[3]
    nothing = jnp.zeros((pairs, wide), BF16)

    def row(f, r):
        ref, at = (far, f) if f < frames else (near, f - frames)
        return jnp.where(keep(f), ref[at, r], nothing)

    span = frames + 2
    rows = [[row(f, r) for r in range(2)] for f in range(2 * frames)]
    inner = [row(f, 1 - side) for f in range(2 * frames)]
    parts = [
        jnp.concatenate([x for f in range(span) for x in rows[f + a]], axis=0) for a in range(3)
    ]
    both = add_moved(*products(parts, [weight[a, 2 * side] for a in range(3)], channels), pairs)
    parts = [jnp.concatenate([inner[f + a] for f in range(span)], axis=0) for a in range(3)]
    outer = add_moved(*products(parts, [weight[a, 1] for a in range(3)], channels), pairs)
    tall = 2 * pairs
    halo = lax.broadcasted_iota(jnp.int32, (tall, channels), 0) // pairs == side

    def at(q, h):
        one = outer[q][h * pairs : (h + 1) * pairs]
        one = jnp.where(halo, jnp.concatenate([one, one], axis=0), 0.0)
        return both[q][h * tall : (h + 1) * tall] + one

    return at


def finish(bands, count, own, near, far, bias, weight, gain_two, bias_two, weight_two, mixed_two, out, total, hidden, mixed, final, ready):
    frames, rows, pairs, wide = near[0].shape[0], own.shape[1], near[0].shape[2], near[0].shape[3]
    channels = wide // 2
    deep = total[0].shape[1]
    tm, space = lax.axis_index("tm"), lax.axis_index("space")
    fill = deep * pairs

    def valid(f):
        at = (tm - 1) * frames + f
        return (at >= 0) & (at < count[0])

    start = (1 - space) if bands == 2 else 0
    if bands == 2:
        sides = [(near[0], far[0], 1 - space, valid)]
        first, deep_inner = 2 * space, deep - 2
    else:
        sides = [
            (near[0], far[0], 0, lambda f: valid(f) & (space > 0)),
            (near[1], far[1], 1, lambda f: valid(f) & (space < bands - 1)),
        ]
        first, deep_inner = 2, deep - 4
    bias_wide, gain_wide = twice(bias), twice(gain_two)

    def norm_rows(h, sums, base):
        t = jnp.concatenate(sums, axis=1)
        number = t.shape[0] // pairs
        row = lax.broadcasted_iota(jnp.int32, (t.shape[0], 1), 0) // pairs
        row = row + (space * rows - 1 + start + base)
        good = (row >= 0) & (row < bands * rows) & valid(frames + h - 2)
        t = jnp.where(good, t + bias_wide, 0.0).astype(BF16).astype(F32)
        lanes = lax.broadcasted_iota(jnp.int32, t.shape, 1) < channels
        y = norm_silu_pair(t, gain_wide, lanes, channels).astype(BF16)
        for r in range(number):
            hidden[h][start + base + r] = y[r * pairs : (r + 1) * pairs]

    def rows_of(h, q, base, number):
        return total[h][q, pl.ds(base, number)].reshape(number * pairs, channels)

    def norm_rims(h):
        for (_, _, side, _), sums in zip(sides, added):
            low = (deep - 2) * side
            norm_rows(h, [rows_of(h, q, low, 2) + sums(q, h) for q in range(2)], low)

    def product(i):
        for n in range(half):
            mix(hidden[2 * n : 2 * n + 4], i, mixed[half * i + n])
        taps = [(weight_two[0, b], mixed_two[0, b], mixed_two[1, b], weight_two[2, b])[i] for b in range(3)]
        return mixed_product(mixed[half * i : half * (i + 1)], taps, rows, channels)

    def emit(n, result):
        both = add_moved(result[:2], result[2:], pairs)
        both = jnp.concatenate(both, axis=1) + bias_two_wide
        for k in range(3):
            final[n][k] = both[:, k * LANES : (k + 1) * LANES]
        for m in range(0, half, 2):
            good = [valid(frames + n + 2 * (m + j)) for j in range(2)]
            for p in range(pairs):
                for k in range(3):
                    at = pl.ds(m * rows * pairs + p, 2 * rows, stride=pairs)
                    block = final[n][k, at, :]
                    lanes = pl.ds(p * wide + k * LANES, LANES)
                    for j in range(2):
                        f = n + 2 * (m + j)
                        value = own[f, :, lanes].astype(F32) + block[j * rows : (j + 1) * rows]
                        out[f, :, lanes] = jnp.where(good[j], value, 0.0).astype(BF16)
        for m in range(half):
            ready(n + 2 * m)

    half = frames // 2
    bias_two_wide = twice(bias_two)
    added = [rim_sums(n, f, weight, side, keep, channels, frames) for n, f, side, keep in sides]
    for h in range(frames + 2):
        hidden[h][0] = jnp.zeros((pairs, wide), BF16)
        hidden[h][rows + 1] = jnp.zeros((pairs, wide), BF16)
        norm_rows(h, [rows_of(h, q, first, deep_inner) for q in range(2)], first)
    for h in range(1, frames + 1):
        norm_rims(h)
    one = product(1)
    two = product(2)
    norm_rims(0)
    zero = product(0)
    norm_rims(frames + 1)
    three = product(3)
    emit(0, [x - y - z for x, y, z in zip(zero, one, two)])
    emit(1, [z - y - x for x, y, z in zip(three, one, two)])


def first_block_kernel(
    bands, count, own, above, below, from_own, mixed_two, bias, weight, gain_two, bias_two,
    weight_two, out, *scratch,
):
    parts = split(scratch, own.shape[0])

    @pl.when(lax.axis_index("tm") == 0)
    def _():
        for h, part in enumerate(parts[0]):
            part[...] = jnp.zeros(part.shape, F32) if h < 2 else from_own[:, h - 2]
        near = (above, below)
        finish(
            bands, count, own, near, near, bias, weight, gain_two, bias_two, weight_two,
            mixed_two, out, *parts, lambda f: None,
        )


def split(scratch, frames):
    rest = scratch[2 * frames + 4 :]
    return scratch[: frames + 2], scratch[frames + 2 : 2 * frames + 4], rest[: 2 * frames], rest[2 * frames :]


def last_kernel(
    bands, count, own, above, below, far_above, far_below, from_own, from_earlier, first_out,
    mixed_two, bias, weight, gain_two, bias_two, weight_two, out, result, sems, *scratch,
):
    frames = own.shape[0]
    parts = split(scratch, frames)
    tm = lax.axis_index("tm")

    @pl.when(tm == 0)
    def _():
        copy = pltpu.make_async_copy(first_out, out, sems.at[0])
        copy.start()
        copy.wait()

    @pl.when(tm > 0)
    def _():
        for h, part in enumerate(parts[0]):
            if h < 2:
                part[...] = from_earlier[:, h]
            elif h < frames:
                part[...] = from_own[:, h - 2] + from_earlier[:, h]
            else:
                part[...] = from_own[:, h - 2]
        copies = [
            pltpu.make_async_copy(result.at[f], out.at[f], sems.at[f]) for f in range(frames)
        ]
        finish(
            bands, count, own, (above, below), (far_above, far_below), bias, weight, gain_two,
            bias_two, weight_two, mixed_two, result, *parts, lambda f: copies[f].start(),
        )
        for copy in copies:
            copy.wait()


def shards(latents, counts, gain_first, bias_first, weight_first, gain_second, bias_second, weight_second):
    channels = gain_first.shape[0]
    frames, rows, flat = latents.shape[1:]
    wide = 2 * channels
    pairs = flat // wide
    blocks, bands = lax.axis_size("tm"), lax.axis_size("space")
    block = latents.reshape(frames, rows, flat)

    def shift(sent, step, along):
        pairs_of = [
            (t * bands + s, (t + along) % blocks * bands + (s + step * (t + along < blocks)) % bands)
            for t in range(blocks)
            for s in range(bands)
        ]
        return lax.ppermute(sent, ("tm", "space"), pairs_of)

    vmem = pl.BlockSpec(memory_space=pltpu.VMEM)
    smem = pl.BlockSpec(memory_space=pltpu.SMEM)
    params = pltpu.CompilerParams(vmem_limit_bytes=24 << 20)
    swap = bands == 2
    rims = 1 if swap else 2
    rim = jax.ShapeDtypeStruct((frames, 2, pairs, wide), BF16)
    stages = [pltpu.VMEM((3, 2 * rows * pairs, LANES), F32)] * (frames // 2)
    mask = pl.pallas_call(
        functools.partial(mask_kernel, channels),
        out_shape=jax.ShapeDtypeStruct((2 * rows, wide), F32),
        out_specs=vmem,
        compiler_params=params,
        cost_estimate=pl.CostEstimate(flops=4 << 30, bytes_accessed=1 << 16, transcendentals=0),
        name="lane_mask",
    )()
    normed, *sent = pl.pallas_call(
        functools.partial(norm_kernel, swap),
        out_shape=[jax.ShapeDtypeStruct((frames, rows, pairs, wide), BF16)] + [rim] * rims,
        in_specs=[vmem] * 3,
        out_specs=[vmem] * (1 + rims),
        scratch_shapes=stages,
        compiler_params=params,
        cost_estimate=pl.CostEstimate(flops=4 << 30, bytes_accessed=1 << 20, transcendentals=0),
        name="norm_and_cut",
    )(mask, block, gain_first.reshape(1, channels))
    earlier = shift(block, 0, 1)
    if swap:
        near = (shift(sent[0], 1, 0),) * 2
        far = (shift(sent[0], 1, 1),) * 2
        deep = rows + 1
    else:
        near = (shift(sent[0], 1, 0), shift(sent[1], -1, 0))
        far = (shift(sent[0], 1, 1), shift(sent[1], -1, 1))
        deep = rows + 2

    first_weight = weight_first.reshape(3, 3, 3 * channels, channels)
    second_weight = weight_second.reshape(3, 3, 3 * channels, channels)
    share = (2, frames, deep, pairs, channels)
    window = [pltpu.VMEM((deep + 2, pairs, wide), BF16)] * (frames + 1)
    cost = pl.CostEstimate(flops=1 << 20, bytes_accessed=1 << 16, transcendentals=0)
    taps = jax.ShapeDtypeStruct((2, *first_weight.shape[1:]), BF16)
    from_own, mixed_two = pl.pallas_call(
        functools.partial(own_kernel, bands, deep),
        out_shape=[jax.ShapeDtypeStruct(share, F32), taps],
        in_specs=[smem] + [vmem] * 6,
        out_specs=[vmem] * 2,
        scratch_shapes=window,
        compiler_params=params,
        cost_estimate=cost,
        name="conv_one_own",
    )(
        counts, normed, first_weight, second_weight, gain_second.reshape(1, channels),
        bias_first.reshape(1, channels), bias_second.reshape(1, channels),
    )
    constants = (
        bias_first.reshape(1, channels), first_weight,
        gain_second.reshape(1, channels), bias_second.reshape(1, channels), second_weight,
    )
    result = jax.ShapeDtypeStruct((frames, rows, flat), BF16)
    scratch = (
        [pltpu.VMEM((2, deep, pairs, channels), F32)] * (frames + 2)
        + [pltpu.VMEM((rows + 2, pairs, wide), BF16)] * (frames + 2 + 2 * frames)
        + [pltpu.VMEM((3, frames // 2 * rows * pairs, LANES), F32)] * 2
    )
    first_out = pl.pallas_call(
        functools.partial(first_block_kernel, bands),
        out_shape=result,
        in_specs=[smem] + [vmem] * 10,
        out_specs=vmem,
        scratch_shapes=scratch,
        compiler_params=params,
        cost_estimate=cost,
        name="first_block",
    )(counts, block, *near, from_own, mixed_two, *constants)
    from_earlier = pl.pallas_call(
        functools.partial(earlier_kernel, bands, deep),
        out_shape=jax.ShapeDtypeStruct(share, F32),
        in_specs=[smem] + [vmem] * 5,
        out_specs=vmem,
        scratch_shapes=window + stages,
        compiler_params=params,
        cost_estimate=cost,
        name="conv_one_earlier",
    )(counts, mask, earlier, gain_first.reshape(1, channels), first_weight, first_out)
    out = pl.pallas_call(
        functools.partial(last_kernel, bands),
        out_shape=result,
        in_specs=[smem] + [vmem] * 14,
        out_specs=pl.BlockSpec(memory_space=pl.ANY),
        scratch_shapes=[
            pltpu.VMEM((frames, rows, flat), BF16), pltpu.SemaphoreType.DMA((frames,))
        ] + scratch,
        compiler_params=params,
        cost_estimate=pl.CostEstimate(flops=4 << 30, bytes_accessed=6 << 20, transcendentals=0),
        name="last",
    )(counts, block, *near, *far, from_own, from_earlier, first_out, mixed_two, *constants)
    return out.reshape(1, frames, rows, flat)


def solution(mesh):
    spread = P(("groups", "clip"), "tm", "space", None)
    return jax.shard_map(
        shards,
        mesh=mesh,
        in_specs=(spread, P(("groups", "clip")), P(), P(), P(), P(), P(), P()),
        out_specs=spread,
        check_vma=False,
    )
```

```python
import functools

import jax
import jax.numpy as jnp
from jax import lax
from jax.experimental import pallas as pl
from jax.experimental.pallas import tpu as pltpu
from jax.sharding import PartitionSpec as P

F32 = jnp.float32
BF16 = jnp.bfloat16
LANES = 128


def mask_kernel(channels, mask):
    lane = lax.broadcasted_iota(jnp.int32, mask.shape, 1)
    mask[...] = jnp.where(lane < channels, 1.0, 0.0)


def norm_silu_pair(t, gain, first, channels):
    square = t * t
    left = jnp.sum(jnp.where(first, square, 0.0), axis=1, keepdims=True)
    right = jnp.sum(jnp.where(first, 0.0, square), axis=1, keepdims=True)
    left = lax.rsqrt(left * (1.0 / channels) + 1e-06)
    right = lax.rsqrt(right * (1.0 / channels) + 1e-06)
    y = t * jnp.where(first, left, right) * gain
    return y * (0.5 + 0.5 * jnp.tanh(0.5 * y))


def twice(ref):
    return jnp.concatenate([ref[...], ref[...]], axis=1)


def norm_frames(block, f, gain_wide, first, stage, store, pairs):
    rows = block.shape[1]
    wide = gain_wide.shape[1]
    for p in range(pairs):
        lanes = pl.ds(p * wide, wide)
        t = jnp.concatenate([block[f + n, :, lanes].astype(F32) for n in range(2)], axis=0)
        y = norm_silu_pair(t, gain_wide, first, wide // 2)
        for k in range(3):
            stage[k, pl.ds(p, 2 * rows, stride=pairs), :] = y[:, k * LANES : (k + 1) * LANES]
    for n in range(2):
        for r in range(rows):
            at = pl.ds((n * rows + r) * pairs, pairs)
            store(f + n, r, [stage[k, at, :].astype(BF16) for k in range(3)])


def norm_kernel(swap, mask, block, gain, normed, *rest):
    frames, rows, pairs, _ = normed.shape
    sent, stages = rest[: -(frames // 2)], rest[-(frames // 2) :]

    def store(f, r, parts):
        for k in range(3):
            normed[f, r, :, k * LANES : (k + 1) * LANES] = parts[k]

    for f in range(0, frames, 2):
        norm_frames(block, f, twice(gain), mask[...] > 0.5, stages[f // 2], store, pairs)
    if swap:
        first = (rows - 2) * (1 - lax.axis_index("space"))
        sent[0][...] = normed[:, pl.ds(first, 2)]
    else:
        sent[0][...] = normed[:, rows - 2 :]
        sent[1][...] = normed[:, :2]


def dot(left, right):
    return jnp.dot(
        jnp.concatenate(left, axis=1), jnp.concatenate(right, axis=0), preferred_element_type=F32
    )


def products(parts, rims, channels):
    lead = jnp.zeros((2 * LANES - channels, channels), BF16)
    mine = (
        dot(parts, [w[channels:] for w in rims]),
        dot(parts, [w[: 2 * channels] for w in rims]),
    )
    high = [x[:, LANES:] for x in parts]
    low = [x[:, : 2 * LANES] for x in parts]
    moved = (
        dot(high, [x for w in rims for x in (lead, w[:channels])]),
        dot(low, [x for w in rims for x in (w[2 * channels :], lead)]),
    )
    return mine, moved


def conv(window, weight, source, frames, rows, times, channels):
    pairs, wide = window[0].shape[1:]
    taps = [(a, b) for a in times for b in range(3)]

    def patch(a, b):
        at = source + a - times[0]
        rows_of = [window[f][b : b + rows].reshape(rows * pairs, wide) for f in range(at, at + frames)]
        return jnp.concatenate(rows_of, axis=0)

    parts = [patch(a, b) for a, b in taps]
    return add_moved(*products(parts, [weight[a, b] for a, b in taps], channels), pairs)


def mix_weights(weight, mixed):
    for b in range(3):
        outer = weight[0, b] + weight[2, b]
        mixed[0, b] = outer + weight[1, b]
        mixed[1, b] = outer - weight[1, b]


def mix(frames, i, out):
    if i == 1:
        out[...] = (frames[1][...] + frames[2][...]) * -0.5
    elif i == 2:
        out[...] = (frames[1][...] - frames[2][...]) * 0.5
    else:
        one, other = (0, 2) if i == 0 else (1, 3)
        out[...] = frames[one][...] - frames[other][...]


def mixed_product(mixed, taps, rows, channels):
    pairs, wide = mixed[0].shape[1:]
    parts = [
        jnp.concatenate([m[b : b + rows].reshape(rows * pairs, wide) for m in mixed], axis=0)
        for b in range(3)
    ]
    mine, moved = products(parts, taps, channels)
    return [*mine, *moved]


def add_moved(mine, moved, pairs):
    place = lax.broadcasted_iota(jnp.int32, mine[0].shape, 0) % pairs
    count = mine[0].shape[0]
    left = jnp.where(place == 0, 0.0, pltpu.roll(moved[0], 1, 0))
    right = jnp.where(place == pairs - 1, 0.0, pltpu.roll(moved[1], count - 1, 0))
    return mine[0] + left, mine[1] + right


def own_kernel(
    bands, deep, count, normed, weight, weight_two, gain_two, bias, bias_two, total, mixed_two, *window
):
    frames, rows, pairs, wide = normed.shape
    tm, space = lax.axis_index("tm"), lax.axis_index("space")
    nothing = jnp.zeros((pairs, wide), BF16)
    top = clear_rims(window[1:], bands, space, rows)
    window[0][...] = jnp.zeros(window[0].shape, BF16)
    for f in range(frames):
        good = tm * frames + f < count[0]
        for r in range(rows):
            window[f + 1][top + r] = jnp.where(good, normed[f, r], nothing)
    late = conv(window, weight, 1, frames - 2, deep, (0, 1, 2), wide // 2)
    soon = conv(window, weight, 0, 2, deep, (1, 2), wide // 2)
    mix_weights(weight_two, mixed_two)
    for q in range(2):
        total[q, 0:2] = soon[q].reshape(2, *total.shape[2:])
        total[q, 2:] = late[q].reshape(frames - 2, *total.shape[2:])


def clear_rims(window, bands, space, rows):
    for part in window:
        nothing = jnp.zeros(part.shape[1:], BF16)
        if bands == 2:
            part[(rows + 2) * space] = nothing
            for r in range(2):
                part[(rows + 1) * (1 - space) + r] = nothing
        else:
            for r in range(2):
                part[r] = nothing
                part[rows + 2 + r] = nothing
    return 1 + space if bands == 2 else 2


def earlier_kernel(bands, deep, count, mask, earlier, gain, weight, after, total, *scratch):
    frames, rows = earlier.shape[0], earlier.shape[1]
    window, stages = scratch[: frames + 1], scratch[frames + 1 :]
    pairs, wide = window[0].shape[1:]
    tm, space = lax.axis_index("tm"), lax.axis_index("space")

    @pl.when(tm > 0)
    def _():
        top = clear_rims(window[:frames], bands, space, rows)
        window[frames][...] = jnp.zeros(window[frames].shape, BF16)

        def store(f, r, parts):
            good = (tm - 1) * frames + f < count[0]
            for k in range(3):
                part = jnp.where(good, parts[k], jnp.zeros_like(parts[k]))
                window[f][top + r, :, k * LANES : (k + 1) * LANES] = part

        def norm(f):
            norm_frames(earlier, f, twice(gain), mask[...] > 0.5, stages[f // 2], store, pairs)

        norm(frames - 2)
        late = conv(window, weight, frames - 2, 2, deep, (0, 1), wide // 2)
        for f in range(0, frames - 2, 2):
            norm(f)
        for q in range(2):
            total[q, frames - 2 :] = late[q].reshape(2, *total.shape[2:])
        soon = conv(window, weight, 0, frames - 2, deep, (0, 1, 2), wide // 2)
        for q in range(2):
            total[q, 0 : frames - 2] = soon[q].reshape(frames - 2, *total.shape[2:])


def rim_sums(near, far, weight, side, keep, channels, frames):
    pairs, wide = near.shape[2], near.shape[3]
    nothing = jnp.zeros((pairs, wide), BF16)

    def row(f, r):
        ref, at = (far, f) if f < frames else (near, f - frames)
        return jnp.where(keep(f), ref[at, r], nothing)

    span = frames + 2
    rows = [[row(f, r) for r in range(2)] for f in range(2 * frames)]
    inner = [row(f, 1 - side) for f in range(2 * frames)]
    parts = [
        jnp.concatenate([x for f in range(span) for x in rows[f + a]], axis=0) for a in range(3)
    ]
    both = add_moved(*products(parts, [weight[a, 2 * side] for a in range(3)], channels), pairs)
    parts = [jnp.concatenate([inner[f + a] for f in range(span)], axis=0) for a in range(3)]
    outer = add_moved(*products(parts, [weight[a, 1] for a in range(3)], channels), pairs)
    tall = 2 * pairs
    halo = lax.broadcasted_iota(jnp.int32, (tall, channels), 0) // pairs == side

    def at(q, h):
        one = outer[q][h * pairs : (h + 1) * pairs]
        one = jnp.where(halo, jnp.concatenate([one, one], axis=0), 0.0)
        return both[q][h * tall : (h + 1) * tall] + one

    return at


def finish(bands, count, own, near, far, bias, weight, gain_two, bias_two, weight_two, mixed_two, out, deep, sums_at, hidden, mixed, final, ready):
    frames, rows, pairs, wide = near[0].shape[0], own.shape[1], near[0].shape[2], near[0].shape[3]
    channels = wide // 2
    tm, space = lax.axis_index("tm"), lax.axis_index("space")

    def valid(f):
        at = (tm - 1) * frames + f
        return (at >= 0) & (at < count[0])

    start = (1 - space) if bands == 2 else 0
    if bands == 2:
        sides = [(near[0], far[0], 1 - space, valid)]
        first, deep_inner = 2 * space, deep - 2
    else:
        sides = [
            (near[0], far[0], 0, lambda f: valid(f) & (space > 0)),
            (near[1], far[1], 1, lambda f: valid(f) & (space < bands - 1)),
        ]
        first, deep_inner = 2, deep - 4
    bias_wide, gain_wide = twice(bias), twice(gain_two)

    def norm_rows(h, sums, base):
        t = jnp.concatenate(sums, axis=1)
        number = t.shape[0] // pairs
        row = lax.broadcasted_iota(jnp.int32, (t.shape[0], 1), 0) // pairs
        row = row + (space * rows - 1 + start + base)
        good = (row >= 0) & (row < bands * rows) & valid(frames + h - 2)
        t = jnp.where(good, t + bias_wide, 0.0).astype(BF16).astype(F32)
        lanes = lax.broadcasted_iota(jnp.int32, t.shape, 1) < channels
        y = norm_silu_pair(t, gain_wide, lanes, channels).astype(BF16)
        for r in range(number):
            hidden[h][start + base + r] = y[r * pairs : (r + 1) * pairs]

    def rows_of(h, q, base, number):
        return sums_at(h, q, pl.ds(base, number)).reshape(number * pairs, channels)

    def norm_rims(h):
        for (_, _, side, _), sums in zip(sides, added):
            low = (deep - 2) * side
            norm_rows(h, [rows_of(h, q, low, 2) + sums(q, h) for q in range(2)], low)

    def product(i):
        for n in range(half):
            mix(hidden[2 * n : 2 * n + 4], i, mixed[half * i + n])
        taps = [(weight_two[0, b], mixed_two[0, b], mixed_two[1, b], weight_two[2, b])[i] for b in range(3)]
        return mixed_product(mixed[half * i : half * (i + 1)], taps, rows, channels)

    def emit(n, result):
        both = add_moved(result[:2], result[2:], pairs)
        both = jnp.concatenate(both, axis=1) + bias_two_wide
        for k in range(3):
            final[n][k] = both[:, k * LANES : (k + 1) * LANES]
        for m in range(0, half, 2):
            good = [valid(frames + n + 2 * (m + j)) for j in range(2)]
            for p in range(pairs):
                for k in range(3):
                    at = pl.ds(m * rows * pairs + p, 2 * rows, stride=pairs)
                    block = final[n][k, at, :]
                    lanes = pl.ds(p * wide + k * LANES, LANES)
                    for j in range(2):
                        f = n + 2 * (m + j)
                        value = own[f, :, lanes].astype(F32) + block[j * rows : (j + 1) * rows]
                        out[f, :, lanes] = jnp.where(good[j], value, 0.0).astype(BF16)
        for m in range(half):
            ready(n + 2 * m)

    half = frames // 2
    bias_two_wide = twice(bias_two)
    added = [rim_sums(n, f, weight, side, keep, channels, frames) for n, f, side, keep in sides]
    for h in range(frames + 2):
        hidden[h][0] = jnp.zeros((pairs, wide), BF16)
        hidden[h][rows + 1] = jnp.zeros((pairs, wide), BF16)
        norm_rows(h, [rows_of(h, q, first, deep_inner) for q in range(2)], first)
    for h in range(1, frames + 1):
        norm_rims(h)
    one = product(1)
    two = product(2)
    norm_rims(0)
    zero = product(0)
    norm_rims(frames + 1)
    emit(0, [x - y - z for x, y, z in zip(zero, one, two)])
    three = product(3)
    emit(1, [z - y - x for x, y, z in zip(three, one, two)])


def first_block_kernel(
    bands, count, own, above, below, from_own, mixed_two, bias, weight, gain_two, bias_two,
    weight_two, out, *scratch,
):
    parts = split(scratch, own.shape[0])

    @pl.when(lax.axis_index("tm") == 0)
    def _():
        def sums_at(h, q, rows):
            value = from_own[q, max(h - 2, 0), rows]
            return value if h >= 2 else jnp.zeros_like(value)

        near = (above, below)
        finish(
            bands, count, own, near, near, bias, weight, gain_two, bias_two, weight_two,
            mixed_two, out, from_own.shape[2], sums_at, *parts, lambda f: None,
        )


def split(scratch, frames):
    rest = scratch[frames + 2 :]
    return scratch[: frames + 2], rest[: 2 * frames], rest[2 * frames :]


def last_kernel(
    bands, count, own, above, below, far_above, far_below, from_own, from_earlier, first_out,
    mixed_two, bias, weight, gain_two, bias_two, weight_two, out, result, sems, *scratch,
):
    frames = own.shape[0]
    parts = split(scratch, frames)
    tm = lax.axis_index("tm")

    @pl.when(tm == 0)
    def _():
        copy = pltpu.make_async_copy(first_out, out, sems.at[0])
        copy.start()
        copy.wait()

    @pl.when(tm > 0)
    def _():
        def sums_at(h, q, rows):
            if h < 2:
                return from_earlier[q, h, rows]
            if h < frames:
                return from_own[q, h - 2, rows] + from_earlier[q, h, rows]
            return from_own[q, h - 2, rows]

        copies = [
            pltpu.make_async_copy(result.at[f], out.at[f], sems.at[f]) for f in range(frames)
        ]
        finish(
            bands, count, own, (above, below), (far_above, far_below), bias, weight, gain_two,
            bias_two, weight_two, mixed_two, result, from_own.shape[2], sums_at, *parts,
            lambda f: copies[f].start(),
        )
        for copy in copies:
            copy.wait()


def shards(latents, counts, gain_first, bias_first, weight_first, gain_second, bias_second, weight_second):
    channels = gain_first.shape[0]
    frames, rows, flat = latents.shape[1:]
    wide = 2 * channels
    pairs = flat // wide
    blocks, bands = lax.axis_size("tm"), lax.axis_size("space")
    block = latents.reshape(frames, rows, flat)

    def shift(sent, step, along):
        pairs_of = [
            (t * bands + s, (t + along) % blocks * bands + (s + step * (t + along < blocks)) % bands)
            for t in range(blocks)
            for s in range(bands)
        ]
        return lax.ppermute(sent, ("tm", "space"), pairs_of)

    vmem = pl.BlockSpec(memory_space=pltpu.VMEM)
    smem = pl.BlockSpec(memory_space=pltpu.SMEM)
    params = pltpu.CompilerParams(vmem_limit_bytes=24 << 20)
    swap = bands == 2
    rims = 1 if swap else 2
    rim = jax.ShapeDtypeStruct((frames, 2, pairs, wide), BF16)
    stages = [pltpu.VMEM((3, 2 * rows * pairs, LANES), F32)] * (frames // 2)
    mask = pl.pallas_call(
        functools.partial(mask_kernel, channels),
        out_shape=jax.ShapeDtypeStruct((2 * rows, wide), F32),
        out_specs=vmem,
        compiler_params=params,
        cost_estimate=pl.CostEstimate(flops=4 << 30, bytes_accessed=1 << 16, transcendentals=0),
        name="lane_mask",
    )()
    normed, *sent = pl.pallas_call(
        functools.partial(norm_kernel, swap),
        out_shape=[jax.ShapeDtypeStruct((frames, rows, pairs, wide), BF16)] + [rim] * rims,
        in_specs=[vmem] * 3,
        out_specs=[vmem] * (1 + rims),
        scratch_shapes=stages,
        compiler_params=params,
        cost_estimate=pl.CostEstimate(flops=4 << 30, bytes_accessed=1 << 20, transcendentals=0),
        name="norm_and_cut",
    )(mask, block, gain_first.reshape(1, channels))
    earlier = shift(block, 0, 1)
    if swap:
        near = (shift(sent[0], 1, 0),) * 2
        far = (shift(sent[0], 1, 1),) * 2
        deep = rows + 1
    else:
        near = (shift(sent[0], 1, 0), shift(sent[1], -1, 0))
        far = (shift(sent[0], 1, 1), shift(sent[1], -1, 1))
        deep = rows + 2

    first_weight = weight_first.reshape(3, 3, 3 * channels, channels)
    second_weight = weight_second.reshape(3, 3, 3 * channels, channels)
    share = (2, frames, deep, pairs, channels)
    window = [pltpu.VMEM((deep + 2, pairs, wide), BF16)] * (frames + 1)
    cost = pl.CostEstimate(flops=1 << 20, bytes_accessed=1 << 16, transcendentals=0)
    taps = jax.ShapeDtypeStruct((2, *first_weight.shape[1:]), BF16)
    from_own, mixed_two = pl.pallas_call(
        functools.partial(own_kernel, bands, deep),
        out_shape=[jax.ShapeDtypeStruct(share, F32), taps],
        in_specs=[smem] + [vmem] * 6,
        out_specs=[vmem] * 2,
        scratch_shapes=window,
        compiler_params=params,
        cost_estimate=cost,
        name="conv_one_own",
    )(
        counts, normed, first_weight, second_weight, gain_second.reshape(1, channels),
        bias_first.reshape(1, channels), bias_second.reshape(1, channels),
    )
    constants = (
        bias_first.reshape(1, channels), first_weight,
        gain_second.reshape(1, channels), bias_second.reshape(1, channels), second_weight,
    )
    result = jax.ShapeDtypeStruct((frames, rows, flat), BF16)
    scratch = (
        [pltpu.VMEM((rows + 2, pairs, wide), BF16)] * (frames + 2 + 2 * frames)
        + [pltpu.VMEM((3, frames // 2 * rows * pairs, LANES), F32)] * 2
    )
    first_out = pl.pallas_call(
        functools.partial(first_block_kernel, bands),
        out_shape=result,
        in_specs=[smem] + [vmem] * 10,
        out_specs=vmem,
        scratch_shapes=scratch,
        compiler_params=params,
        cost_estimate=cost,
        name="first_block",
    )(counts, block, *near, from_own, mixed_two, *constants)
    from_earlier = pl.pallas_call(
        functools.partial(earlier_kernel, bands, deep),
        out_shape=jax.ShapeDtypeStruct(share, F32),
        in_specs=[smem] + [vmem] * 5,
        out_specs=vmem,
        scratch_shapes=window + stages,
        compiler_params=params,
        cost_estimate=cost,
        name="conv_one_earlier",
    )(counts, mask, earlier, gain_first.reshape(1, channels), first_weight, first_out)
    out = pl.pallas_call(
        functools.partial(last_kernel, bands),
        out_shape=result,
        in_specs=[smem] + [vmem] * 14,
        out_specs=pl.BlockSpec(memory_space=pl.ANY),
        scratch_shapes=[
            pltpu.VMEM((frames, rows, flat), BF16), pltpu.SemaphoreType.DMA((frames,))
        ] + scratch,
        compiler_params=params,
        cost_estimate=pl.CostEstimate(flops=4 << 30, bytes_accessed=6 << 20, transcendentals=0),
        name="last",
    )(counts, block, *near, *far, from_own, from_earlier, first_out, mixed_two, *constants)
    return out.reshape(1, frames, rows, flat)


def solution(mesh):
    spread = P(("groups", "clip"), "tm", "space", None)
    return jax.shard_map(
        shards,
        mesh=mesh,
        in_specs=(spread, P(("groups", "clip")), P(), P(), P(), P(), P(), P()),
        out_specs=spread,
        check_vma=False,
    )
```

```python
import functools

import jax
import jax.numpy as jnp
from jax import lax
from jax.experimental import pallas as pl
from jax.experimental.pallas import tpu as pltpu
from jax.sharding import PartitionSpec as P

F32 = jnp.float32
BF16 = jnp.bfloat16
LANES = 128


def mask_kernel(channels, mask):
    lane = lax.broadcasted_iota(jnp.int32, mask.shape, 1)
    mask[...] = jnp.where(lane < channels - LANES, 1.0, 0.0)


def norm_silu_pair(t, half_gain, middle, channels):
    tiles = [t[:, k * LANES : (k + 1) * LANES] for k in range(3)]
    square = [tile * tile for tile in tiles]
    left = square[0] + jnp.where(middle, square[1], 0.0)
    right = square[2] + jnp.where(middle, 0.0, square[1])
    left, right = [
        lax.rsqrt(jnp.sum(x, axis=1, keepdims=True) * (1.0 / channels) + 1e-06)
        for x in (left, right)
    ]
    results = []
    for k, scale in enumerate((left, jnp.where(middle, left, right), right)):
        h = tiles[k] * scale * half_gain[:, k * LANES : (k + 1) * LANES]
        results.append(h + h * jnp.tanh(h))
    return jnp.concatenate(results, axis=1)


def twice(ref):
    return jnp.concatenate([ref[...], ref[...]], axis=1)


def norm_frames(block, f, gain_wide, first, stage, store, pairs):
    rows = block.shape[1]
    wide = gain_wide.shape[1]
    for p in range(pairs):
        lanes = pl.ds(p * wide, wide)
        t = jnp.concatenate([block[f + n, :, lanes].astype(F32) for n in range(2)], axis=0)
        y = norm_silu_pair(t, gain_wide, first, wide // 2)
        for k in range(3):
            stage[k, pl.ds(p, 2 * rows, stride=pairs), :] = y[:, k * LANES : (k + 1) * LANES]
    for n in range(2):
        for r in range(rows):
            at = pl.ds((n * rows + r) * pairs, pairs)
            store(f + n, r, [stage[k, at, :].astype(BF16) for k in range(3)])


def norm_kernel(swap, mask, block, gain, normed, *rest):
    frames, rows, pairs, _ = normed.shape
    sent, stages = rest[: -(frames // 2)], rest[-(frames // 2) :]

    def store(f, r, parts):
        for k in range(3):
            normed[f, r, :, k * LANES : (k + 1) * LANES] = parts[k]

    for f in range(0, frames, 2):
        norm_frames(block, f, twice(gain) * 0.5, mask[...] > 0.5, stages[f // 2], store, pairs)
    if swap:
        first = (rows - 2) * (1 - lax.axis_index("space"))
        sent[0][...] = normed[:, pl.ds(first, 2)]
    else:
        sent[0][...] = normed[:, rows - 2 :]
        sent[1][...] = normed[:, :2]


def dot(left, right):
    return jnp.dot(
        jnp.concatenate(left, axis=1), jnp.concatenate(right, axis=0), preferred_element_type=F32
    )


def products(parts, rims, channels):
    lead = jnp.zeros((2 * LANES - channels, channels), BF16)
    mine = (
        dot(parts, [w[channels:] for w in rims]),
        dot(parts, [w[: 2 * channels] for w in rims]),
    )
    high = [x[:, LANES:] for x in parts]
    low = [x[:, : 2 * LANES] for x in parts]
    moved = (
        dot(high, [x for w in rims for x in (lead, w[:channels])]),
        dot(low, [x for w in rims for x in (w[2 * channels :], lead)]),
    )
    return mine, moved


def conv(window, weight, source, frames, rows, times, channels):
    pairs, wide = window[0].shape[1:]
    taps = [(a, b) for a in times for b in range(3)]

    def patch(a, b):
        at = source + a - times[0]
        rows_of = [window[f][b : b + rows].reshape(rows * pairs, wide) for f in range(at, at + frames)]
        return jnp.concatenate(rows_of, axis=0)

    parts = [patch(a, b) for a, b in taps]
    return add_moved(*products(parts, [weight[a, b] for a, b in taps], channels), pairs)


def mix_weights(weight, mixed):
    for b in range(3):
        outer = weight[0, b] + weight[2, b]
        mixed[0, b] = outer + weight[1, b]
        mixed[1, b] = outer - weight[1, b]


def mix(frames, i, out):
    if i == 1:
        out[...] = (frames[1][...] + frames[2][...]) * -0.5
    elif i == 2:
        out[...] = (frames[1][...] - frames[2][...]) * 0.5
    else:
        one, other = (0, 2) if i == 0 else (1, 3)
        out[...] = frames[one][...] - frames[other][...]


def mixed_product(mixed, taps, rows, channels):
    pairs, wide = mixed[0].shape[1:]
    parts = [
        jnp.concatenate([m[b : b + rows].reshape(rows * pairs, wide) for m in mixed], axis=0)
        for b in range(3)
    ]
    mine, moved = products(parts, taps, channels)
    return [*mine, *moved]


def add_moved(mine, moved, pairs):
    place = lax.broadcasted_iota(jnp.int32, mine[0].shape, 0) % pairs
    count = mine[0].shape[0]
    left = jnp.where(place == 0, 0.0, pltpu.roll(moved[0], 1, 0))
    right = jnp.where(place == pairs - 1, 0.0, pltpu.roll(moved[1], count - 1, 0))
    return mine[0] + left, mine[1] + right


def own_kernel(
    bands, deep, count, normed, weight, weight_two, gain_two, bias, bias_two, total, mixed_two, *window
):
    frames, rows, pairs, wide = normed.shape
    tm, space = lax.axis_index("tm"), lax.axis_index("space")
    nothing = jnp.zeros((pairs, wide), BF16)
    top = clear_rims(window[1:], bands, space, rows)
    window[0][...] = jnp.zeros(window[0].shape, BF16)
    for f in range(frames):
        good = tm * frames + f < count[0]
        for r in range(rows):
            window[f + 1][top + r] = jnp.where(good, normed[f, r], nothing)
    late = conv(window, weight, 1, frames - 2, deep, (0, 1, 2), wide // 2)
    soon = conv(window, weight, 0, 2, deep, (1, 2), wide // 2)
    mix_weights(weight_two, mixed_two)
    for q in range(2):
        total[q, 0:2] = soon[q].reshape(2, *total.shape[2:])
        total[q, 2:] = late[q].reshape(frames - 2, *total.shape[2:])


def clear_rims(window, bands, space, rows):
    for part in window:
        nothing = jnp.zeros(part.shape[1:], BF16)
        if bands == 2:
            part[(rows + 2) * space] = nothing
            for r in range(2):
                part[(rows + 1) * (1 - space) + r] = nothing
        else:
            for r in range(2):
                part[r] = nothing
                part[rows + 2 + r] = nothing
    return 1 + space if bands == 2 else 2


def earlier_kernel(bands, deep, count, mask, earlier, gain, weight, after, total, *scratch):
    frames, rows = earlier.shape[0], earlier.shape[1]
    window, stages = scratch[: frames + 1], scratch[frames + 1 :]
    pairs, wide = window[0].shape[1:]
    tm, space = lax.axis_index("tm"), lax.axis_index("space")

    @pl.when(tm > 0)
    def _():
        top = clear_rims(window[:frames], bands, space, rows)
        window[frames][...] = jnp.zeros(window[frames].shape, BF16)

        def store(f, r, parts):
            good = (tm - 1) * frames + f < count[0]
            for k in range(3):
                part = jnp.where(good, parts[k], jnp.zeros_like(parts[k]))
                window[f][top + r, :, k * LANES : (k + 1) * LANES] = part

        def norm(f):
            norm_frames(earlier, f, twice(gain) * 0.5, mask[...] > 0.5, stages[f // 2], store, pairs)

        norm(frames - 2)
        late = conv(window, weight, frames - 2, 2, deep, (0, 1), wide // 2)
        for f in range(0, frames - 2, 2):
            norm(f)
        for q in range(2):
            total[q, frames - 2 :] = late[q].reshape(2, *total.shape[2:])
        soon = conv(window, weight, 0, frames - 2, deep, (0, 1, 2), wide // 2)
        for q in range(2):
            total[q, 0 : frames - 2] = soon[q].reshape(frames - 2, *total.shape[2:])


def rim_sums(near, far, weight, side, keep, channels, frames):
    pairs, wide = near.shape[2], near.shape[3]
    nothing = jnp.zeros((pairs, wide), BF16)

    def row(f, r):
        ref, at = (far, f) if f < frames else (near, f - frames)
        return jnp.where(keep(f), ref[at, r], nothing)

    span = frames + 2
    rows = [[row(f, r) for r in range(2)] for f in range(2 * frames)]
    inner = [row(f, 1 - side) for f in range(2 * frames)]
    parts = [
        jnp.concatenate([x for f in range(span) for x in rows[f + a]], axis=0) for a in range(3)
    ]
    both = add_moved(*products(parts, [weight[a, 2 * side] for a in range(3)], channels), pairs)
    parts = [jnp.concatenate([inner[f + a] for f in range(span)], axis=0) for a in range(3)]
    outer = add_moved(*products(parts, [weight[a, 1] for a in range(3)], channels), pairs)
    tall = 2 * pairs
    halo = lax.broadcasted_iota(jnp.int32, (tall, channels), 0) // pairs == side

    def at(q, h):
        one = outer[q][h * pairs : (h + 1) * pairs]
        one = jnp.where(halo, jnp.concatenate([one, one], axis=0), 0.0)
        return both[q][h * tall : (h + 1) * tall] + one

    return at


def finish(bands, count, own, near, far, bias, weight, gain_two, bias_two, weight_two, mixed_two, out, deep, sums_at, hidden, mixed, final, ready):
    frames, rows, pairs, wide = near[0].shape[0], own.shape[1], near[0].shape[2], near[0].shape[3]
    channels = wide // 2
    tm, space = lax.axis_index("tm"), lax.axis_index("space")

    def valid(f):
        at = (tm - 1) * frames + f
        return (at >= 0) & (at < count[0])

    start = (1 - space) if bands == 2 else 0
    if bands == 2:
        sides = [(near[0], far[0], 1 - space, valid)]
        first, deep_inner = 2 * space, deep - 2
    else:
        sides = [
            (near[0], far[0], 0, lambda f: valid(f) & (space > 0)),
            (near[1], far[1], 1, lambda f: valid(f) & (space < bands - 1)),
        ]
        first, deep_inner = 2, deep - 4
    bias_wide, gain_wide = twice(bias), twice(gain_two) * 0.5

    def norm_rows(h, sums, base):
        t = jnp.concatenate(sums, axis=1)
        number = t.shape[0] // pairs
        row = lax.broadcasted_iota(jnp.int32, (t.shape[0], 1), 0) // pairs
        row = row + (space * rows - 1 + start + base)
        good = (row >= 0) & (row < bands * rows) & valid(frames + h - 2)
        t = jnp.where(good, t + bias_wide, 0.0).astype(BF16).astype(F32)
        middle = lax.broadcasted_iota(jnp.int32, (t.shape[0], LANES), 1) < channels - LANES
        y = norm_silu_pair(t, gain_wide, middle, channels).astype(BF16)
        for r in range(number):
            hidden[h][start + base + r] = y[r * pairs : (r + 1) * pairs]

    def rows_of(h, q, base, number):
        return sums_at(h, q, pl.ds(base, number)).reshape(number * pairs, channels)

    def norm_rims(h):
        for (_, _, side, _), sums in zip(sides, added):
            low = (deep - 2) * side
            norm_rows(h, [rows_of(h, q, low, 2) + sums(q, h) for q in range(2)], low)

    def product(i):
        for n in range(half):
            mix(hidden[2 * n : 2 * n + 4], i, mixed[half * i + n])
        taps = [(weight_two[0, b], mixed_two[0, b], mixed_two[1, b], weight_two[2, b])[i] for b in range(3)]
        return mixed_product(mixed[half * i : half * (i + 1)], taps, rows, channels)

    def emit(n, result):
        both = add_moved(result[:2], result[2:], pairs)
        both = jnp.concatenate(both, axis=1) + bias_two_wide
        for k in range(3):
            final[n][k] = both[:, k * LANES : (k + 1) * LANES]
        for m in range(0, half, 2):
            good = [valid(frames + n + 2 * (m + j)) for j in range(2)]
            for p in range(pairs):
                for k in range(3):
                    at = pl.ds(m * rows * pairs + p, 2 * rows, stride=pairs)
                    block = final[n][k, at, :]
                    lanes = pl.ds(p * wide + k * LANES, LANES)
                    for j in range(2):
                        f = n + 2 * (m + j)
                        value = own[f, :, lanes].astype(F32) + block[j * rows : (j + 1) * rows]
                        out[f, :, lanes] = jnp.where(good[j], value, 0.0).astype(BF16)
        for m in range(half):
            ready(n + 2 * m)

    half = frames // 2
    bias_two_wide = twice(bias_two)
    added = [rim_sums(n, f, weight, side, keep, channels, frames) for n, f, side, keep in sides]
    for h in range(frames + 2):
        hidden[h][0] = jnp.zeros((pairs, wide), BF16)
        hidden[h][rows + 1] = jnp.zeros((pairs, wide), BF16)
        norm_rows(h, [rows_of(h, q, first, deep_inner) for q in range(2)], first)
    for h in range(1, frames + 1):
        norm_rims(h)
    one = product(1)
    two = product(2)
    norm_rims(0)
    zero = product(0)
    norm_rims(frames + 1)
    emit(0, [x - y - z for x, y, z in zip(zero, one, two)])
    three = product(3)
    emit(1, [z - y - x for x, y, z in zip(three, one, two)])


def first_block_kernel(
    bands, count, own, above, below, from_own, mixed_two, bias, weight, gain_two, bias_two,
    weight_two, out, *scratch,
):
    parts = split(scratch, own.shape[0])

    @pl.when(lax.axis_index("tm") == 0)
    def _():
        def sums_at(h, q, rows):
            value = from_own[q, max(h - 2, 0), rows]
            return value if h >= 2 else jnp.zeros_like(value)

        near = (above, below)
        finish(
            bands, count, own, near, near, bias, weight, gain_two, bias_two, weight_two,
            mixed_two, out, from_own.shape[2], sums_at, *parts, lambda f: None,
        )


def split(scratch, frames):
    rest = scratch[frames + 2 :]
    return scratch[: frames + 2], rest[: 2 * frames], rest[2 * frames :]


def last_kernel(
    bands, count, own, above, below, far_above, far_below, from_own, from_earlier, first_out,
    mixed_two, bias, weight, gain_two, bias_two, weight_two, out, result, sems, *scratch,
):
    frames = own.shape[0]
    parts = split(scratch, frames)
    tm = lax.axis_index("tm")

    @pl.when(tm == 0)
    def _():
        copy = pltpu.make_async_copy(first_out, out, sems.at[0])
        copy.start()
        copy.wait()

    @pl.when(tm > 0)
    def _():
        def sums_at(h, q, rows):
            if h < 2:
                return from_earlier[q, h, rows]
            if h < frames:
                return from_own[q, h - 2, rows] + from_earlier[q, h, rows]
            return from_own[q, h - 2, rows]

        copies = [
            pltpu.make_async_copy(result.at[f], out.at[f], sems.at[f]) for f in range(frames)
        ]
        finish(
            bands, count, own, (above, below), (far_above, far_below), bias, weight, gain_two,
            bias_two, weight_two, mixed_two, result, from_own.shape[2], sums_at, *parts,
            lambda f: copies[f].start(),
        )
        for copy in copies:
            copy.wait()


def shards(latents, counts, gain_first, bias_first, weight_first, gain_second, bias_second, weight_second):
    channels = gain_first.shape[0]
    frames, rows, flat = latents.shape[1:]
    wide = 2 * channels
    pairs = flat // wide
    blocks, bands = lax.axis_size("tm"), lax.axis_size("space")
    block = latents.reshape(frames, rows, flat)

    def shift(sent, step, along):
        pairs_of = [
            (t * bands + s, (t + along) % blocks * bands + (s + step * (t + along < blocks)) % bands)
            for t in range(blocks)
            for s in range(bands)
        ]
        return lax.ppermute(sent, ("tm", "space"), pairs_of)

    vmem = pl.BlockSpec(memory_space=pltpu.VMEM)
    smem = pl.BlockSpec(memory_space=pltpu.SMEM)
    params = pltpu.CompilerParams(vmem_limit_bytes=24 << 20)
    swap = bands == 2
    rims = 1 if swap else 2
    rim = jax.ShapeDtypeStruct((frames, 2, pairs, wide), BF16)
    stages = [pltpu.VMEM((3, 2 * rows * pairs, LANES), F32)] * (frames // 2)
    mask = pl.pallas_call(
        functools.partial(mask_kernel, channels),
        out_shape=jax.ShapeDtypeStruct((2 * rows, LANES), F32),
        out_specs=vmem,
        compiler_params=params,
        cost_estimate=pl.CostEstimate(flops=4 << 30, bytes_accessed=1 << 16, transcendentals=0),
        name="lane_mask",
    )()
    normed, *sent = pl.pallas_call(
        functools.partial(norm_kernel, swap),
        out_shape=[jax.ShapeDtypeStruct((frames, rows, pairs, wide), BF16)] + [rim] * rims,
        in_specs=[vmem] * 3,
        out_specs=[vmem] * (1 + rims),
        scratch_shapes=stages,
        compiler_params=params,
        cost_estimate=pl.CostEstimate(flops=4 << 30, bytes_accessed=1 << 20, transcendentals=0),
        name="norm_and_cut",
    )(mask, block, gain_first.reshape(1, channels))
    earlier = shift(block, 0, 1)
    if swap:
        near = (shift(sent[0], 1, 0),) * 2
        far = (shift(sent[0], 1, 1),) * 2
        deep = rows + 1
    else:
        near = (shift(sent[0], 1, 0), shift(sent[1], -1, 0))
        far = (shift(sent[0], 1, 1), shift(sent[1], -1, 1))
        deep = rows + 2

    first_weight = weight_first.reshape(3, 3, 3 * channels, channels)
    second_weight = weight_second.reshape(3, 3, 3 * channels, channels)
    share = (2, frames, deep, pairs, channels)
    window = [pltpu.VMEM((deep + 2, pairs, wide), BF16)] * (frames + 1)
    cost = pl.CostEstimate(flops=1 << 20, bytes_accessed=1 << 16, transcendentals=0)
    taps = jax.ShapeDtypeStruct((2, *first_weight.shape[1:]), BF16)
    from_own, mixed_two = pl.pallas_call(
        functools.partial(own_kernel, bands, deep),
        out_shape=[jax.ShapeDtypeStruct(share, F32), taps],
        in_specs=[smem] + [vmem] * 6,
        out_specs=[vmem] * 2,
        scratch_shapes=window,
        compiler_params=params,
        cost_estimate=cost,
        name="conv_one_own",
    )(
        counts, normed, first_weight, second_weight, gain_second.reshape(1, channels),
        bias_first.reshape(1, channels), bias_second.reshape(1, channels),
    )
    constants = (
        bias_first.reshape(1, channels), first_weight,
        gain_second.reshape(1, channels), bias_second.reshape(1, channels), second_weight,
    )
    result = jax.ShapeDtypeStruct((frames, rows, flat), BF16)
    scratch = (
        [pltpu.VMEM((rows + 2, pairs, wide), BF16)] * (frames + 2 + 2 * frames)
        + [pltpu.VMEM((3, frames // 2 * rows * pairs, LANES), F32)] * 2
    )
    first_out = pl.pallas_call(
        functools.partial(first_block_kernel, bands),
        out_shape=result,
        in_specs=[smem] + [vmem] * 10,
        out_specs=vmem,
        scratch_shapes=scratch,
        compiler_params=params,
        cost_estimate=cost,
        name="first_block",
    )(counts, block, *near, from_own, mixed_two, *constants)
    from_earlier = pl.pallas_call(
        functools.partial(earlier_kernel, bands, deep),
        out_shape=jax.ShapeDtypeStruct(share, F32),
        in_specs=[smem] + [vmem] * 5,
        out_specs=vmem,
        scratch_shapes=window + stages,
        compiler_params=params,
        cost_estimate=cost,
        name="conv_one_earlier",
    )(counts, mask, earlier, gain_first.reshape(1, channels), first_weight, first_out)
    out = pl.pallas_call(
        functools.partial(last_kernel, bands),
        out_shape=result,
        in_specs=[smem] + [vmem] * 14,
        out_specs=pl.BlockSpec(memory_space=pl.ANY),
        scratch_shapes=[
            pltpu.VMEM((frames, rows, flat), BF16), pltpu.SemaphoreType.DMA((frames,))
        ] + scratch,
        compiler_params=params,
        cost_estimate=pl.CostEstimate(flops=4 << 30, bytes_accessed=6 << 20, transcendentals=0),
        name="last",
    )(counts, block, *near, *far, from_own, from_earlier, first_out, mixed_two, *constants)
    return out.reshape(1, frames, rows, flat)


def solution(mesh):
    spread = P(("groups", "clip"), "tm", "space", None)
    return jax.shard_map(
        shards,
        mesh=mesh,
        in_specs=(spread, P(("groups", "clip")), P(), P(), P(), P(), P(), P()),
        out_specs=spread,
        check_vma=False,
    )
```

```python
import functools

import jax
import jax.numpy as jnp
from jax import lax
from jax.experimental import pallas as pl
from jax.experimental.pallas import tpu as pltpu
from jax.sharding import PartitionSpec as P

F32 = jnp.float32
BF16 = jnp.bfloat16
LANES = 128


def mask_kernel(channels, mask):
    lane = lax.broadcasted_iota(jnp.int32, mask.shape, 1)
    mask[...] = jnp.where(lane < channels - LANES, 1.0, 0.0)


def norm_silu_pair(t, half_gain, middle, channels):
    tiles = [t[:, k * LANES : (k + 1) * LANES] for k in range(3)]
    square = [tile * tile for tile in tiles]
    left = square[0] + jnp.where(middle, square[1], 0.0)
    right = square[2] + jnp.where(middle, 0.0, square[1])
    left, right = [
        lax.rsqrt(jnp.sum(x, axis=1, keepdims=True) * (1.0 / channels) + 1e-06)
        for x in (left, right)
    ]
    results = []
    for k, scale in enumerate((left, jnp.where(middle, left, right), right)):
        h = tiles[k] * scale * half_gain[:, k * LANES : (k + 1) * LANES]
        results.append(h + h * jnp.tanh(h))
    return jnp.concatenate(results, axis=1)


def norm_silu_rows(t, gain, channels):
    square = t * t
    first = lax.broadcasted_iota(jnp.int32, t.shape, 1) < channels
    left = jnp.sum(jnp.where(first, square, 0.0), axis=1, keepdims=True)
    right = jnp.sum(jnp.where(first, 0.0, square), axis=1, keepdims=True)
    left = lax.rsqrt(left * (1.0 / channels) + 1e-06)
    right = lax.rsqrt(right * (1.0 / channels) + 1e-06)
    y = t * jnp.where(first, left, right) * gain
    return y * (0.5 + 0.5 * jnp.tanh(0.5 * y))


def twice(ref):
    return jnp.concatenate([ref[...], ref[...]], axis=1)


def norm_frames(block, f, gain_wide, first, stage, store, pairs):
    rows = block.shape[1]
    wide = gain_wide.shape[1]
    for p in range(pairs):
        lanes = pl.ds(p * wide, wide)
        t = jnp.concatenate([block[f + n, :, lanes].astype(F32) for n in range(2)], axis=0)
        y = norm_silu_pair(t, gain_wide, first, wide // 2)
        for k in range(3):
            stage[k, pl.ds(p, 2 * rows, stride=pairs), :] = y[:, k * LANES : (k + 1) * LANES]
    for n in range(2):
        for r in range(rows):
            at = pl.ds((n * rows + r) * pairs, pairs)
            store(f + n, r, [stage[k, at, :].astype(BF16) for k in range(3)])


def norm_kernel(swap, mask, block, gain, normed, *rest):
    frames, rows, pairs, _ = normed.shape
    sent, stages = rest[: -(frames // 2)], rest[-(frames // 2) :]

    def store(f, r, parts):
        for k in range(3):
            normed[f, r, :, k * LANES : (k + 1) * LANES] = parts[k]

    for f in range(0, frames, 2):
        norm_frames(block, f, twice(gain) * 0.5, mask[...] > 0.5, stages[f // 2], store, pairs)
    if swap:
        first = (rows - 2) * (1 - lax.axis_index("space"))
        sent[0][...] = normed[:, pl.ds(first, 2)]
    else:
        sent[0][...] = normed[:, rows - 2 :]
        sent[1][...] = normed[:, :2]


def dot(left, right):
    return jnp.dot(
        jnp.concatenate(left, axis=1), jnp.concatenate(right, axis=0), preferred_element_type=F32
    )


def products(parts, rims, channels):
    lead = jnp.zeros((2 * LANES - channels, channels), BF16)
    mine = (
        dot(parts, [w[channels:] for w in rims]),
        dot(parts, [w[: 2 * channels] for w in rims]),
    )
    high = [x[:, LANES:] for x in parts]
    low = [x[:, : 2 * LANES] for x in parts]
    moved = (
        dot(high, [x for w in rims for x in (lead, w[:channels])]),
        dot(low, [x for w in rims for x in (w[2 * channels :], lead)]),
    )
    return mine, moved


def conv(window, weight, source, frames, rows, times, channels):
    pairs, wide = window[0].shape[1:]
    taps = [(a, b) for a in times for b in range(3)]

    def patch(a, b):
        at = source + a - times[0]
        rows_of = [window[f][b : b + rows].reshape(rows * pairs, wide) for f in range(at, at + frames)]
        return jnp.concatenate(rows_of, axis=0)

    parts = [patch(a, b) for a, b in taps]
    return add_moved(*products(parts, [weight[a, b] for a, b in taps], channels), pairs)


def mix_weights(weight, mixed):
    for b in range(3):
        outer = weight[0, b] + weight[2, b]
        mixed[0, b] = outer + weight[1, b]
        mixed[1, b] = outer - weight[1, b]


def mix(frames, i, out):
    if i == 1:
        out[...] = (frames[1][...] + frames[2][...]) * -0.5
    elif i == 2:
        out[...] = (frames[1][...] - frames[2][...]) * 0.5
    else:
        one, other = (0, 2) if i == 0 else (1, 3)
        out[...] = frames[one][...] - frames[other][...]


def mixed_product(mixed, taps, rows, channels):
    pairs, wide = mixed[0].shape[1:]
    parts = [
        jnp.concatenate([m[b : b + rows].reshape(rows * pairs, wide) for m in mixed], axis=0)
        for b in range(3)
    ]
    mine, moved = products(parts, taps, channels)
    return [*mine, *moved]


def add_moved(mine, moved, pairs):
    place = lax.broadcasted_iota(jnp.int32, mine[0].shape, 0) % pairs
    count = mine[0].shape[0]
    left = jnp.where(place == 0, 0.0, pltpu.roll(moved[0], 1, 0))
    right = jnp.where(place == pairs - 1, 0.0, pltpu.roll(moved[1], count - 1, 0))
    return mine[0] + left, mine[1] + right


def own_kernel(
    bands, deep, count, normed, weight, weight_two, gain_two, bias, bias_two, total, mixed_two, *window
):
    frames, rows, pairs, wide = normed.shape
    tm, space = lax.axis_index("tm"), lax.axis_index("space")
    nothing = jnp.zeros((pairs, wide), BF16)
    top = clear_rims(window[1:], bands, space, rows)
    window[0][...] = jnp.zeros(window[0].shape, BF16)
    for f in range(frames):
        good = tm * frames + f < count[0]
        for r in range(rows):
            window[f + 1][top + r] = jnp.where(good, normed[f, r], nothing)
    late = conv(window, weight, 1, frames - 2, deep, (0, 1, 2), wide // 2)
    soon = conv(window, weight, 0, 2, deep, (1, 2), wide // 2)
    mix_weights(weight_two, mixed_two)
    for q in range(2):
        total[q, 0:2] = soon[q].reshape(2, *total.shape[2:])
        total[q, 2:] = late[q].reshape(frames - 2, *total.shape[2:])


def clear_rims(window, bands, space, rows):
    for part in window:
        nothing = jnp.zeros(part.shape[1:], BF16)
        if bands == 2:
            part[(rows + 2) * space] = nothing
            for r in range(2):
                part[(rows + 1) * (1 - space) + r] = nothing
        else:
            for r in range(2):
                part[r] = nothing
                part[rows + 2 + r] = nothing
    return 1 + space if bands == 2 else 2


def earlier_kernel(bands, deep, count, mask, earlier, gain, weight, after, total, *scratch):
    frames, rows = earlier.shape[0], earlier.shape[1]
    window, stages = scratch[: frames + 1], scratch[frames + 1 :]
    pairs, wide = window[0].shape[1:]
    tm, space = lax.axis_index("tm"), lax.axis_index("space")

    @pl.when(tm > 0)
    def _():
        top = clear_rims(window[:frames], bands, space, rows)
        window[frames][...] = jnp.zeros(window[frames].shape, BF16)

        def store(f, r, parts):
            good = (tm - 1) * frames + f < count[0]
            for k in range(3):
                part = jnp.where(good, parts[k], jnp.zeros_like(parts[k]))
                window[f][top + r, :, k * LANES : (k + 1) * LANES] = part

        def norm(f):
            norm_frames(earlier, f, twice(gain) * 0.5, mask[...] > 0.5, stages[f // 2], store, pairs)

        norm(frames - 2)
        late = conv(window, weight, frames - 2, 2, deep, (0, 1), wide // 2)
        for f in range(0, frames - 2, 2):
            norm(f)
        for q in range(2):
            total[q, frames - 2 :] = late[q].reshape(2, *total.shape[2:])
        soon = conv(window, weight, 0, frames - 2, deep, (0, 1, 2), wide // 2)
        for q in range(2):
            total[q, 0 : frames - 2] = soon[q].reshape(frames - 2, *total.shape[2:])


def rim_sums(near, far, weight, side, keep, channels, frames):
    pairs, wide = near.shape[2], near.shape[3]
    nothing = jnp.zeros((pairs, wide), BF16)

    def row(f, r):
        ref, at = (far, f) if f < frames else (near, f - frames)
        return jnp.where(keep(f), ref[at, r], nothing)

    span = frames + 2
    rows = [[row(f, r) for r in range(2)] for f in range(2 * frames)]
    inner = [row(f, 1 - side) for f in range(2 * frames)]
    parts = [
        jnp.concatenate([x for f in range(span) for x in rows[f + a]], axis=0) for a in range(3)
    ]
    both = add_moved(*products(parts, [weight[a, 2 * side] for a in range(3)], channels), pairs)
    parts = [jnp.concatenate([inner[f + a] for f in range(span)], axis=0) for a in range(3)]
    outer = add_moved(*products(parts, [weight[a, 1] for a in range(3)], channels), pairs)
    tall = 2 * pairs
    halo = lax.broadcasted_iota(jnp.int32, (tall, channels), 0) // pairs == side

    def at(q, h):
        one = outer[q][h * pairs : (h + 1) * pairs]
        one = jnp.where(halo, jnp.concatenate([one, one], axis=0), 0.0)
        return both[q][h * tall : (h + 1) * tall] + one

    return at


def finish(bands, count, own, near, far, bias, weight, gain_two, bias_two, weight_two, mixed_two, out, deep, sums_at, hidden, mixed, final, ready):
    frames, rows, pairs, wide = near[0].shape[0], own.shape[1], near[0].shape[2], near[0].shape[3]
    channels = wide // 2
    tm, space = lax.axis_index("tm"), lax.axis_index("space")

    def valid(f):
        at = (tm - 1) * frames + f
        return (at >= 0) & (at < count[0])

    start = (1 - space) if bands == 2 else 0
    if bands == 2:
        sides = [(near[0], far[0], 1 - space, valid)]
        first, deep_inner = 2 * space, deep - 2
    else:
        sides = [
            (near[0], far[0], 0, lambda f: valid(f) & (space > 0)),
            (near[1], far[1], 1, lambda f: valid(f) & (space < bands - 1)),
        ]
        first, deep_inner = 2, deep - 4
    bias_wide, gain_wide = twice(bias), twice(gain_two)

    def norm_rows(h, sums, base):
        t = jnp.concatenate(sums, axis=1)
        number = t.shape[0] // pairs
        row = lax.broadcasted_iota(jnp.int32, (t.shape[0], 1), 0) // pairs
        row = row + (space * rows - 1 + start + base)
        good = (row >= 0) & (row < bands * rows) & valid(frames + h - 2)
        t = jnp.where(good, t + bias_wide, 0.0).astype(BF16).astype(F32)
        y = norm_silu_rows(t, gain_wide, channels).astype(BF16)
        for r in range(number):
            hidden[h][start + base + r] = y[r * pairs : (r + 1) * pairs]

    def rows_of(h, q, base, number):
        return sums_at(h, q, pl.ds(base, number)).reshape(number * pairs, channels)

    def norm_rims(h):
        for (_, _, side, _), sums in zip(sides, added):
            low = (deep - 2) * side
            norm_rows(h, [rows_of(h, q, low, 2) + sums(q, h) for q in range(2)], low)

    def product(i):
        for n in range(half):
            mix(hidden[2 * n : 2 * n + 4], i, mixed[half * i + n])
        taps = [(weight_two[0, b], mixed_two[0, b], mixed_two[1, b], weight_two[2, b])[i] for b in range(3)]
        return mixed_product(mixed[half * i : half * (i + 1)], taps, rows, channels)

    def emit(n, result):
        both = add_moved(result[:2], result[2:], pairs)
        both = jnp.concatenate(both, axis=1) + bias_two_wide
        for k in range(3):
            final[n][k] = both[:, k * LANES : (k + 1) * LANES]
        for m in range(0, half, 2):
            good = [valid(frames + n + 2 * (m + j)) for j in range(2)]
            for p in range(pairs):
                for k in range(3):
                    at = pl.ds(m * rows * pairs + p, 2 * rows, stride=pairs)
                    block = final[n][k, at, :]
                    lanes = pl.ds(p * wide + k * LANES, LANES)
                    for j in range(2):
                        f = n + 2 * (m + j)
                        value = own[f, :, lanes].astype(F32) + block[j * rows : (j + 1) * rows]
                        out[f, :, lanes] = jnp.where(good[j], value, 0.0).astype(BF16)
        for m in range(half):
            ready(n + 2 * m)

    half = frames // 2
    bias_two_wide = twice(bias_two)
    added = [rim_sums(n, f, weight, side, keep, channels, frames) for n, f, side, keep in sides]
    for h in range(frames + 2):
        hidden[h][0] = jnp.zeros((pairs, wide), BF16)
        hidden[h][rows + 1] = jnp.zeros((pairs, wide), BF16)
        norm_rows(h, [rows_of(h, q, first, deep_inner) for q in range(2)], first)
    for h in range(1, frames + 1):
        norm_rims(h)
    one = product(1)
    two = product(2)
    norm_rims(0)
    zero = product(0)
    norm_rims(frames + 1)
    emit(0, [x - y - z for x, y, z in zip(zero, one, two)])
    three = product(3)
    emit(1, [z - y - x for x, y, z in zip(three, one, two)])


def first_block_kernel(
    bands, count, own, above, below, from_own, mixed_two, bias, weight, gain_two, bias_two,
    weight_two, out, *scratch,
):
    parts = split(scratch, own.shape[0])

    @pl.when(lax.axis_index("tm") == 0)
    def _():
        def sums_at(h, q, rows):
            value = from_own[q, max(h - 2, 0), rows]
            return value if h >= 2 else jnp.zeros_like(value)

        near = (above, below)
        finish(
            bands, count, own, near, near, bias, weight, gain_two, bias_two, weight_two,
            mixed_two, out, from_own.shape[2], sums_at, *parts, lambda f: None,
        )


def split(scratch, frames):
    rest = scratch[frames + 2 :]
    return scratch[: frames + 2], rest[: 2 * frames], rest[2 * frames :]


def last_kernel(
    bands, count, own, above, below, far_above, far_below, from_own, from_earlier, first_out,
    mixed_two, bias, weight, gain_two, bias_two, weight_two, out, result, sems, *scratch,
):
    frames = own.shape[0]
    parts = split(scratch, frames)
    tm = lax.axis_index("tm")

    @pl.when(tm == 0)
    def _():
        copy = pltpu.make_async_copy(first_out, out, sems.at[0])
        copy.start()
        copy.wait()

    @pl.when(tm > 0)
    def _():
        def sums_at(h, q, rows):
            if h < 2:
                return from_earlier[q, h, rows]
            if h < frames:
                return from_own[q, h - 2, rows] + from_earlier[q, h, rows]
            return from_own[q, h - 2, rows]

        copies = [
            pltpu.make_async_copy(result.at[f], out.at[f], sems.at[f]) for f in range(frames)
        ]
        finish(
            bands, count, own, (above, below), (far_above, far_below), bias, weight, gain_two,
            bias_two, weight_two, mixed_two, result, from_own.shape[2], sums_at, *parts,
            lambda f: copies[f].start(),
        )
        for copy in copies:
            copy.wait()


def shards(latents, counts, gain_first, bias_first, weight_first, gain_second, bias_second, weight_second):
    channels = gain_first.shape[0]
    frames, rows, flat = latents.shape[1:]
    wide = 2 * channels
    pairs = flat // wide
    blocks, bands = lax.axis_size("tm"), lax.axis_size("space")
    block = latents.reshape(frames, rows, flat)

    def shift(sent, step, along):
        pairs_of = [
            (t * bands + s, (t + along) % blocks * bands + (s + step * (t + along < blocks)) % bands)
            for t in range(blocks)
            for s in range(bands)
        ]
        return lax.ppermute(sent, ("tm", "space"), pairs_of)

    vmem = pl.BlockSpec(memory_space=pltpu.VMEM)
    smem = pl.BlockSpec(memory_space=pltpu.SMEM)
    params = pltpu.CompilerParams(vmem_limit_bytes=24 << 20)
    swap = bands == 2
    rims = 1 if swap else 2
    rim = jax.ShapeDtypeStruct((frames, 2, pairs, wide), BF16)
    stages = [pltpu.VMEM((3, 2 * rows * pairs, LANES), F32)] * (frames // 2)
    mask = pl.pallas_call(
        functools.partial(mask_kernel, channels),
        out_shape=jax.ShapeDtypeStruct((2 * rows, LANES), F32),
        out_specs=vmem,
        compiler_params=params,
        cost_estimate=pl.CostEstimate(flops=4 << 30, bytes_accessed=1 << 16, transcendentals=0),
        name="lane_mask",
    )()
    normed, *sent = pl.pallas_call(
        functools.partial(norm_kernel, swap),
        out_shape=[jax.ShapeDtypeStruct((frames, rows, pairs, wide), BF16)] + [rim] * rims,
        in_specs=[vmem] * 3,
        out_specs=[vmem] * (1 + rims),
        scratch_shapes=stages,
        compiler_params=params,
        cost_estimate=pl.CostEstimate(flops=4 << 30, bytes_accessed=1 << 20, transcendentals=0),
        name="norm_and_cut",
    )(mask, block, gain_first.reshape(1, channels))
    earlier = shift(block, 0, 1)
    if swap:
        near = (shift(sent[0], 1, 0),) * 2
        far = (shift(sent[0], 1, 1),) * 2
        deep = rows + 1
    else:
        near = (shift(sent[0], 1, 0), shift(sent[1], -1, 0))
        far = (shift(sent[0], 1, 1), shift(sent[1], -1, 1))
        deep = rows + 2

    first_weight = weight_first.reshape(3, 3, 3 * channels, channels)
    second_weight = weight_second.reshape(3, 3, 3 * channels, channels)
    share = (2, frames, deep, pairs, channels)
    window = [pltpu.VMEM((deep + 2, pairs, wide), BF16)] * (frames + 1)
    cost = pl.CostEstimate(flops=1 << 20, bytes_accessed=1 << 16, transcendentals=0)
    taps = jax.ShapeDtypeStruct((2, *first_weight.shape[1:]), BF16)
    from_own, mixed_two = pl.pallas_call(
        functools.partial(own_kernel, bands, deep),
        out_shape=[jax.ShapeDtypeStruct(share, F32), taps],
        in_specs=[smem] + [vmem] * 6,
        out_specs=[vmem] * 2,
        scratch_shapes=window,
        compiler_params=params,
        cost_estimate=cost,
        name="conv_one_own",
    )(
        counts, normed, first_weight, second_weight, gain_second.reshape(1, channels),
        bias_first.reshape(1, channels), bias_second.reshape(1, channels),
    )
    constants = (
        bias_first.reshape(1, channels), first_weight,
        gain_second.reshape(1, channels), bias_second.reshape(1, channels), second_weight,
    )
    result = jax.ShapeDtypeStruct((frames, rows, flat), BF16)
    scratch = (
        [pltpu.VMEM((rows + 2, pairs, wide), BF16)] * (frames + 2 + 2 * frames)
        + [pltpu.VMEM((3, frames // 2 * rows * pairs, LANES), F32)] * 2
    )
    first_out = pl.pallas_call(
        functools.partial(first_block_kernel, bands),
        out_shape=result,
        in_specs=[smem] + [vmem] * 10,
        out_specs=vmem,
        scratch_shapes=scratch,
        compiler_params=params,
        cost_estimate=cost,
        name="first_block",
    )(counts, block, *near, from_own, mixed_two, *constants)
    from_earlier = pl.pallas_call(
        functools.partial(earlier_kernel, bands, deep),
        out_shape=jax.ShapeDtypeStruct(share, F32),
        in_specs=[smem] + [vmem] * 5,
        out_specs=vmem,
        scratch_shapes=window + stages,
        compiler_params=params,
        cost_estimate=cost,
        name="conv_one_earlier",
    )(counts, mask, earlier, gain_first.reshape(1, channels), first_weight, first_out)
    out = pl.pallas_call(
        functools.partial(last_kernel, bands),
        out_shape=result,
        in_specs=[smem] + [vmem] * 14,
        out_specs=pl.BlockSpec(memory_space=pl.ANY),
        scratch_shapes=[
            pltpu.VMEM((frames, rows, flat), BF16), pltpu.SemaphoreType.DMA((frames,))
        ] + scratch,
        compiler_params=params,
        cost_estimate=pl.CostEstimate(flops=4 << 30, bytes_accessed=6 << 20, transcendentals=0),
        name="last",
    )(counts, block, *near, *far, from_own, from_earlier, first_out, mixed_two, *constants)
    return out.reshape(1, frames, rows, flat)


def solution(mesh):
    spread = P(("groups", "clip"), "tm", "space", None)
    return jax.shard_map(
        shards,
        mesh=mesh,
        in_specs=(spread, P(("groups", "clip")), P(), P(), P(), P(), P(), P()),
        out_specs=spread,
        check_vma=False,
    )
```

```python
import functools

import jax
import jax.numpy as jnp
from jax import lax
from jax.experimental import pallas as pl
from jax.experimental.pallas import tpu as pltpu
from jax.sharding import PartitionSpec as P

F32 = jnp.float32
BF16 = jnp.bfloat16
LANES = 128


def mask_kernel(channels, mask):
    lane = lax.broadcasted_iota(jnp.int32, mask.shape, 1)
    mask[...] = jnp.where(lane < channels - LANES, 1.0, 0.0)


def norm_silu_pair(t, half_gain, middle, channels):
    tiles = [t[:, k * LANES : (k + 1) * LANES] for k in range(3)]
    square = [tile * tile for tile in tiles]
    left = square[0] + jnp.where(middle, square[1], 0.0)
    right = square[2] + jnp.where(middle, 0.0, square[1])
    left, right = [
        lax.rsqrt(jnp.sum(x, axis=1, keepdims=True) * (1.0 / channels) + 1e-06)
        for x in (left, right)
    ]
    results = []
    for k, scale in enumerate((left, jnp.where(middle, left, right), right)):
        h = tiles[k] * scale * half_gain[:, k * LANES : (k + 1) * LANES]
        results.append(h + h * jnp.tanh(h))
    return jnp.concatenate(results, axis=1)


def norm_silu_rows(t, half_gain, channels):
    square = t * t
    first = lax.broadcasted_iota(jnp.int32, t.shape, 1) < channels
    left = jnp.sum(jnp.where(first, square, 0.0), axis=1, keepdims=True)
    right = jnp.sum(jnp.where(first, 0.0, square), axis=1, keepdims=True)
    left = lax.rsqrt(left * (1.0 / channels) + 1e-06)
    right = lax.rsqrt(right * (1.0 / channels) + 1e-06)
    h = t * jnp.where(first, left, right) * half_gain
    return h + h * jnp.tanh(h)


def twice(ref):
    return jnp.concatenate([ref[...], ref[...]], axis=1)


def norm_frames(block, f, gain_wide, first, stage, store, pairs):
    rows = block.shape[1]
    wide = gain_wide.shape[1]
    for p in range(pairs):
        lanes = pl.ds(p * wide, wide)
        t = jnp.concatenate([block[f + n, :, lanes].astype(F32) for n in range(2)], axis=0)
        y = norm_silu_pair(t, gain_wide, first, wide // 2)
        for k in range(3):
            stage[k, pl.ds(p, 2 * rows, stride=pairs), :] = y[:, k * LANES : (k + 1) * LANES]
    for n in range(2):
        for r in range(rows):
            at = pl.ds((n * rows + r) * pairs, pairs)
            store(f + n, r, [stage[k, at, :].astype(BF16) for k in range(3)])


def norm_kernel(swap, mask, block, gain, normed, *rest):
    frames, rows, pairs, _ = normed.shape
    sent, stages = rest[: -(frames // 2)], rest[-(frames // 2) :]

    def store(f, r, parts):
        for k in range(3):
            normed[f, r, :, k * LANES : (k + 1) * LANES] = parts[k]

    for f in range(0, frames, 2):
        norm_frames(block, f, twice(gain) * 0.5, mask[...] > 0.5, stages[f // 2], store, pairs)
    if swap:
        first = (rows - 2) * (1 - lax.axis_index("space"))
        sent[0][...] = normed[:, pl.ds(first, 2)]
    else:
        sent[0][...] = normed[:, rows - 2 :]
        sent[1][...] = normed[:, :2]


def dot(left, right):
    return jnp.dot(
        jnp.concatenate(left, axis=1), jnp.concatenate(right, axis=0), preferred_element_type=F32
    )


def products(parts, rims, channels):
    lead = jnp.zeros((2 * LANES - channels, channels), BF16)
    mine = (
        dot(parts, [w[channels:] for w in rims]),
        dot(parts, [w[: 2 * channels] for w in rims]),
    )
    high = [x[:, LANES:] for x in parts]
    low = [x[:, : 2 * LANES] for x in parts]
    moved = (
        dot(high, [x for w in rims for x in (lead, w[:channels])]),
        dot(low, [x for w in rims for x in (w[2 * channels :], lead)]),
    )
    return mine, moved


def conv(window, weight, source, frames, rows, times, channels):
    pairs, wide = window[0].shape[1:]
    taps = [(a, b) for a in times for b in range(3)]

    def patch(a, b):
        at = source + a - times[0]
        rows_of = [window[f][b : b + rows].reshape(rows * pairs, wide) for f in range(at, at + frames)]
        return jnp.concatenate(rows_of, axis=0)

    parts = [patch(a, b) for a, b in taps]
    return add_moved(*products(parts, [weight[a, b] for a, b in taps], channels), pairs)


def mix_weights(weight, mixed):
    for b in range(3):
        outer = weight[0, b] + weight[2, b]
        mixed[0, b] = outer + weight[1, b]
        mixed[1, b] = outer - weight[1, b]


def mix(frames, i, out):
    if i == 1:
        out[...] = (frames[1][...] + frames[2][...]) * -0.5
    elif i == 2:
        out[...] = (frames[1][...] - frames[2][...]) * 0.5
    else:
        one, other = (0, 2) if i == 0 else (1, 3)
        out[...] = frames[one][...] - frames[other][...]


def mixed_product(mixed, taps, rows, channels):
    pairs, wide = mixed[0].shape[1:]
    parts = [
        jnp.concatenate([m[b : b + rows].reshape(rows * pairs, wide) for m in mixed], axis=0)
        for b in range(3)
    ]
    mine, moved = products(parts, taps, channels)
    return [*mine, *moved]


def add_moved(mine, moved, pairs):
    place = lax.broadcasted_iota(jnp.int32, mine[0].shape, 0) % pairs
    count = mine[0].shape[0]
    left = jnp.where(place == 0, 0.0, pltpu.roll(moved[0], 1, 0))
    right = jnp.where(place == pairs - 1, 0.0, pltpu.roll(moved[1], count - 1, 0))
    return mine[0] + left, mine[1] + right


def own_kernel(
    bands, deep, count, normed, weight, weight_two, gain_two, bias, bias_two, total, mixed_two, *window
):
    frames, rows, pairs, wide = normed.shape
    tm, space = lax.axis_index("tm"), lax.axis_index("space")
    nothing = jnp.zeros((pairs, wide), BF16)
    top = clear_rims(window[1:], bands, space, rows)
    window[0][...] = jnp.zeros(window[0].shape, BF16)
    for f in range(frames):
        good = tm * frames + f < count[0]
        for r in range(rows):
            window[f + 1][top + r] = jnp.where(good, normed[f, r], nothing)
    mix_weights(weight_two, mixed_two)
    late = conv(window, weight, 1, frames - 2, deep, (0, 1, 2), wide // 2)
    soon = conv(window, weight, 0, 2, deep, (1, 2), wide // 2)
    for q in range(2):
        total[q, 0:2] = soon[q].reshape(2, *total.shape[2:])
        total[q, 2:] = late[q].reshape(frames - 2, *total.shape[2:])


def clear_rims(window, bands, space, rows):
    for part in window:
        nothing = jnp.zeros(part.shape[1:], BF16)
        if bands == 2:
            part[(rows + 2) * space] = nothing
            for r in range(2):
                part[(rows + 1) * (1 - space) + r] = nothing
        else:
            for r in range(2):
                part[r] = nothing
                part[rows + 2 + r] = nothing
    return 1 + space if bands == 2 else 2


def earlier_kernel(bands, deep, count, mask, earlier, gain, weight, after, total, *scratch):
    frames, rows = earlier.shape[0], earlier.shape[1]
    window, stages = scratch[: frames + 1], scratch[frames + 1 :]
    pairs, wide = window[0].shape[1:]
    tm, space = lax.axis_index("tm"), lax.axis_index("space")

    @pl.when(tm > 0)
    def _():
        top = clear_rims(window[:frames], bands, space, rows)
        window[frames][...] = jnp.zeros(window[frames].shape, BF16)

        def store(f, r, parts):
            good = (tm - 1) * frames + f < count[0]
            for k in range(3):
                part = jnp.where(good, parts[k], jnp.zeros_like(parts[k]))
                window[f][top + r, :, k * LANES : (k + 1) * LANES] = part

        def norm(f):
            norm_frames(earlier, f, twice(gain) * 0.5, mask[...] > 0.5, stages[f // 2], store, pairs)

        norm(frames - 2)
        late = conv(window, weight, frames - 2, 2, deep, (0, 1), wide // 2)
        for f in range(0, frames - 2, 2):
            norm(f)
        for q in range(2):
            total[q, frames - 2 :] = late[q].reshape(2, *total.shape[2:])
        soon = conv(window, weight, 0, frames - 2, deep, (0, 1, 2), wide // 2)
        for q in range(2):
            total[q, 0 : frames - 2] = soon[q].reshape(frames - 2, *total.shape[2:])


def rim_sums(near, far, weight, side, keep, channels, frames):
    pairs, wide = near.shape[2], near.shape[3]
    nothing = jnp.zeros((pairs, wide), BF16)

    def row(f, r):
        ref, at = (far, f) if f < frames else (near, f - frames)
        return jnp.where(keep(f), ref[at, r], nothing)

    span = frames + 2
    rows = [[row(f, r) for r in range(2)] for f in range(2 * frames)]
    inner = [row(f, 1 - side) for f in range(2 * frames)]
    parts = [
        jnp.concatenate([x for f in range(span) for x in rows[f + a]], axis=0) for a in range(3)
    ]
    both = add_moved(*products(parts, [weight[a, 2 * side] for a in range(3)], channels), pairs)
    parts = [jnp.concatenate([inner[f + a] for f in range(span)], axis=0) for a in range(3)]
    outer = add_moved(*products(parts, [weight[a, 1] for a in range(3)], channels), pairs)
    tall = 2 * pairs
    halo = lax.broadcasted_iota(jnp.int32, (tall, channels), 0) // pairs == side

    def at(q, h):
        one = outer[q][h * pairs : (h + 1) * pairs]
        one = jnp.where(halo, jnp.concatenate([one, one], axis=0), 0.0)
        return both[q][h * tall : (h + 1) * tall] + one

    return at


def finish(bands, count, own, near, far, bias, weight, gain_two, bias_two, weight_two, mixed_two, out, deep, sums_at, hidden, mixed, final, ready):
    frames, rows, pairs, wide = near[0].shape[0], own.shape[1], near[0].shape[2], near[0].shape[3]
    channels = wide // 2
    tm, space = lax.axis_index("tm"), lax.axis_index("space")

    def valid(f):
        at = (tm - 1) * frames + f
        return (at >= 0) & (at < count[0])

    start = (1 - space) if bands == 2 else 0
    if bands == 2:
        sides = [(near[0], far[0], 1 - space, valid)]
        first, deep_inner = 2 * space, deep - 2
    else:
        sides = [
            (near[0], far[0], 0, lambda f: valid(f) & (space > 0)),
            (near[1], far[1], 1, lambda f: valid(f) & (space < bands - 1)),
        ]
        first, deep_inner = 2, deep - 4
    bias_wide, gain_wide = twice(bias), twice(gain_two) * 0.5

    def norm_rows(h, sums, base):
        t = jnp.concatenate(sums, axis=1)
        number = t.shape[0] // pairs
        good = valid(frames + h - 2)
        if bands != 2:
            row = lax.broadcasted_iota(jnp.int32, (t.shape[0], 1), 0) // pairs
            row = row + (space * rows - 1 + start + base)
            good = (row >= 0) & (row < bands * rows) & good
        t = jnp.where(good, t + bias_wide, 0.0).astype(BF16).astype(F32)
        y = norm_silu_rows(t, gain_wide, channels).astype(BF16)
        for r in range(number):
            hidden[h][start + base + r] = y[r * pairs : (r + 1) * pairs]

    def rows_of(h, q, base, number):
        return sums_at(h, q, pl.ds(base, number)).reshape(number * pairs, channels)

    def norm_rims(h):
        for (_, _, side, _), sums in zip(sides, added):
            low = (deep - 2) * side
            norm_rows(h, [rows_of(h, q, low, 2) + sums(q, h) for q in range(2)], low)

    def product(i):
        for n in range(half):
            mix(hidden[2 * n : 2 * n + 4], i, mixed[half * i + n])
        taps = [(weight_two[0, b], mixed_two[0, b], mixed_two[1, b], weight_two[2, b])[i] for b in range(3)]
        return mixed_product(mixed[half * i : half * (i + 1)], taps, rows, channels)

    def emit(n, result):
        both = add_moved(result[:2], result[2:], pairs)
        both = jnp.concatenate(both, axis=1) + bias_two_wide
        for k in range(3):
            final[n][k] = both[:, k * LANES : (k + 1) * LANES]
        for m in range(0, half, 2):
            good = [valid(frames + n + 2 * (m + j)) for j in range(2)]
            for p in range(pairs):
                for k in range(3):
                    at = pl.ds(m * rows * pairs + p, 2 * rows, stride=pairs)
                    block = final[n][k, at, :]
                    lanes = pl.ds(p * wide + k * LANES, LANES)
                    for j in range(2):
                        f = n + 2 * (m + j)
                        value = own[f, :, lanes].astype(F32) + block[j * rows : (j + 1) * rows]
                        out[f, :, lanes] = jnp.where(good[j], value, 0.0).astype(BF16)
        for m in range(half):
            ready(n + 2 * m)

    half = frames // 2
    bias_two_wide = twice(bias_two)
    added = [rim_sums(n, f, weight, side, keep, channels, frames) for n, f, side, keep in sides]
    for h in range(frames + 2):
        hidden[h][0] = jnp.zeros((pairs, wide), BF16)
        hidden[h][rows + 1] = jnp.zeros((pairs, wide), BF16)
        norm_rows(h, [rows_of(h, q, first, deep_inner) for q in range(2)], first)
    for h in range(1, frames + 1):
        norm_rims(h)
    one = product(1)
    two = product(2)
    norm_rims(0)
    zero = product(0)
    norm_rims(frames + 1)
    emit(0, [x - y - z for x, y, z in zip(zero, one, two)])
    three = product(3)
    emit(1, [z - y - x for x, y, z in zip(three, one, two)])


def first_block_kernel(
    bands, count, own, above, below, from_own, mixed_two, bias, weight, gain_two, bias_two,
    weight_two, out, *scratch,
):
    parts = split(scratch, own.shape[0])

    @pl.when(lax.axis_index("tm") == 0)
    def _():
        def sums_at(h, q, rows):
            value = from_own[q, max(h - 2, 0), rows]
            return value if h >= 2 else jnp.zeros_like(value)

        near = (above, below)
        finish(
            bands, count, own, near, near, bias, weight, gain_two, bias_two, weight_two,
            mixed_two, out, from_own.shape[2], sums_at, *parts, lambda f: None,
        )


def split(scratch, frames):
    rest = scratch[frames + 2 :]
    return scratch[: frames + 2], rest[: 2 * frames], rest[2 * frames :]


def last_kernel(
    bands, count, own, above, below, far_above, far_below, from_own, from_earlier, first_out,
    mixed_two, bias, weight, gain_two, bias_two, weight_two, out, result, sems, *scratch,
):
    frames = own.shape[0]
    parts = split(scratch, frames)
    tm = lax.axis_index("tm")

    @pl.when(tm == 0)
    def _():
        copy = pltpu.make_async_copy(first_out, out, sems.at[0])
        copy.start()
        copy.wait()

    @pl.when(tm > 0)
    def _():
        def sums_at(h, q, rows):
            if h < 2:
                return from_earlier[q, h, rows]
            if h < frames:
                return from_own[q, h - 2, rows] + from_earlier[q, h, rows]
            return from_own[q, h - 2, rows]

        copies = [
            pltpu.make_async_copy(result.at[f], out.at[f], sems.at[f]) for f in range(frames)
        ]
        finish(
            bands, count, own, (above, below), (far_above, far_below), bias, weight, gain_two,
            bias_two, weight_two, mixed_two, result, from_own.shape[2], sums_at, *parts,
            lambda f: copies[f].start(),
        )
        for copy in copies:
            copy.wait()


def shards(latents, counts, gain_first, bias_first, weight_first, gain_second, bias_second, weight_second):
    channels = gain_first.shape[0]
    frames, rows, flat = latents.shape[1:]
    wide = 2 * channels
    pairs = flat // wide
    blocks, bands = lax.axis_size("tm"), lax.axis_size("space")
    block = latents.reshape(frames, rows, flat)

    def shift(sent, step, along):
        pairs_of = [
            (t * bands + s, (t + along) % blocks * bands + (s + step * (t + along < blocks)) % bands)
            for t in range(blocks)
            for s in range(bands)
        ]
        return lax.ppermute(sent, ("tm", "space"), pairs_of)

    vmem = pl.BlockSpec(memory_space=pltpu.VMEM)
    smem = pl.BlockSpec(memory_space=pltpu.SMEM)
    params = pltpu.CompilerParams(vmem_limit_bytes=24 << 20)
    swap = bands == 2
    rims = 1 if swap else 2
    rim = jax.ShapeDtypeStruct((frames, 2, pairs, wide), BF16)
    stages = [pltpu.VMEM((3, 2 * rows * pairs, LANES), F32)] * (frames // 2)
    mask = pl.pallas_call(
        functools.partial(mask_kernel, channels),
        out_shape=jax.ShapeDtypeStruct((2 * rows, LANES), F32),
        out_specs=vmem,
        compiler_params=params,
        cost_estimate=pl.CostEstimate(flops=4 << 30, bytes_accessed=1 << 16, transcendentals=0),
        name="lane_mask",
    )()
    normed, *sent = pl.pallas_call(
        functools.partial(norm_kernel, swap),
        out_shape=[jax.ShapeDtypeStruct((frames, rows, pairs, wide), BF16)] + [rim] * rims,
        in_specs=[vmem] * 3,
        out_specs=[vmem] * (1 + rims),
        scratch_shapes=stages,
        compiler_params=params,
        cost_estimate=pl.CostEstimate(flops=4 << 30, bytes_accessed=1 << 20, transcendentals=0),
        name="norm_and_cut",
    )(mask, block, gain_first.reshape(1, channels))
    earlier = shift(block, 0, 1)
    if swap:
        near = (shift(sent[0], 1, 0),) * 2
        far = (shift(sent[0], 1, 1),) * 2
        deep = rows + 1
    else:
        near = (shift(sent[0], 1, 0), shift(sent[1], -1, 0))
        far = (shift(sent[0], 1, 1), shift(sent[1], -1, 1))
        deep = rows + 2

    first_weight = weight_first.reshape(3, 3, 3 * channels, channels)
    second_weight = weight_second.reshape(3, 3, 3 * channels, channels)
    share = (2, frames, deep, pairs, channels)
    window = [pltpu.VMEM((deep + 2, pairs, wide), BF16)] * (frames + 1)
    cost = pl.CostEstimate(flops=1 << 20, bytes_accessed=1 << 16, transcendentals=0)
    taps = jax.ShapeDtypeStruct((2, *first_weight.shape[1:]), BF16)
    from_own, mixed_two = pl.pallas_call(
        functools.partial(own_kernel, bands, deep),
        out_shape=[jax.ShapeDtypeStruct(share, F32), taps],
        in_specs=[smem] + [vmem] * 6,
        out_specs=[vmem] * 2,
        scratch_shapes=window,
        compiler_params=params,
        cost_estimate=cost,
        name="conv_one_own",
    )(
        counts, normed, first_weight, second_weight, gain_second.reshape(1, channels),
        bias_first.reshape(1, channels), bias_second.reshape(1, channels),
    )
    constants = (
        bias_first.reshape(1, channels), first_weight,
        gain_second.reshape(1, channels), bias_second.reshape(1, channels), second_weight,
    )
    result = jax.ShapeDtypeStruct((frames, rows, flat), BF16)
    scratch = (
        [pltpu.VMEM((rows + 2, pairs, wide), BF16)] * (frames + 2 + 2 * frames)
        + [pltpu.VMEM((3, frames // 2 * rows * pairs, LANES), F32)] * 2
    )
    first_out = pl.pallas_call(
        functools.partial(first_block_kernel, bands),
        out_shape=result,
        in_specs=[smem] + [vmem] * 10,
        out_specs=vmem,
        scratch_shapes=scratch,
        compiler_params=params,
        cost_estimate=cost,
        name="first_block",
    )(counts, block, *near, from_own, mixed_two, *constants)
    from_earlier = pl.pallas_call(
        functools.partial(earlier_kernel, bands, deep),
        out_shape=jax.ShapeDtypeStruct(share, F32),
        in_specs=[smem] + [vmem] * 5,
        out_specs=vmem,
        scratch_shapes=window + stages,
        compiler_params=params,
        cost_estimate=cost,
        name="conv_one_earlier",
    )(counts, mask, earlier, gain_first.reshape(1, channels), first_weight, first_out)
    out = pl.pallas_call(
        functools.partial(last_kernel, bands),
        out_shape=result,
        in_specs=[smem] + [vmem] * 14,
        out_specs=pl.BlockSpec(memory_space=pl.ANY),
        scratch_shapes=[
            pltpu.VMEM((frames, rows, flat), BF16), pltpu.SemaphoreType.DMA((frames,))
        ] + scratch,
        compiler_params=params,
        cost_estimate=pl.CostEstimate(flops=4 << 30, bytes_accessed=6 << 20, transcendentals=0),
        name="last",
    )(counts, block, *near, *far, from_own, from_earlier, first_out, mixed_two, *constants)
    return out.reshape(1, frames, rows, flat)


def solution(mesh):
    spread = P(("groups", "clip"), "tm", "space", None)
    return jax.shard_map(
        shards,
        mesh=mesh,
        in_specs=(spread, P(("groups", "clip")), P(), P(), P(), P(), P(), P()),
        out_specs=spread,
        check_vma=False,
    )
```

```python
import functools

import jax
import jax.numpy as jnp
from jax import lax
from jax.experimental import pallas as pl
from jax.experimental.pallas import tpu as pltpu
from jax.sharding import PartitionSpec as P

F32 = jnp.float32
BF16 = jnp.bfloat16
LANES = 128


def mask_kernel(channels, mask):
    lane = lax.broadcasted_iota(jnp.int32, mask.shape, 1)
    mask[...] = jnp.where(lane < channels - LANES, 1.0, 0.0)


def norm_silu_pair(t, half_gain, middle, channels):
    tiles = [t[:, k * LANES : (k + 1) * LANES] for k in range(3)]
    square = [tile * tile for tile in tiles]
    left = square[0] + jnp.where(middle, square[1], 0.0)
    right = square[2] + jnp.where(middle, 0.0, square[1])
    left, right = [
        lax.rsqrt(jnp.sum(x, axis=1, keepdims=True) * (1.0 / channels) + 1e-06)
        for x in (left, right)
    ]
    results = []
    for k, scale in enumerate((left, jnp.where(middle, left, right), right)):
        h = tiles[k] * scale * half_gain[:, k * LANES : (k + 1) * LANES]
        results.append(h + h * jnp.tanh(h))
    return jnp.concatenate(results, axis=1)


def norm_silu_rows(t, gain, channels):
    square = t * t
    first = lax.broadcasted_iota(jnp.int32, t.shape, 1) < channels
    left = jnp.sum(jnp.where(first, square, 0.0), axis=1, keepdims=True)
    right = jnp.sum(jnp.where(first, 0.0, square), axis=1, keepdims=True)
    left = lax.rsqrt(left * (1.0 / channels) + 1e-06)
    right = lax.rsqrt(right * (1.0 / channels) + 1e-06)
    y = t * jnp.where(first, left, right) * gain
    return y * (0.5 + 0.5 * jnp.tanh(0.5 * y))


def twice(ref):
    return jnp.concatenate([ref[...], ref[...]], axis=1)


def norm_frames(block, f, gain_wide, first, stage, store, pairs):
    rows = block.shape[1]
    wide = gain_wide.shape[1]
    for p in range(pairs):
        lanes = pl.ds(p * wide, wide)
        t = jnp.concatenate([block[f + n, :, lanes].astype(F32) for n in range(2)], axis=0)
        y = norm_silu_pair(t, gain_wide, first, wide // 2)
        for k in range(3):
            stage[k, pl.ds(p, 2 * rows, stride=pairs), :] = y[:, k * LANES : (k + 1) * LANES]
    for n in range(2):
        for r in range(rows):
            at = pl.ds((n * rows + r) * pairs, pairs)
            store(f + n, r, [stage[k, at, :].astype(BF16) for k in range(3)])


def norm_kernel(swap, mask, block, gain, normed, *rest):
    frames, rows, pairs, _ = normed.shape
    sent, stages = rest[: -(frames // 2)], rest[-(frames // 2) :]

    def store(f, r, parts):
        for k in range(3):
            normed[f, r, :, k * LANES : (k + 1) * LANES] = parts[k]

    for f in range(0, frames, 2):
        norm_frames(block, f, twice(gain) * 0.5, mask[...] > 0.5, stages[f // 2], store, pairs)
    if swap:
        first = (rows - 2) * (1 - lax.axis_index("space"))
        sent[0][...] = normed[:, pl.ds(first, 2)]
    else:
        sent[0][...] = normed[:, rows - 2 :]
        sent[1][...] = normed[:, :2]


def dot(left, right):
    return jnp.dot(
        jnp.concatenate(left, axis=1), jnp.concatenate(right, axis=0), preferred_element_type=F32
    )


def products(parts, rims, channels):
    lead = jnp.zeros((2 * LANES - channels, channels), BF16)
    mine = (
        dot(parts, [w[channels:] for w in rims]),
        dot(parts, [w[: 2 * channels] for w in rims]),
    )
    high = [x[:, LANES:] for x in parts]
    low = [x[:, : 2 * LANES] for x in parts]
    moved = (
        dot(high, [x for w in rims for x in (lead, w[:channels])]),
        dot(low, [x for w in rims for x in (w[2 * channels :], lead)]),
    )
    return mine, moved


def conv(window, weight, source, frames, rows, times, channels):
    pairs, wide = window[0].shape[1:]
    taps = [(a, b) for a in times for b in range(3)]

    def patch(a, b):
        at = source + a - times[0]
        rows_of = [window[f][b : b + rows].reshape(rows * pairs, wide) for f in range(at, at + frames)]
        return jnp.concatenate(rows_of, axis=0)

    parts = [patch(a, b) for a, b in taps]
    return add_moved(*products(parts, [weight[a, b] for a, b in taps], channels), pairs)


def mix_weights(weight, mixed):
    for b in range(3):
        outer = weight[0, b] + weight[2, b]
        mixed[0, b] = outer + weight[1, b]
        mixed[1, b] = outer - weight[1, b]


def mix(frames, i, out):
    if i == 1:
        out[...] = (frames[1][...] + frames[2][...]) * -0.5
    elif i == 2:
        out[...] = (frames[1][...] - frames[2][...]) * 0.5
    else:
        one, other = (0, 2) if i == 0 else (1, 3)
        out[...] = frames[one][...] - frames[other][...]


def mixed_product(mixed, taps, rows, channels):
    pairs, wide = mixed[0].shape[1:]
    parts = [
        jnp.concatenate([m[b : b + rows].reshape(rows * pairs, wide) for m in mixed], axis=0)
        for b in range(3)
    ]
    mine, moved = products(parts, taps, channels)
    return [*mine, *moved]


def add_moved(mine, moved, pairs):
    place = lax.broadcasted_iota(jnp.int32, mine[0].shape, 0) % pairs
    count = mine[0].shape[0]
    left = jnp.where(place == 0, 0.0, pltpu.roll(moved[0], 1, 0))
    right = jnp.where(place == pairs - 1, 0.0, pltpu.roll(moved[1], count - 1, 0))
    return mine[0] + left, mine[1] + right


def own_kernel(
    bands, deep, count, normed, weight, weight_two, gain_two, bias, bias_two, total, mixed_two, *window
):
    frames, rows, pairs, wide = normed.shape
    tm, space = lax.axis_index("tm"), lax.axis_index("space")
    nothing = jnp.zeros((pairs, wide), BF16)
    top = clear_rims(window[1:], bands, space, rows)
    window[0][...] = jnp.zeros(window[0].shape, BF16)
    for f in range(frames):
        good = tm * frames + f < count[0]
        for r in range(rows):
            window[f + 1][top + r] = jnp.where(good, normed[f, r], nothing)
    late = conv(window, weight, 1, frames - 2, deep, (0, 1, 2), wide // 2)
    soon = conv(window, weight, 0, 2, deep, (1, 2), wide // 2)
    mix_weights(weight_two, mixed_two)
    for q in range(2):
        total[q, 0:2] = soon[q].reshape(2, *total.shape[2:])
        total[q, 2:] = late[q].reshape(frames - 2, *total.shape[2:])


def clear_rims(window, bands, space, rows):
    for part in window:
        nothing = jnp.zeros(part.shape[1:], BF16)
        if bands == 2:
            part[(rows + 2) * space] = nothing
            for r in range(2):
                part[(rows + 1) * (1 - space) + r] = nothing
        else:
            for r in range(2):
                part[r] = nothing
                part[rows + 2 + r] = nothing
    return 1 + space if bands == 2 else 2


def earlier_kernel(bands, deep, count, mask, earlier, gain, weight, after, total, *scratch):
    frames, rows = earlier.shape[0], earlier.shape[1]
    window, stages = scratch[: frames + 1], scratch[frames + 1 :]
    pairs, wide = window[0].shape[1:]
    tm, space = lax.axis_index("tm"), lax.axis_index("space")

    @pl.when(tm > 0)
    def _():
        top = clear_rims(window[:frames], bands, space, rows)
        window[frames][...] = jnp.zeros(window[frames].shape, BF16)

        def store(f, r, parts):
            good = (tm - 1) * frames + f < count[0]
            for k in range(3):
                part = jnp.where(good, parts[k], jnp.zeros_like(parts[k]))
                window[f][top + r, :, k * LANES : (k + 1) * LANES] = part

        def norm(f):
            norm_frames(earlier, f, twice(gain) * 0.5, mask[...] > 0.5, stages[f // 2], store, pairs)

        def add(a):
            both = conv(window, weight, a, frames - a, deep, (a,), wide // 2)
            for q in range(2):
                value = both[q].reshape(frames - a, *total.shape[2:])
                if a < 2:
                    total[q, 0 : frames - a - 1] += value[: frames - a - 1]
                    total[q, frames - a - 1 : frames - a] = value[frames - a - 1 :]
                else:
                    total[q, 0 : frames - a] = value

        norm(frames - 2)
        add(2)
        for f in range(0, frames - 2, 2):
            norm(f)
        add(1)
        add(0)


def rim_sums(near, far, weight, side, keep, channels, frames):
    pairs, wide = near.shape[2], near.shape[3]
    nothing = jnp.zeros((pairs, wide), BF16)

    def row(f, r):
        ref, at = (far, f) if f < frames else (near, f - frames)
        return jnp.where(keep(f), ref[at, r], nothing)

    span = frames + 2
    rows = [[row(f, r) for r in range(2)] for f in range(2 * frames)]
    inner = [row(f, 1 - side) for f in range(2 * frames)]
    parts = [
        jnp.concatenate([x for f in range(span) for x in rows[f + a]], axis=0) for a in range(3)
    ]
    both = add_moved(*products(parts, [weight[a, 2 * side] for a in range(3)], channels), pairs)
    parts = [jnp.concatenate([inner[f + a] for f in range(span)], axis=0) for a in range(3)]
    outer = add_moved(*products(parts, [weight[a, 1] for a in range(3)], channels), pairs)
    tall = 2 * pairs
    halo = lax.broadcasted_iota(jnp.int32, (tall, channels), 0) // pairs == side

    def at(q, h):
        one = outer[q][h * pairs : (h + 1) * pairs]
        one = jnp.where(halo, jnp.concatenate([one, one], axis=0), 0.0)
        return both[q][h * tall : (h + 1) * tall] + one

    return at


def finish(bands, count, own, near, far, bias, weight, gain_two, bias_two, weight_two, mixed_two, out, deep, sums_at, hidden, mixed, final, ready):
    frames, rows, pairs, wide = near[0].shape[0], own.shape[1], near[0].shape[2], near[0].shape[3]
    channels = wide // 2
    tm, space = lax.axis_index("tm"), lax.axis_index("space")

    def valid(f):
        at = (tm - 1) * frames + f
        return (at >= 0) & (at < count[0])

    start = (1 - space) if bands == 2 else 0
    if bands == 2:
        sides = [(near[0], far[0], 1 - space, valid)]
        first, deep_inner = 2 * space, deep - 2
    else:
        sides = [
            (near[0], far[0], 0, lambda f: valid(f) & (space > 0)),
            (near[1], far[1], 1, lambda f: valid(f) & (space < bands - 1)),
        ]
        first, deep_inner = 2, deep - 4
    bias_wide, gain_wide = twice(bias), twice(gain_two)

    def norm_rows(h, sums, base):
        t = jnp.concatenate(sums, axis=1)
        number = t.shape[0] // pairs
        row = lax.broadcasted_iota(jnp.int32, (t.shape[0], 1), 0) // pairs
        row = row + (space * rows - 1 + start + base)
        good = (row >= 0) & (row < bands * rows) & valid(frames + h - 2)
        t = jnp.where(good, t + bias_wide, 0.0).astype(BF16).astype(F32)
        y = norm_silu_rows(t, gain_wide, channels).astype(BF16)
        for r in range(number):
            hidden[h][start + base + r] = y[r * pairs : (r + 1) * pairs]

    def rows_of(h, q, base, number):
        return sums_at(h, q, pl.ds(base, number)).reshape(number * pairs, channels)

    def norm_rims(h):
        for (_, _, side, _), sums in zip(sides, added):
            low = (deep - 2) * side
            norm_rows(h, [rows_of(h, q, low, 2) + sums(q, h) for q in range(2)], low)

    def product(i):
        for n in range(half):
            mix(hidden[2 * n : 2 * n + 4], i, mixed[half * i + n])
        taps = [(weight_two[0, b], mixed_two[0, b], mixed_two[1, b], weight_two[2, b])[i] for b in range(3)]
        return mixed_product(mixed[half * i : half * (i + 1)], taps, rows, channels)

    def emit(n, result):
        both = add_moved(result[:2], result[2:], pairs)
        both = jnp.concatenate(both, axis=1) + bias_two_wide
        for k in range(3):
            final[n][k] = both[:, k * LANES : (k + 1) * LANES]
        for m in range(0, half, 2):
            good = [valid(frames + n + 2 * (m + j)) for j in range(2)]
            for p in range(pairs):
                for k in range(3):
                    at = pl.ds(m * rows * pairs + p, 2 * rows, stride=pairs)
                    block = final[n][k, at, :]
                    lanes = pl.ds(p * wide + k * LANES, LANES)
                    for j in range(2):
                        f = n + 2 * (m + j)
                        value = own[f, :, lanes].astype(F32) + block[j * rows : (j + 1) * rows]
                        out[f, :, lanes] = jnp.where(good[j], value, 0.0).astype(BF16)
        for m in range(half):
            ready(n + 2 * m)

    half = frames // 2
    bias_two_wide = twice(bias_two)
    added = [rim_sums(n, f, weight, side, keep, channels, frames) for n, f, side, keep in sides]
    for h in range(frames + 2):
        hidden[h][0] = jnp.zeros((pairs, wide), BF16)
        hidden[h][rows + 1] = jnp.zeros((pairs, wide), BF16)
        norm_rows(h, [rows_of(h, q, first, deep_inner) for q in range(2)], first)
    for h in range(1, frames + 1):
        norm_rims(h)
    one = product(1)
    two = product(2)
    norm_rims(0)
    zero = product(0)
    norm_rims(frames + 1)
    emit(0, [x - y - z for x, y, z in zip(zero, one, two)])
    three = product(3)
    emit(1, [z - y - x for x, y, z in zip(three, one, two)])


def first_block_kernel(
    bands, count, own, above, below, from_own, mixed_two, bias, weight, gain_two, bias_two,
    weight_two, out, *scratch,
):
    parts = split(scratch, own.shape[0])

    @pl.when(lax.axis_index("tm") == 0)
    def _():
        def sums_at(h, q, rows):
            value = from_own[q, max(h - 2, 0), rows]
            return value if h >= 2 else jnp.zeros_like(value)

        near = (above, below)
        finish(
            bands, count, own, near, near, bias, weight, gain_two, bias_two, weight_two,
            mixed_two, out, from_own.shape[2], sums_at, *parts, lambda f: None,
        )


def split(scratch, frames):
    rest = scratch[frames + 2 :]
    return scratch[: frames + 2], rest[: 2 * frames], rest[2 * frames :]


def last_kernel(
    bands, count, own, above, below, far_above, far_below, from_own, from_earlier, first_out,
    mixed_two, bias, weight, gain_two, bias_two, weight_two, out, result, sems, *scratch,
):
    frames = own.shape[0]
    parts = split(scratch, frames)
    tm = lax.axis_index("tm")

    @pl.when(tm == 0)
    def _():
        copy = pltpu.make_async_copy(first_out, out, sems.at[0])
        copy.start()
        copy.wait()

    @pl.when(tm > 0)
    def _():
        def sums_at(h, q, rows):
            if h < 2:
                return from_earlier[q, h, rows]
            if h < frames:
                return from_own[q, h - 2, rows] + from_earlier[q, h, rows]
            return from_own[q, h - 2, rows]

        copies = [
            pltpu.make_async_copy(result.at[f], out.at[f], sems.at[f]) for f in range(frames)
        ]
        finish(
            bands, count, own, (above, below), (far_above, far_below), bias, weight, gain_two,
            bias_two, weight_two, mixed_two, result, from_own.shape[2], sums_at, *parts,
            lambda f: copies[f].start(),
        )
        for copy in copies:
            copy.wait()


def shards(latents, counts, gain_first, bias_first, weight_first, gain_second, bias_second, weight_second):
    channels = gain_first.shape[0]
    frames, rows, flat = latents.shape[1:]
    wide = 2 * channels
    pairs = flat // wide
    blocks, bands = lax.axis_size("tm"), lax.axis_size("space")
    block = latents.reshape(frames, rows, flat)

    def shift(sent, step, along):
        pairs_of = [
            (t * bands + s, (t + along) % blocks * bands + (s + step * (t + along < blocks)) % bands)
            for t in range(blocks)
            for s in range(bands)
        ]
        return lax.ppermute(sent, ("tm", "space"), pairs_of)

    vmem = pl.BlockSpec(memory_space=pltpu.VMEM)
    smem = pl.BlockSpec(memory_space=pltpu.SMEM)
    params = pltpu.CompilerParams(vmem_limit_bytes=24 << 20)
    swap = bands == 2
    rims = 1 if swap else 2
    rim = jax.ShapeDtypeStruct((frames, 2, pairs, wide), BF16)
    stages = [pltpu.VMEM((3, 2 * rows * pairs, LANES), F32)] * (frames // 2)
    mask = pl.pallas_call(
        functools.partial(mask_kernel, channels),
        out_shape=jax.ShapeDtypeStruct((2 * rows, LANES), F32),
        out_specs=vmem,
        compiler_params=params,
        cost_estimate=pl.CostEstimate(flops=4 << 30, bytes_accessed=1 << 16, transcendentals=0),
        name="lane_mask",
    )()
    normed, *sent = pl.pallas_call(
        functools.partial(norm_kernel, swap),
        out_shape=[jax.ShapeDtypeStruct((frames, rows, pairs, wide), BF16)] + [rim] * rims,
        in_specs=[vmem] * 3,
        out_specs=[vmem] * (1 + rims),
        scratch_shapes=stages,
        compiler_params=params,
        cost_estimate=pl.CostEstimate(flops=4 << 30, bytes_accessed=1 << 20, transcendentals=0),
        name="norm_and_cut",
    )(mask, block, gain_first.reshape(1, channels))
    earlier = shift(block, 0, 1)
    if swap:
        near = (shift(sent[0], 1, 0),) * 2
        far = (shift(sent[0], 1, 1),) * 2
        deep = rows + 1
    else:
        near = (shift(sent[0], 1, 0), shift(sent[1], -1, 0))
        far = (shift(sent[0], 1, 1), shift(sent[1], -1, 1))
        deep = rows + 2

    first_weight = weight_first.reshape(3, 3, 3 * channels, channels)
    second_weight = weight_second.reshape(3, 3, 3 * channels, channels)
    share = (2, frames, deep, pairs, channels)
    window = [pltpu.VMEM((deep + 2, pairs, wide), BF16)] * (frames + 1)
    cost = pl.CostEstimate(flops=1 << 20, bytes_accessed=1 << 16, transcendentals=0)
    taps = jax.ShapeDtypeStruct((2, *first_weight.shape[1:]), BF16)
    from_own, mixed_two = pl.pallas_call(
        functools.partial(own_kernel, bands, deep),
        out_shape=[jax.ShapeDtypeStruct(share, F32), taps],
        in_specs=[smem] + [vmem] * 6,
        out_specs=[vmem] * 2,
        scratch_shapes=window,
        compiler_params=params,
        cost_estimate=cost,
        name="conv_one_own",
    )(
        counts, normed, first_weight, second_weight, gain_second.reshape(1, channels),
        bias_first.reshape(1, channels), bias_second.reshape(1, channels),
    )
    constants = (
        bias_first.reshape(1, channels), first_weight,
        gain_second.reshape(1, channels), bias_second.reshape(1, channels), second_weight,
    )
    result = jax.ShapeDtypeStruct((frames, rows, flat), BF16)
    scratch = (
        [pltpu.VMEM((rows + 2, pairs, wide), BF16)] * (frames + 2 + 2 * frames)
        + [pltpu.VMEM((3, frames // 2 * rows * pairs, LANES), F32)] * 2
    )
    first_out = pl.pallas_call(
        functools.partial(first_block_kernel, bands),
        out_shape=result,
        in_specs=[smem] + [vmem] * 10,
        out_specs=vmem,
        scratch_shapes=scratch,
        compiler_params=params,
        cost_estimate=cost,
        name="first_block",
    )(counts, block, *near, from_own, mixed_two, *constants)
    from_earlier = pl.pallas_call(
        functools.partial(earlier_kernel, bands, deep),
        out_shape=jax.ShapeDtypeStruct(share, F32),
        in_specs=[smem] + [vmem] * 5,
        out_specs=vmem,
        scratch_shapes=window + stages,
        compiler_params=params,
        cost_estimate=cost,
        name="conv_one_earlier",
    )(counts, mask, earlier, gain_first.reshape(1, channels), first_weight, first_out)
    out = pl.pallas_call(
        functools.partial(last_kernel, bands),
        out_shape=result,
        in_specs=[smem] + [vmem] * 14,
        out_specs=pl.BlockSpec(memory_space=pl.ANY),
        scratch_shapes=[
            pltpu.VMEM((frames, rows, flat), BF16), pltpu.SemaphoreType.DMA((frames,))
        ] + scratch,
        compiler_params=params,
        cost_estimate=pl.CostEstimate(flops=4 << 30, bytes_accessed=6 << 20, transcendentals=0),
        name="last",
    )(counts, block, *near, *far, from_own, from_earlier, first_out, mixed_two, *constants)
    return out.reshape(1, frames, rows, flat)


def solution(mesh):
    spread = P(("groups", "clip"), "tm", "space", None)
    return jax.shard_map(
        shards,
        mesh=mesh,
        in_specs=(spread, P(("groups", "clip")), P(), P(), P(), P(), P(), P()),
        out_specs=spread,
        check_vma=False,
    )
```
